256 devices in a mesh: lat: 16 (over x_hi, y, core), lon: 16 (over z, x_lo).
Axes of the slice: x: 4 (x_hi: 2, x_lo: 2; x = x_hi * 2 + x_lo), y: 4, z: 8, core: 2. Of those that a mesh axis runs over, the one named last changes fastest.
Arguments:
- tokens: bfloat16 [8, 96, 192, 192], P(None, 'lat', 'lon'), may hold values from -6 to 6
- grad_out: bfloat16 [8, 96, 192, 192], P(None, 'lat', 'lon'), may hold values from -6 to 6
- gain_one: float32 [192], replicated, may hold values from 0.5 to 1.5
- qkv_one: bfloat16 [192, 576], replicated, may hold values from -0.4375 to 0.4375
- proj_one: bfloat16 [192, 192], replicated, may hold values from -0.4375 to 0.4375
- bias_one: float32 [16, 79488], P('lat'), may hold values from -4 to 300
- gain_two: float32 [192], replicated, may hold values from 0.5 to 1.5
- qkv_two: bfloat16 [192, 576], replicated, may hold values from -0.4375 to 0.4375
- proj_two: bfloat16 [192, 192], replicated, may hold values from -0.4375 to 0.4375
- bias_two: float32 [16, 79488], P('lat'), may hold values from -4 to 300
Outputs:
- grad_tokens: bfloat16 [8, 96, 192, 192], P(None, 'lat', 'lon')
- grad_bias_one: float32 [16, 79488], P('lat', 'lon')
- grad_bias_two: float32 [16, 79488], P('lat', 'lon')
The draws below stay inside these ranges and needn't reach their ends.
All inputs are finite; a program needn't handle non-finite values.
Results may differ from the reference program's by a relative error of at most 0.029.
Values may be sent and summed in bfloat16 or wider, within the bound.
No kernel may reach another device: no remote copies, remote signals or barrier semaphores. Data moves between devices by JAX's collectives and lax.ppermute only.
A program may use at most 192 MiB of HBM per device.

```python
import jax
import jax.numpy as jnp
from jax import lax

D = 192
HEADS = 6
HEAD_DIM = 32
WIN_LEV = 2
WIN_LAT = 6
WIN_LON = 12
WIN_TOK = 144
TABLE = 3312
LEV = 8
NLAT = 96
NLON = 192
LEV_WIN = 4
LAT_WIN = 16


def drawn_bias(key):
    shape = (LAT_WIN, LEV_WIN * HEADS * TABLE)
    return jnp.clip(jax.random.normal(key, shape, jnp.float32), -4.0, 4.0)


def draw_bias_one(key, part):
    key = jax.random.fold_in(key, 11)
    return drawn_bias(key)


def draw_bias_two(key, part):
    key = jax.random.fold_in(key, 12)
    return drawn_bias(key)


def steps_of(rng, dims, cuts, low, largest):
    gain, own = 1.0, jax.random.fold_in(rng, 6)
    for position, blocks in cuts:
        draws = jnp.exp(jax.random.uniform(jax.random.fold_in(own, position), (blocks,), jnp.float32, low / len(cuts), largest / len(cuts)))
        gain = gain * jnp.repeat(draws, dims[position] // blocks).reshape([-1 if axis == position else 1 for axis in range(len(dims))])
    return gain


def gaussian(own_key, dims, deviation, limit, cuts=(), held_as=jnp.bfloat16):
    entries = jax.random.normal(own_key, dims, jnp.float32) * deviation
    if len(cuts) > 0:
        entries = steps_of(own_key, dims, cuts, -0.22, 0.18) * entries
    return jnp.clip(entries, min=-limit, max=limit).astype(held_as)


def setup_inputs(seed: int = 0) -> dict:
    key_of = jax.random.split(jax.random.key(seed), 11)
    tokens = gaussian(key_of[0], (LEV, NLAT, NLON, D), 1.0, 6.0, ((1, 16), (2, 16)))
    grad_out = gaussian(key_of[1], (LEV, NLAT, NLON, D), 1.0, 6.0, ((1, 16), (2, 16)))
    gain_one = jnp.clip(1.0 + 0.1 * jax.random.normal(key_of[2], (D,), jnp.float32), 0.5, 1.5)
    qkv_one = gaussian(key_of[3], (D, 3 * D), D ** -0.5, 0.4375)
    proj_one = gaussian(key_of[4], (D, D), D ** -0.5, 0.4375)
    bias_one = draw_bias_one(jax.random.fold_in(key_of[10], 71), 0)
    gain_two = jnp.clip(1.0 + 0.1 * jax.random.normal(key_of[6], (D,), jnp.float32), 0.5, 1.5)
    qkv_two = gaussian(key_of[7], (D, 3 * D), D ** -0.5, 0.4375)
    proj_two = gaussian(key_of[8], (D, D), D ** -0.5, 0.4375)
    bias_two = draw_bias_two(jax.random.fold_in(key_of[10], 71), 0)
    return dict(tokens=tokens, grad_out=grad_out, gain_one=gain_one, qkv_one=qkv_one, proj_one=proj_one, bias_one=bias_one, gain_two=gain_two, qkv_two=qkv_two, proj_two=proj_two, bias_two=bias_two)


def widen(array_in):
    return lax.optimization_barrier(array_in).astype(jnp.float32)

def to_windows(grid, lat_win, lon_win):
    width = grid.shape[-1]
    parts = grid.reshape(LEV // WIN_LEV, WIN_LEV, lat_win, WIN_LAT, lon_win, WIN_LON, width)
    parts = parts.transpose(0, 2, 4, 1, 3, 5, 6)
    return parts.reshape(-1, WIN_TOK, width)

def from_windows(windows, lat_win, lon_win):
    width = windows.shape[-1]
    parts = windows.reshape(LEV // WIN_LEV, lat_win, lon_win, WIN_LEV, WIN_LAT, WIN_LON, width)
    parts = parts.transpose(0, 3, 1, 4, 2, 5, 6)
    return parts.reshape(LEV, lat_win * WIN_LAT, lon_win * WIN_LON, width)

def group_mask():
    lat_index = jnp.arange(WIN_TOK, dtype=jnp.int32) // WIN_LON % WIN_LAT
    upper = lat_index >= WIN_LAT // 2
    return jnp.where(upper[:, None] != upper[None, :], jnp.float32(-10000.0), jnp.float32(0.0))

def pair_index():
    place = jnp.arange(WIN_TOK, dtype=jnp.int32)
    level = place // (WIN_LAT * WIN_LON)
    latitude = place // WIN_LON % WIN_LAT
    longitude = place % WIN_LON
    block = ((level[:, None] * WIN_LAT + latitude[:, None]) * WIN_LEV + level[None, :]) * WIN_LAT + latitude[None, :]
    offset = longitude[:, None] - longitude[None, :] + (WIN_LON - 1)
    return (block * (2 * WIN_LON - 1) + offset).astype(jnp.int32)

def expand_table(row):
    table = row.reshape(LEV_WIN, HEADS, TABLE)
    return jnp.take(table, pair_index(), axis=2)

def fold_table(grad_pairs):
    zeros = jnp.zeros((LEV_WIN * HEADS * TABLE,), jnp.float32)
    primal, pullback = jax.vjp(expand_table, zeros)
    return pullback(grad_pairs)[0]

def window_forward(windows, bias_win, mask_add, gain_vec, w_qkv, w_proj):
    num_win = windows.shape[0]
    scaling = HEAD_DIM ** (-0.5)
    inputs_f = windows.astype(jnp.float32)
    centred = inputs_f - lax.optimization_barrier(jnp.mean(inputs_f, -1, keepdims=True))
    inv_std = lax.rsqrt(lax.optimization_barrier(jnp.mean(centred * centred, -1, keepdims=True)) + 1e-05)
    normed = centred * inv_std
    hidden = (normed * gain_vec).astype(jnp.bfloat16)
    packed = jnp.dot(hidden, w_qkv, preferred_element_type=jnp.float32).astype(jnp.bfloat16)
    packed = packed.reshape(num_win, WIN_TOK, 3, HEADS, HEAD_DIM)
    q_rows, k_rows, v_rows = (packed[:, :, 0], packed[:, :, 1], packed[:, :, 2])
    scores = jnp.einsum('nqhc,nkhc->nhqk', widen(q_rows), widen(k_rows)) * scaling + bias_win
    if mask_add is not None:
        scores = scores + mask_add[:, None]
    row_max = lax.optimization_barrier(jnp.max(scores, -1, keepdims=True))
    exp_scores = jnp.exp(scores - row_max)
    attn_probs = exp_scores / lax.optimization_barrier(jnp.sum(exp_scores, -1, keepdims=True))
    probs_low = attn_probs.astype(jnp.bfloat16)
    attended = jnp.einsum('nhqk,nkhc->nqhc', widen(probs_low), widen(v_rows)).astype(jnp.bfloat16)
    attended = attended.reshape(num_win, WIN_TOK, D)
    block_out = (inputs_f + jnp.dot(attended, w_proj, preferred_element_type=jnp.float32)).astype(jnp.bfloat16)
    return (block_out, (normed, inv_std, q_rows, k_rows, v_rows, attn_probs, probs_low))

def window_backward(saved, grad_win, gain_vec, w_qkv, w_proj):
    normed, inv_std, q_rows, k_rows, v_rows, attn_probs, probs_low = saved
    num_win = grad_win.shape[0]
    scaling = HEAD_DIM ** (-0.5)
    grad_mixed = jnp.dot(grad_win, w_proj.T, preferred_element_type=jnp.float32).astype(jnp.bfloat16)
    grad_mixed = grad_mixed.reshape(num_win, WIN_TOK, HEADS, HEAD_DIM)
    grad_probs = jnp.einsum('nqhc,nkhc->nhqk', widen(grad_mixed), widen(v_rows))
    grad_v = jnp.einsum('nhqk,nqhc->nkhc', widen(probs_low), widen(grad_mixed)).astype(jnp.bfloat16)
    grad_scores = attn_probs * (grad_probs - lax.optimization_barrier(jnp.sum(grad_probs * attn_probs, -1, keepdims=True)))
    scaled_low = (grad_scores * scaling).astype(jnp.bfloat16)
    grad_q = jnp.einsum('nhqk,nkhc->nqhc', widen(scaled_low), widen(k_rows)).astype(jnp.bfloat16)
    grad_k = jnp.einsum('nhqk,nqhc->nkhc', widen(scaled_low), widen(q_rows)).astype(jnp.bfloat16)
    grad_packed = jnp.stack([grad_q, grad_k, grad_v], 2).reshape(num_win, WIN_TOK, 3 * D)
    grad_hidden = jnp.dot(grad_packed, w_qkv.T, preferred_element_type=jnp.float32)
    grad_normed = grad_hidden * gain_vec
    grad_local = inv_std * (grad_normed - lax.optimization_barrier(jnp.mean(grad_normed, -1, keepdims=True)) - normed * lax.optimization_barrier(jnp.mean(grad_normed * normed, -1, keepdims=True)))
    input_grad = (grad_win.astype(jnp.float32) + grad_local).astype(jnp.bfloat16)
    return (input_grad, grad_scores)

def spread_bias(bias_band, lon_win):
    return jnp.broadcast_to(bias_band[:, None], (LEV_WIN, lon_win, HEADS, WIN_TOK, WIN_TOK)).reshape(-1, HEADS, WIN_TOK, WIN_TOK)

def band_mask(band, masked, lon_win):
    if not masked:
        return None
    active = jnp.where(band == LAT_WIN - 1, jnp.float32(1.0), jnp.float32(0.0))
    return jnp.broadcast_to(active * group_mask(), (LEV_WIN * lon_win, WIN_TOK, WIN_TOK))

def band_bias(bias_all, band):
    row = lax.dynamic_index_in_dim(bias_all, band, 0, keepdims=False)
    return expand_table(row)

def grid_forward(source, bias_all, gain_vec, w_qkv, w_proj):
    lon_win = NLON // WIN_LON

    def one_band(band):
        start = (band * WIN_LAT).astype(jnp.int32)
        slab = lax.dynamic_slice_in_dim(source, start, WIN_LAT, 1)
        bias_band = band_bias(bias_all, band)
        out_win, saved = window_forward(to_windows(slab, 1, lon_win), spread_bias(bias_band, lon_win), None, gain_vec, w_qkv, w_proj)
        return from_windows(out_win, 1, lon_win)
    bands = lax.map(one_band, jnp.arange(LAT_WIN, dtype=jnp.int32))
    return bands.transpose(1, 0, 2, 3, 4).reshape(LEV, NLAT, NLON, D)

def grid_backward(source, grad_src, bias_all, gain_vec, w_qkv, w_proj, masked):
    lon_win = NLON // WIN_LON

    def one_band(band):
        start = (band * WIN_LAT).astype(jnp.int32)
        slab = lax.dynamic_slice_in_dim(source, start, WIN_LAT, 1)
        grad_slab = lax.dynamic_slice_in_dim(grad_src, start, WIN_LAT, 1)
        bias_band = band_bias(bias_all, band)
        out_win, saved = window_forward(to_windows(slab, 1, lon_win), spread_bias(bias_band, lon_win), band_mask(band, masked, lon_win), gain_vec, w_qkv, w_proj)
        grad_win, grad_scores = window_backward(saved, to_windows(grad_slab, 1, lon_win), gain_vec, w_qkv, w_proj)
        summed = grad_scores.reshape(LEV_WIN, lon_win, HEADS, WIN_TOK, WIN_TOK).sum(1)
        return (from_windows(grad_win, 1, lon_win), fold_table(summed))
    bands, biases = lax.map(one_band, jnp.arange(LAT_WIN, dtype=jnp.int32))
    grid = bands.transpose(1, 0, 2, 3, 4).reshape(LEV, NLAT, NLON, D)
    return (grid, biases)

def reference(tokens, grad_out, gain_one, qkv_one, proj_one, bias_one, gain_two, qkv_two, proj_two, bias_two):
    half_lat = WIN_LAT // 2
    half_lon = WIN_LON // 2
    first_out = grid_forward(tokens, bias_one, gain_one, qkv_one, proj_one)
    rolled = jnp.roll(first_out, (-half_lat, -half_lon), (1, 2))
    rolled_grad = jnp.roll(grad_out, (-half_lat, -half_lon), (1, 2))
    grad_rolled, grad_bias_two = grid_backward(rolled, rolled_grad, bias_two, gain_two, qkv_two, proj_two, True)
    grad_first = jnp.roll(grad_rolled, (half_lat, half_lon), (1, 2))
    grad_tokens, grad_bias_one = grid_backward(tokens, grad_first, bias_one, gain_one, qkv_one, proj_one, False)
    return (grad_tokens, grad_bias_one, grad_bias_two)
```

```python
import functools
import math

import jax
import jax.numpy as jnp
import numpy as np
from jax import lax
from jax.experimental import pallas as pl
from jax.experimental.pallas import tpu as pltpu
from jax.sharding import PartitionSpec as P

D = 192
HEADS = 6
HEAD_DIM = 32
WIN_LEV = 2
WIN_LAT = 6
WIN_LON = 12
WIN_TOK = 144
LEV = 8
LEV_WIN = LEV // WIN_LEV
BAND = WIN_LEV * WIN_LAT
OFFSETS = 2 * WIN_LON - 1
ROWS = OFFSETS * BAND
SLAB = HEADS * BAND
LANES = WIN_LON * SLAB
PIECE = 48
PIECES = 4 * PIECE
LOG2E = math.log2(math.e)
SCALE = HEAD_DIM ** (-0.5)
BF16 = jnp.bfloat16
F32 = jnp.float32


def constants():
    lanes = np.arange(LANES)
    lane_lon, lane_head, lane_pair = lanes // SLAB, lanes // BAND % HEADS, lanes % BAND
    rep = (lane_lon * BAND + lane_pair)[:, None] == np.arange(WIN_TOK)[None, :]
    mask = lane_head[:, None] == (np.arange(D) // HEAD_DIM)[None, :]
    rows = np.arange(ROWS)
    source = (rows % BAND) * OFFSETS + (OFFSETS - 1 - rows // BAND)
    perm = source[:, None] == np.arange(ROWS)[None, :]
    tok = np.arange(WIN_TOK)
    lon, lev, lat = tok // BAND, tok // WIN_LAT % WIN_LEV, tok % WIN_LAT
    within = (lon % 6) * 6 + lev * 3 + lat % 3
    cut = 2 * (lat < 3) + (lon < 6)
    joined = 2 * (lat >= 3) + (lon >= 6)
    places = np.arange(PIECES)
    split = (cut * PIECE + within)[:, None] == places[None, :]
    turn = ((lev * WIN_LAT + lat) * WIN_LON + lon)[:, None] == tok[None, :]
    join = (joined * PIECE + within)[:, None] == places[None, :]
    return dict(
        rep=rep, mask=mask, mask_t=mask.T, perm=perm, split=split, split_t=split.T, join=join, join_t=join.T, turn=turn, turn_t=turn.T
    )


CONST = {name: value.astype(jnp.bfloat16) for name, value in constants().items()}


def dot(a, b, contract=((1,), (0,))):
    return lax.dot_general(a, b, (contract, ((), ())), preferred_element_type=F32)


NT = ((1,), (1,))
TN = ((0,), (0,))


def expand_table(table, perm_ref, spread_ref):
    high = table.astype(BF16)
    rest = table - high.astype(F32)
    middle = rest.astype(BF16)
    low = (rest - middle.astype(F32)).astype(BF16)
    perm = perm_ref[...]
    spread_ref[...] = (dot(perm, high, NT) + dot(perm, middle, NT) + dot(perm, low, NT)) * LOG2E


def write_bias(spread_ref, store):
    for query_lon in range(WIN_LON):
        first = (WIN_LON - 1 - query_lon) * BAND
        store(query_lon * SLAB, spread_ref[first : first + WIN_TOK, :])


def fold_scores(low, perm_ref, folded_ref):
    folded_ref[...] = jnp.zeros_like(folded_ref)
    wide = low.astype(F32)
    for query_lon in range(WIN_LON):
        first = (WIN_LON - 1 - query_lon) * BAND
        folded_ref[first : first + WIN_TOK, :] += wide[:, query_lon * SLAB : (query_lon + 1) * SLAB]
    folded = (folded_ref[...] * (1.0 / SCALE)).astype(BF16)
    return dot(folded, perm_ref[...], TN).astype(BF16)


def gather_tokens(grid_ref, rows_ref):
    for lev in range(WIN_LEV):
        for lat in range(WIN_LAT):
            first = (lev * WIN_LAT + lat) * WIN_LON
            rows_ref[first : first + WIN_LON, :] = grid_ref[lev, lat].astype(F32)
    return rows_ref[...].astype(BF16)


def forward(inputs_f, bias, gain, w_qkv_ref, w_proj, rep, mask, mask_t):
    centred = inputs_f - jnp.mean(inputs_f, -1, keepdims=True)
    inv_std = lax.rsqrt(jnp.mean(centred * centred, -1, keepdims=True) + 1e-05)
    normed = centred * inv_std
    hidden = (normed * gain).astype(BF16)
    packed = dot(hidden, w_qkv_ref[...]).astype(BF16)
    q_rows, k_rows, v_rows = packed[:, :D], packed[:, D : 2 * D], packed[:, 2 * D :]
    q_spread = dot(rep, q_rows).astype(BF16) * mask
    scores = dot(k_rows, q_spread, NT) * (SCALE * LOG2E) + bias
    exp_scores = jnp.exp2(scores - jnp.max(scores, 0, keepdims=True))
    attn_probs = exp_scores * (1.0 / jnp.sum(exp_scores, 0, keepdims=True))
    probs_low = attn_probs.astype(BF16)
    return normed, inv_std, q_spread, k_rows, v_rows, attn_probs, probs_low


def gathered(values, weights, rep, mask_t):
    spread = dot(values, weights, TN).astype(BF16) * mask_t
    return dot(spread, rep)


def backward(normed, inv_std, q_spread, k_rows, v_rows, attn_probs, probs_low, grad, gain, w_qkv_ref, w_proj, rep, mask, mask_t):
    grad_mixed = dot(grad, w_proj, NT).astype(BF16)
    mixed_spread = dot(rep, grad_mixed).astype(BF16) * mask
    grad_probs = dot(v_rows, mixed_spread, NT)
    grad_v = dot(probs_low, mixed_spread).astype(BF16)
    grad_scores = attn_probs * (grad_probs - jnp.sum(grad_probs * attn_probs, 0, keepdims=True))
    scaled_low = (grad_scores * SCALE).astype(BF16)
    grad_k = dot(scaled_low, q_spread).astype(BF16)
    grad_q = gathered(k_rows, scaled_low, rep, mask_t).T.astype(BF16)
    grad_hidden = (
        dot(grad_q, w_qkv_ref[:, :D], NT)
        + dot(grad_k, w_qkv_ref[:, D : 2 * D], NT)
        + dot(grad_v, w_qkv_ref[:, 2 * D :], NT)
    )
    grad_normed = grad_hidden * gain
    grad_local = inv_std * (
        grad_normed
        - jnp.mean(grad_normed, -1, keepdims=True)
        - normed * jnp.mean(grad_normed * normed, -1, keepdims=True)
    )
    return (grad.astype(F32) + grad_local).astype(BF16), scaled_low


def first_kernel(
    tokens_ref, grad_ref, table_ref, gain_ref, w_qkv_ref, w_proj_ref, rep_ref, mask_ref, mask_t_ref, perm_ref, split_t_ref, turn_ref,
    stay_ref, lon_ref, lat_ref, both_ref, normed_ref, inv_ref, q_ref, k_ref, v_ref, probs_ref,
    rows_ref, spread_ref, bias_ref,
):
    expand_table(table_ref[0], perm_ref, spread_ref)

    def store(lane, block):
        bias_ref[:, lane : lane + SLAB] = block

    write_bias(spread_ref, store)
    rep, mask, mask_t = rep_ref[...], mask_ref[...], mask_t_ref[...]
    inputs_f = dot(turn_ref[...], gather_tokens(tokens_ref, rows_ref))
    normed, inv_std, q_spread, k_rows, v_rows, attn_probs, probs_low = forward(
        inputs_f, bias_ref[...], gain_ref[...], w_qkv_ref, w_proj_ref[...], rep, mask, mask_t
    )
    attended = gathered(v_rows, probs_low, rep, mask_t).T.astype(BF16)
    block_out = (inputs_f + dot(attended, w_proj_ref[...])).astype(BF16)
    normed_ref[0] = normed
    inv_ref[0] = jnp.broadcast_to(inv_std, (WIN_TOK, 128))
    q_ref[0] = q_spread
    k_ref[0] = k_rows
    v_ref[0] = v_rows
    probs_ref[0] = probs_low
    out_pieces = dot(split_t_ref[...], block_out).astype(BF16)
    grad_rows = dot(turn_ref[...], gather_tokens(grad_ref, rows_ref)).astype(BF16)
    grad_pieces = dot(split_t_ref[...], grad_rows).astype(BF16)
    for place, ref in enumerate((stay_ref, lon_ref, lat_ref, both_ref)):
        ref[0, 0] = out_pieces[place * PIECE : (place + 1) * PIECE]
        ref[1, 0] = grad_pieces[place * PIECE : (place + 1) * PIECE]


def bias_kernel(active_ref, table_ref, perm_ref, bias_ref, spread_ref):
    expand_table(table_ref[0], perm_ref, spread_ref)
    blocked = active_ref[0, 0] * (-10000.0 * LOG2E)
    key_lat = lax.broadcasted_iota(jnp.int32, (WIN_TOK, SLAB), 0) % WIN_LAT
    query_lat = lax.broadcasted_iota(jnp.int32, (WIN_TOK, SLAB), 1) % WIN_LAT
    apart = jnp.where((key_lat < 3) != (query_lat < 3), blocked, 0.0)

    def store(lane, block):
        bias_ref[0, :, lane : lane + SLAB] = block + apart

    write_bias(spread_ref, store)


def second_kernel(
    stay_ref, lon_ref, lat_ref, both_ref, bias_ref, gain_ref, w_qkv_ref, w_proj_ref, rep_ref, mask_ref, mask_t_ref, join_ref, join_t_ref,
    stay_out, lon_out, lat_out, both_out, low_ref,
):
    rep, mask, mask_t = rep_ref[...], mask_ref[...], mask_t_ref[...]
    join = join_ref[...]
    arrived = (stay_ref, lon_ref, lat_ref, both_ref)
    inputs = dot(join, jnp.concatenate([ref[0, 0] for ref in arrived], 0))
    grad = dot(join, jnp.concatenate([ref[1, 0] for ref in arrived], 0)).astype(BF16)
    gain, w_proj = gain_ref[...], w_proj_ref[...]
    saved = forward(inputs, bias_ref[0], gain, w_qkv_ref, w_proj, rep, mask, mask_t)
    input_grad, scaled_low = backward(*saved, grad, gain, w_qkv_ref, w_proj, rep, mask, mask_t)
    low_ref[0] = scaled_low
    pieces = dot(join_t_ref[...], input_grad).astype(BF16)
    for place, ref in enumerate((stay_out, lon_out, lat_out, both_out)):
        ref[0] = pieces[place * PIECE : (place + 1) * PIECE]


def fold_kernel(low_ref, perm_ref, out_ref, folded_ref):
    out_ref[0] = fold_scores(low_ref[0], perm_ref, folded_ref)


def third_kernel(
    stay_ref, lon_ref, lat_ref, both_ref, normed_ref, inv_ref, q_ref, k_ref, v_ref, probs_ref,
    gain_ref, w_qkv_ref, w_proj_ref, rep_ref, mask_ref, mask_t_ref, perm_ref, split_ref, turn_ref,
    grid_ref, term_ref,
    rows_ref, folded_ref,
):
    rep, mask, mask_t = rep_ref[...], mask_ref[...], mask_t_ref[...]
    arrived = (stay_ref, lon_ref, lat_ref, both_ref)
    grad = dot(split_ref[...], jnp.concatenate([ref[0] for ref in arrived], 0)).astype(BF16)
    probs_low = probs_ref[0]
    saved = (normed_ref[0], inv_ref[0][:, :1], q_ref[0], k_ref[0], v_ref[0], probs_low.astype(F32), probs_low)
    input_grad, scaled_low = backward(*saved, grad, gain_ref[...], w_qkv_ref, w_proj_ref[...], rep, mask, mask_t)
    rows_ref[...] = dot(turn_ref[...], input_grad)
    for lev in range(WIN_LEV):
        for lat in range(WIN_LAT):
            first = (lev * WIN_LAT + lat) * WIN_LON
            grid_ref[lev, lat] = rows_ref[first : first + WIN_LON, :].astype(BF16)
    term_ref[0] = fold_scores(scaled_low, perm_ref, folded_ref)


def fixed(*shape):
    return pl.BlockSpec(shape, lambda v: (0,) * len(shape))


def level(*shape):
    return pl.BlockSpec((1,) + shape, lambda v: (v,) + (0,) * len(shape))


def pair_of(*shape):
    return pl.BlockSpec((2, 1) + shape, lambda v: (0, v) + (0,) * len(shape))


GRID = pl.BlockSpec((WIN_LEV, WIN_LAT, WIN_LON, D), lambda v: (v, 0, 0, 0))
WEIGHTS = [fixed(1, D), fixed(D, 3 * D), fixed(D, D), fixed(LANES, WIN_TOK), fixed(LANES, D), fixed(D, LANES)]


def call(kernel, in_specs, out_specs, out_shapes, scratch, flops):
    return pl.pallas_call(
        kernel,
        grid=(LEV_WIN,),
        in_specs=in_specs,
        out_specs=out_specs,
        out_shape=[jax.ShapeDtypeStruct(shape, dtype) for shape, dtype in out_shapes],
        scratch_shapes=[pltpu.VMEM(shape, F32) for shape in scratch],
        compiler_params=pltpu.CompilerParams(vmem_limit_bytes=48 * 1024 * 1024),
        cost_estimate=pl.CostEstimate(flops=flops, bytes_accessed=4_000_000, transcendentals=500_000),
    )


def shifted(axes, by):
    sizes = [lax.axis_size(axis) for axis in axes]
    if len(sizes) == 1:
        return [(i, (i + by) % sizes[0]) for i in range(sizes[0])]
    rows, columns = sizes
    return [
        (a * columns + o, (a + by) % rows * columns + (o + by) % columns)
        for a in range(rows)
        for o in range(columns)
    ]


def exchange(pieces, by):
    stay, lon, lat, both = pieces
    return (
        stay,
        lax.ppermute(lon, ("lon",), shifted(("lon",), by)),
        lax.ppermute(lat, ("lat",), shifted(("lat",), by)),
        lax.ppermute(both, ("lat", "lon"), shifted(("lat", "lon"), by)),
    )


def body(
    tokens, grad_out, gain_one, qkv_one, proj_one, bias_one, gain_two, qkv_two, proj_two, bias_two
):
    const = {name: jnp.asarray(value) for name, value in CONST.items()}
    spread = (const["rep"], const["mask"], const["mask_t"])
    tables = (LEV_WIN, SLAB, ROWS)
    block_one = (gain_one.reshape(1, D), qkv_one, proj_one) + spread
    block_two = (gain_two.reshape(1, D), qkv_two, proj_two) + spread
    pair = ((2, LEV_WIN, PIECE, D), BF16)
    piece = ((LEV_WIN, PIECE, D), BF16)

    first = call(
        first_kernel,
        [GRID, GRID, level(SLAB, ROWS)] + WEIGHTS + [fixed(ROWS, ROWS), fixed(PIECES, WIN_TOK), fixed(WIN_TOK, WIN_TOK)],
        [pair_of(PIECE, D)] * 4
        + [level(WIN_TOK, D), level(WIN_TOK, 128), level(LANES, D)]
        + [level(WIN_TOK, D)] * 2
        + [level(WIN_TOK, LANES)],
        [pair] * 4
        + [((LEV_WIN, WIN_TOK, D), F32), ((LEV_WIN, WIN_TOK, 128), F32), ((LEV_WIN, LANES, D), BF16)]
        + [((LEV_WIN, WIN_TOK, D), BF16)] * 2
        + [((LEV_WIN, WIN_TOK, LANES), BF16)],
        [(WIN_TOK, D), (ROWS, SLAB), (WIN_TOK, LANES)],
        2_000_000_000,
    )(tokens, grad_out, bias_one.reshape(tables), *block_one, const["perm"], const["split_t"], const["turn"])
    pieces, saved = first[:4], first[4:]
    pieces, table_two = lax.optimization_barrier((tuple(pieces), bias_two.reshape(tables)))
    pieces = exchange(pieces, -1)

    active = jnp.where(lax.axis_index("lat") == lax.axis_size("lat") - 1, 1.0, 0.0).astype(F32).reshape(1, 1)
    (bias_full,) = call(
        bias_kernel,
        [pl.BlockSpec(memory_space=pltpu.SMEM), level(SLAB, ROWS), fixed(ROWS, ROWS)],
        [level(WIN_TOK, LANES)],
        [((LEV_WIN, WIN_TOK, LANES), F32)],
        [(ROWS, SLAB)],
        500_000_000,
    )(active, table_two, const["perm"])

    second = call(
        second_kernel,
        [pair_of(PIECE, D)] * 4 + [level(WIN_TOK, LANES)] + WEIGHTS + [fixed(WIN_TOK, PIECES), fixed(PIECES, WIN_TOK)],
        [level(PIECE, D)] * 4 + [level(WIN_TOK, LANES)],
        [piece] * 4 + [((LEV_WIN, WIN_TOK, LANES), BF16)],
        [],
        4_000_000_000,
    )(*pieces, bias_full, *block_two, const["join"], const["join_t"])
    grad_pieces, low_two = second[:4], second[4]
    grad_pieces = exchange(grad_pieces, 1)

    term = ((LEV_WIN, SLAB, ROWS), BF16)
    (term_two,) = call(
        fold_kernel,
        [level(WIN_TOK, LANES), fixed(ROWS, ROWS)],
        [level(SLAB, ROWS)],
        [term],
        [(ROWS, SLAB)],
        500_000_000,
    )(low_two, const["perm"])

    grad_tokens, term_one = call(
        third_kernel,
        [level(PIECE, D)] * 4
        + [level(WIN_TOK, D), level(WIN_TOK, 128), level(LANES, D)]
        + [level(WIN_TOK, D)] * 2
        + [level(WIN_TOK, LANES)]
        + WEIGHTS
        + [fixed(ROWS, ROWS), fixed(WIN_TOK, PIECES), fixed(WIN_TOK, WIN_TOK)],
        [GRID, level(SLAB, ROWS)],
        [((LEV, WIN_LAT, WIN_LON, D), BF16), term],
        [(WIN_TOK, D), (ROWS, SLAB)],
        4_000_000_000,
    )(*grad_pieces, *saved, *block_one, const["perm"], const["split"], const["turn_t"])

    tiles = lax.axis_size("lon")
    share = LEV_WIN * SLAB // tiles
    both_terms = jnp.stack([term_one.reshape(tiles, share, ROWS), term_two.reshape(tiles, share, ROWS)], 1)
    received = lax.all_to_all(both_terms, "lon", 0, 0, tiled=True)
    summed = received.reshape(tiles, 2, share, ROWS).astype(F32).sum(0)
    return grad_tokens, summed[0].reshape(1, -1), summed[1].reshape(1, -1)


def solution(mesh):
    in_specs = (
        P(None, "lat", "lon", None),
        P(None, "lat", "lon", None),
        P(),
        P(),
        P(),
        P("lat", None),
        P(),
        P(),
        P(),
        P("lat", None),
    )
    out_specs = (P(None, "lat", "lon", None), P("lat", "lon"), P("lat", "lon"))
    return jax.shard_map(body, mesh=mesh, in_specs=in_specs, out_specs=out_specs, check_vma=False)
```

```python
import math

import jax
import jax.numpy as jnp
import numpy as np
from jax import lax
from jax.experimental import pallas as pl
from jax.experimental.pallas import tpu as pltpu
from jax.sharding import PartitionSpec as P

D = 192
HEADS = 6
HEAD_DIM = 32
WIN_LEV = 2
WIN_LAT = 6
WIN_LON = 12
WIN_TOK = 144
LEV = 8
LEV_WIN = LEV // WIN_LEV
BAND = WIN_LEV * WIN_LAT
OFFSETS = 2 * WIN_LON - 1
ROWS = OFFSETS * BAND
SLAB = HEADS * BAND
LANES = WIN_LON * SLAB
PIECE = 36
FLAT = 128
TERM = 40
SHARE = 18
REST = ROWS - 2 * FLAT
LOG2E = math.log2(math.e)
SCALE = HEAD_DIM ** (-0.5)
BF16 = jnp.bfloat16
F32 = jnp.float32
LEVELS = range(LEV_WIN)


def constants():
    lanes = np.arange(LANES)
    lane_lon, lane_head, lane_pair = lanes // SLAB, lanes // BAND % HEADS, lanes % BAND
    rep = (lane_lon * BAND + lane_pair)[:, None] == np.arange(WIN_TOK)[None, :]
    mask = lane_head[:, None] == (np.arange(D) // HEAD_DIM)[None, :]
    rows = np.arange(ROWS)
    source = (rows % BAND) * OFFSETS + (OFFSETS - 1 - rows // BAND)
    perm = source[:, None] == np.arange(3 * FLAT)[None, :]
    tok = np.arange(WIN_TOK)
    lon, lev, lat = tok // BAND, tok // WIN_LAT % WIN_LEV, tok % WIN_LAT
    within = (lon % 6) * 6 + lev * 3 + lat % 3
    cut = 2 * (lat < 3) + (lon < 6)
    joined = 2 * (lat >= 3) + (lon >= 6)
    split = (cut * PIECE + within)[:, None] == tok[None, :]
    join = (joined * PIECE + within)[:, None] == tok[None, :]
    turn = ((lev * WIN_LAT + lat) * WIN_LON + lon)[:, None] == tok[None, :]
    return dict(
        rep=rep, mask=mask, mask_t=mask.T, perm=perm, split=split, split_t=split.T, join=join, join_t=join.T,
        turn=turn, turn_t=turn.T,
    )


CONST = {name: value.astype(jnp.bfloat16) for name, value in constants().items()}


def dot(a, b, contract=((1,), (0,))):
    return lax.dot_general(a, b, (contract, ((), ())), preferred_element_type=F32)


NT = ((1,), (1,))
TN = ((0,), (0,))


def expand_table(flat_ref, perm_ref, parts, spread_ref):
    lane = lax.broadcasted_iota(jnp.int32, (9, FLAT), 1)
    for first in range(32):
        base, off = ROWS * first // FLAT, ROWS * first % FLAT
        count = -(-(off + ROWS) // FLAT)
        rows = [flat_ref[pl.ds(base + k, 9, stride=69), :] for k in range(count)]
        if off:
            rows = [pltpu.roll(row, FLAT - off, 1) for row in rows]
        for place, part in enumerate(parts):
            value = rows[place]
            if off and place + 1 < count:
                value = jnp.where(lane < FLAT - off, value, rows[place + 1])
            part[pl.ds(first, 9, stride=32), :] = value
    table = jnp.concatenate([part[...] for part in parts], 1)
    high = table.astype(BF16)
    rest = table - high.astype(F32)
    middle = rest.astype(BF16)
    low = (rest - middle.astype(F32)).astype(BF16)
    perm = perm_ref[...]
    spread_ref[...] = (dot(perm, high, NT) + dot(perm, middle, NT) + dot(perm, low, NT)) * LOG2E


def write_bias(spread_ref, bias_ref, apart=None):
    for query_lon in range(WIN_LON):
        first = (WIN_LON - 1 - query_lon) * BAND
        for v in LEVELS:
            block = spread_ref[first : first + WIN_TOK, v * SLAB : (v + 1) * SLAB]
            if apart is not None:
                block = block + apart
            bias_ref[v, :, query_lon * SLAB : (query_lon + 1) * SLAB] = block


def fold_scores(lows, perm_ref, folded_ref, table_ref, pack_ref):
    folded_ref[...] = jnp.zeros_like(folded_ref)
    wide = [low.astype(F32) for low in lows]
    for query_lon in range(WIN_LON):
        first = (WIN_LON - 1 - query_lon) * BAND
        block = jnp.concatenate([low[:, query_lon * SLAB : (query_lon + 1) * SLAB] for low in wide], 1)
        folded_ref[first : first + WIN_TOK, :] += block
    folded = (folded_ref[...] * (1.0 / SCALE)).astype(BF16)
    table_ref[...] = dot(folded, perm_ref[...], TN)
    for tile in range(LEV_WIN * SLAB // SHARE):
        top = tile * SHARE
        pack_ref[tile, :SHARE, :] = table_ref[top : top + SHARE, :FLAT]
        pack_ref[tile, SHARE : 2 * SHARE, :] = table_ref[top : top + SHARE, FLAT : 2 * FLAT]
        pack_ref[tile, 2 * SHARE : TERM, :] = jnp.zeros((TERM - 2 * SHARE, FLAT), F32)
        for group in range(5):
            count = min(4, SHARE - 4 * group)
            pack_ref[tile, 2 * SHARE : 2 * SHARE + count, group * REST : (group + 1) * REST] = table_ref[
                top + 4 * group : top + 4 * group + count, 2 * FLAT : ROWS
            ]


def load_windows(grid_ref, left_ref, right_ref):
    wide = grid_ref[...].astype(F32).reshape(LEV * BAND // WIN_LEV * WIN_LON, D)
    left_ref[...] = wide[:, :FLAT]
    right_ref[:, : D - FLAT] = wide[:, FLAT:]
    windows = []
    for v in LEVELS:
        halves = []
        for lev in range(WIN_LEV):
            rows = pl.ds(WIN_LEV * v + lev, WIN_LAT * WIN_LON, stride=LEV)
            halves.append(jnp.concatenate([left_ref[rows, :], right_ref[rows, :][:, : D - FLAT]], 1))
        windows.append(jnp.concatenate(halves, 0).astype(BF16))
    return windows


def store_windows(windows, grid_ref, left_ref, right_ref):
    for v in LEVELS:
        for lev in range(WIN_LEV):
            rows = pl.ds(WIN_LEV * v + lev, WIN_LAT * WIN_LON, stride=LEV)
            half = windows[v][lev * WIN_LAT * WIN_LON : (lev + 1) * WIN_LAT * WIN_LON]
            left_ref[rows, :] = half[:, :FLAT]
            right_ref[rows, :] = jnp.concatenate([half[:, FLAT:], jnp.zeros((WIN_LAT * WIN_LON, 2 * FLAT - D), F32)], 1)
    wide = jnp.concatenate([left_ref[...], right_ref[:, : D - FLAT]], 1)
    grid_ref[...] = wide.reshape(WIN_LAT * WIN_LON, LEV, D).astype(BF16)


def forward(inputs, biases, gain, w_qkv, rep, mask):
    centred = [x - jnp.mean(x, -1, keepdims=True) for x in inputs]
    inv_std = [lax.rsqrt(jnp.mean(x * x, -1, keepdims=True) + 1e-05) for x in centred]
    normed = [x * inv for x, inv in zip(centred, inv_std)]
    hidden = [(x * gain).astype(BF16) for x in normed]
    packed = [dot(x, w_qkv).astype(BF16) for x in hidden]
    k_rows = [x[:, D : 2 * D] for x in packed]
    v_rows = [x[:, 2 * D :] for x in packed]
    q_spread = [dot(rep, x[:, :D]).astype(BF16) * mask for x in packed]
    scores = [dot(k, q, NT) * (SCALE * LOG2E) + bias[...] for k, q, bias in zip(k_rows, q_spread, biases)]
    exp_scores = [jnp.exp2(x - jnp.max(x, 0, keepdims=True)) for x in scores]
    attn_probs = [x * (1.0 / jnp.sum(x, 0, keepdims=True)) for x in exp_scores]
    probs_low = [x.astype(BF16) for x in attn_probs]
    return list(zip(normed, inv_std, q_spread, k_rows, v_rows, attn_probs, probs_low))


def gathered(values, weights, rep, mask_t):
    spread = [dot(x, w, TN).astype(BF16) * mask_t for x, w in zip(values, weights)]
    return [dot(x, rep).T.astype(BF16) for x in spread]


def backward(saved, grads, gain, w_qkv_ref, w_proj, rep, mask, mask_t):
    normed, inv_std, q_spread, k_rows, v_rows, attn_probs, probs_low = zip(*saved)
    grad_mixed = [dot(x, w_proj, NT).astype(BF16) for x in grads]
    mixed_spread = [dot(rep, x).astype(BF16) * mask for x in grad_mixed]
    grad_probs = [dot(v, m, NT) for v, m in zip(v_rows, mixed_spread)]
    grad_v = [dot(p, m).astype(BF16) for p, m in zip(probs_low, mixed_spread)]
    lows = [
        ((p * (x - jnp.sum(x * p, 0, keepdims=True))) * SCALE).astype(BF16) for p, x in zip(attn_probs, grad_probs)
    ]
    grad_k = [dot(low, q).astype(BF16) for low, q in zip(lows, q_spread)]
    grad_q = gathered(k_rows, lows, rep, mask_t)
    w_q, w_k, w_v = w_qkv_ref[:, :D], w_qkv_ref[:, D : 2 * D], w_qkv_ref[:, 2 * D :]
    results = []
    for v, grad in enumerate(grads):
        grad_hidden = dot(grad_q[v], w_q, NT) + dot(grad_k[v], w_k, NT) + dot(grad_v[v], w_v, NT)
        grad_normed = grad_hidden * gain
        grad_local = inv_std[v] * (
            grad_normed
            - jnp.mean(grad_normed, -1, keepdims=True)
            - normed[v] * jnp.mean(grad_normed * normed[v], -1, keepdims=True)
        )
        results.append((grad.astype(F32) + grad_local).astype(BF16))
    return results, lows


def first_kernel(
    tokens_ref, grad_ref, flat_ref, gain_ref, w_qkv_ref, w_proj_ref, rep_ref, mask_ref, mask_t_ref, perm_ref, split_t_ref, turn_ref,
    stay_ref, lon_ref, lat_ref, both_ref, normed_ref, inv_ref, q_ref, k_ref, v_ref, probs_ref,
    part_a, part_b, part_c, spread_ref, bias_ref, left_ref, right_ref, piece_ref,
):
    turn = turn_ref[...]
    expand_table(flat_ref, perm_ref, (part_a, part_b, part_c), spread_ref)
    write_bias(spread_ref, bias_ref)
    inputs = [dot(turn, x) for x in load_windows(tokens_ref, left_ref, right_ref)]
    grads = [dot(turn, x).astype(BF16) for x in load_windows(grad_ref, left_ref, right_ref)]
    rep, mask, mask_t = rep_ref[...], mask_ref[...], mask_t_ref[...]
    saved = forward(inputs, [bias_ref.at[v] for v in LEVELS], gain_ref[...], w_qkv_ref[...], rep, mask)
    normed, inv_std, q_spread, k_rows, v_rows, attn_probs, probs_low = zip(*saved)
    attended = gathered(v_rows, probs_low, rep, mask_t)
    for v in LEVELS:
        normed_ref[v] = normed[v]
        inv_ref[v] = jnp.broadcast_to(inv_std[v], (WIN_TOK, FLAT))
        q_ref[v] = q_spread[v]
        k_ref[v] = k_rows[v]
        v_ref[v] = v_rows[v]
        probs_ref[v] = probs_low[v]
    split_t = split_t_ref[...]
    for v in LEVELS:
        block_out = (inputs[v] + dot(attended[v], w_proj_ref[...])).astype(BF16)
        piece_ref[:, v * PIECE : (v + 1) * PIECE, :D] = dot(split_t, block_out).reshape(4, PIECE, D)
        piece_ref[:, v * PIECE : (v + 1) * PIECE, D:] = dot(split_t, grads[v]).reshape(4, PIECE, D)
    for place, ref in enumerate((stay_ref, lon_ref, lat_ref, both_ref)):
        ref[...] = piece_ref[place].astype(BF16)


def bias_kernel(active_ref, flat_ref, perm_ref, bias_ref, part_a, part_b, part_c, spread_ref):
    expand_table(flat_ref, perm_ref, (part_a, part_b, part_c), spread_ref)
    blocked = active_ref[0, 0] * (-10000.0 * LOG2E)
    key_lat = lax.broadcasted_iota(jnp.int32, (WIN_TOK, SLAB), 0) % WIN_LAT
    query_lat = lax.broadcasted_iota(jnp.int32, (WIN_TOK, SLAB), 1) % WIN_LAT
    write_bias(spread_ref, bias_ref, jnp.where((key_lat < 3) != (query_lat < 3), blocked, 0.0))


def second_kernel(
    stay_ref, lon_ref, lat_ref, both_ref, bias_ref, gain_ref, w_qkv_ref, w_proj_ref, rep_ref, mask_ref, mask_t_ref, join_ref, join_t_ref,
    stay_out, lon_out, lat_out, both_out, low_ref,
    window_ref, piece_ref,
):
    rep, mask, mask_t = rep_ref[...], mask_ref[...], mask_t_ref[...]
    join, join_t = join_ref[...], join_t_ref[...]
    for place, ref in enumerate((stay_ref, lon_ref, lat_ref, both_ref)):
        wide = ref[...].astype(F32)
        for v in LEVELS:
            window_ref[v, place * PIECE : (place + 1) * PIECE, :] = wide[v * PIECE : (v + 1) * PIECE]
    pairs = [dot(join, window_ref[v].astype(BF16)) for v in LEVELS]
    inputs = [x[:, :D] for x in pairs]
    grads = [x[:, D:].astype(BF16) for x in pairs]
    gain, w_proj = gain_ref[...], w_proj_ref[...]
    saved = forward(inputs, [bias_ref.at[v] for v in LEVELS], gain, w_qkv_ref[...], rep, mask)
    results, lows = backward(saved, grads, gain, w_qkv_ref, w_proj, rep, mask, mask_t)
    for v in LEVELS:
        low_ref[v] = lows[v]
        row, lane = v % 2 * PIECE, v // 2 * D
        piece_ref[:, row : row + PIECE, lane : lane + D] = dot(join_t, results[v]).reshape(4, PIECE, D)
    for place, ref in enumerate((stay_out, lon_out, lat_out, both_out)):
        ref[...] = piece_ref[place].astype(BF16)


def fold_kernel(low_ref, perm_ref, pack_ref, folded_ref, table_ref):
    fold_scores([low_ref[v] for v in LEVELS], perm_ref, folded_ref, table_ref, pack_ref)


def third_kernel(
    stay_ref, lon_ref, lat_ref, both_ref, normed_ref, inv_ref, q_ref, k_ref, v_ref, probs_ref, other_ref,
    gain_ref, w_qkv_ref, w_proj_ref, rep_ref, mask_ref, mask_t_ref, perm_ref, split_ref, turn_t_ref,
    grid_ref, terms_ref,
    window_ref, left_ref, right_ref, folded_ref, table_ref, pack_ref,
):
    rep, mask, mask_t = rep_ref[...], mask_ref[...], mask_t_ref[...]
    split, turn_t = split_ref[...], turn_t_ref[...]
    for place, ref in enumerate((stay_ref, lon_ref, lat_ref, both_ref)):
        wide = ref[...].astype(F32)
        for v in LEVELS:
            row, lane = v % 2 * PIECE, v // 2 * D
            window_ref[v, place * PIECE : (place + 1) * PIECE, :] = wide[row : row + PIECE, lane : lane + D]
    grads = [dot(split, window_ref[v].astype(BF16)).astype(BF16) for v in LEVELS]
    saved = [
        (normed_ref[v], inv_ref[v][:, :1], q_ref[v], k_ref[v], v_ref[v], probs_ref[v].astype(F32), probs_ref[v])
        for v in LEVELS
    ]
    results, lows = backward(saved, grads, gain_ref[...], w_qkv_ref, w_proj_ref[...], rep, mask, mask_t)
    store_windows([dot(turn_t, x) for x in results], grid_ref, left_ref, right_ref)
    fold_scores(lows, perm_ref, folded_ref, table_ref, pack_ref)
    terms_ref[...] = jnp.concatenate([pack_ref[...], other_ref[...]], 1).astype(BF16)


def sum_kernel(arrived_ref, one_ref, two_ref, total_ref):
    total = arrived_ref[0].astype(F32)
    for tile in range(1, arrived_ref.shape[0]):
        total = total + arrived_ref[tile].astype(F32)
    total_ref[...] = total
    for base, out_ref in ((0, one_ref), (TERM, two_ref)):
        for row in range(SHARE):
            lane = ROWS * row
            out_ref[:, lane : lane + FLAT] = total_ref[base + row : base + row + 1, :]
            place = base + SHARE + row
            out_ref[:, lane + FLAT : lane + 2 * FLAT] = total_ref[place : place + 1, :]
            place, shift = base + 2 * SHARE + row % 4, row // 4 * REST
            out_ref[:, lane + 2 * FLAT : lane + ROWS] = total_ref[place : place + 1, shift : shift + REST]


def call(kernel, out_shapes, scratch, flops, scalars=0):
    return pl.pallas_call(
        kernel,
        out_shape=[jax.ShapeDtypeStruct(shape, dtype) for shape, dtype in out_shapes],
        scratch_shapes=[pltpu.VMEM(shape, F32) for shape in scratch],
        compiler_params=pltpu.CompilerParams(vmem_limit_bytes=VMEM_LIMIT),
        cost_estimate=pl.CostEstimate(flops=flops, bytes_accessed=4_000_000, transcendentals=500_000),
    )


VMEM_LIMIT = 40 * 1024 * 1024


def shifted(axes, by):
    sizes = [lax.axis_size(axis) for axis in axes]
    if len(sizes) == 1:
        return [(i, (i + by) % sizes[0]) for i in range(sizes[0])]
    rows, columns = sizes
    return [
        (a * columns + o, (a + by) % rows * columns + (o + by) % columns)
        for a in range(rows)
        for o in range(columns)
    ]


def exchange(pieces, by):
    stay, lon, lat, both = pieces
    return (
        stay,
        lax.ppermute(lon, ("lon",), shifted(("lon",), by)),
        lax.ppermute(lat, ("lat",), shifted(("lat",), by)),
        lax.ppermute(both, ("lat", "lon"), shifted(("lat", "lon"), by)),
    )


def body(
    tokens, grad_out, gain_one, qkv_one, proj_one, bias_one, gain_two, qkv_two, proj_two, bias_two
):
    const = {name: jnp.asarray(value) for name, value in CONST.items()}
    spread = (const["rep"], const["mask"], const["mask_t"])
    perm = const["perm"]
    flat = (LEV_WIN * SLAB * ROWS // FLAT, FLAT)
    block_one = (gain_one.reshape(1, D), qkv_one, proj_one) + spread
    block_two = (gain_two.reshape(1, D), qkv_two, proj_two) + spread
    columns = (WIN_LAT * WIN_LON, LEV, D)

    def level_last(grid):
        return grid.transpose(1, 2, 0, 3).reshape(columns)

    pair = ((LEV_WIN * PIECE, 2 * D), BF16)
    single = ((LEV_WIN * PIECE // 2, 2 * D), BF16)
    rows = (LEV_WIN, WIN_TOK, D)
    scores = (LEV_WIN, WIN_TOK, LANES)
    parts = [(LEV_WIN * SLAB, FLAT)] * 3
    folded = (ROWS, LEV_WIN * SLAB)
    grid = [(LEV * WIN_LAT * WIN_LON, FLAT)] * 2
    table = (LEV_WIN * SLAB, 3 * FLAT)
    tiles = LEV_WIN * SLAB // SHARE

    first = call(
        first_kernel,
        [pair] * 4
        + [(rows, F32), ((LEV_WIN, WIN_TOK, FLAT), F32), ((LEV_WIN, LANES, D), BF16), (rows, BF16), (rows, BF16), (scores, BF16)],
        parts + [folded, scores] + grid + [(4, LEV_WIN * PIECE, 2 * D)],
        2_000_000_000,
    )(level_last(tokens), level_last(grad_out), bias_one.reshape(flat), *block_one, perm, const["split_t"], const["turn"])
    pieces, saved = first[:4], first[4:]
    pieces, bias_two = lax.optimization_barrier((tuple(pieces), bias_two))
    pieces = exchange(pieces, -1)

    active = jnp.where(lax.axis_index("lat") == lax.axis_size("lat") - 1, 1.0, 0.0).astype(F32).reshape(1, 1)
    (bias_full,) = pl.pallas_call(
        bias_kernel,
        in_specs=[pl.BlockSpec(memory_space=pltpu.SMEM)] + [pl.BlockSpec(memory_space=pltpu.VMEM)] * 2,
        out_shape=[jax.ShapeDtypeStruct(scores, F32)],
        scratch_shapes=[pltpu.VMEM(shape, F32) for shape in parts + [folded]],
        compiler_params=pltpu.CompilerParams(vmem_limit_bytes=VMEM_LIMIT),
        cost_estimate=pl.CostEstimate(flops=500_000_000, bytes_accessed=4_000_000, transcendentals=0),
    )(active, bias_two.reshape(flat), perm)

    second = call(
        second_kernel,
        [single] * 4 + [(scores, BF16)],
        [(LEV_WIN, WIN_TOK, 2 * D), (4, LEV_WIN * PIECE // 2, 2 * D)],
        4_000_000_000,
    )(*pieces, bias_full, *block_two, const["join"], const["join_t"])
    grad_pieces, low_two = second[:4], second[4]
    grad_pieces = exchange(grad_pieces, 1)

    (term_two,) = call(fold_kernel, [((tiles, TERM, FLAT), F32)], [folded, table], 500_000_000)(low_two, perm)

    grid_out, terms = call(
        third_kernel,
        [(columns, BF16), ((tiles, 2 * TERM, FLAT), BF16)],
        [rows] + grid + [folded, table, (tiles, TERM, FLAT)],
        4_000_000_000,
    )(*grad_pieces, *saved, term_two, *block_one, perm, const["split"], const["turn_t"])
    grad_tokens = grid_out.reshape(WIN_LAT, WIN_LON, LEV, D).transpose(2, 0, 1, 3)

    arrived = lax.all_to_all(terms, "lon", 0, 0, tiled=True)
    width = SHARE * ROWS
    summed_one, summed_two = call(
        sum_kernel, [((1, width), F32), ((1, width), F32)], [(2 * TERM, FLAT)], 1_000_000
    )(arrived)
    return grad_tokens, summed_one, summed_two


def solution(mesh):
    in_specs = (
        P(None, "lat", "lon", None),
        P(None, "lat", "lon", None),
        P(),
        P(),
        P(),
        P("lat", None),
        P(),
        P(),
        P(),
        P("lat", None),
    )
    out_specs = (P(None, "lat", "lon", None), P("lat", "lon"), P("lat", "lon"))
    return jax.shard_map(body, mesh=mesh, in_specs=in_specs, out_specs=out_specs, check_vma=False)
```

```python
import math

import jax
import jax.numpy as jnp
import numpy as np
from jax import lax
from jax.experimental import pallas as pl
from jax.experimental.pallas import tpu as pltpu
from jax.sharding import PartitionSpec as P

D = 192
HEADS = 6
HEAD_DIM = 32
WIN_LEV = 2
WIN_LAT = 6
WIN_LON = 12
WIN_TOK = 144
LEV = 8
LEV_WIN = LEV // WIN_LEV
BAND = WIN_LEV * WIN_LAT
OFFSETS = 2 * WIN_LON - 1
ROWS = OFFSETS * BAND
SLAB = HEADS * BAND
LANES = WIN_LON * SLAB
PIECE = 36
FLAT = 128
PERIOD = 32 * ROWS
TERM = 40
SHARE = 18
REST = ROWS - 2 * FLAT
LOG2E = math.log2(math.e)
SCALE = HEAD_DIM ** (-0.5)
BF16 = jnp.bfloat16
F32 = jnp.float32
LEVELS = range(LEV_WIN)


def constants():
    lanes = np.arange(LANES)
    lane_lon, lane_head, lane_pair = lanes // SLAB, lanes // BAND % HEADS, lanes % BAND
    rep = (lane_lon * BAND + lane_pair)[:, None] == np.arange(WIN_TOK)[None, :]
    mask = lane_head[:, None] == (np.arange(D) // HEAD_DIM)[None, :]
    rows = np.arange(ROWS)
    source = (rows % BAND) * OFFSETS + (OFFSETS - 1 - rows // BAND)
    perm = source[:, None] == np.arange(3 * FLAT)[None, :]
    tok = np.arange(WIN_TOK)
    lon, lev, lat = tok // BAND, tok // WIN_LAT % WIN_LEV, tok % WIN_LAT
    within = (lon % 6) * 6 + lev * 3 + lat % 3
    cut = 2 * (lat < 3) + (lon < 6)
    joined = 2 * (lat >= 3) + (lon >= 6)
    split = (cut * PIECE + within)[:, None] == tok[None, :]
    join = (joined * PIECE + within)[:, None] == tok[None, :]
    turn = ((lev * WIN_LAT + lat) * WIN_LON + lon)[:, None] == tok[None, :]
    return dict(
        rep=rep, mask=mask, mask_t=mask.T, perm=perm, split=split, split_t=split.T, join=join, join_t=join.T,
        turn=turn, turn_t=turn.T,
    )


CONST = {name: value.astype(jnp.bfloat16) for name, value in constants().items()}


def dot(a, b, contract=((1,), (0,))):
    return lax.dot_general(a, b, (contract, ((), ())), preferred_element_type=F32)


NT = ((1,), (1,))
TN = ((0,), (0,))


def table_copies(flat_ref, rows_ref, sem):
    return [
        pltpu.make_async_copy(flat_ref.at[:, pl.ds(PERIOD * k, PERIOD)], rows_ref.at[pl.ds(k, 1), :], sem.at[k])
        for k in range(9)
    ]


def expand_table(rows_ref, perm_ref, parts, spread_ref):
    for first in range(32):
        value = rows_ref[:, ROWS * first : ROWS * (first + 1)]
        parts[0][pl.ds(first, 9, stride=32), :] = value[:, :FLAT]
        parts[1][pl.ds(first, 9, stride=32), :] = value[:, FLAT : 2 * FLAT]
        last = jnp.concatenate([value[:, 2 * FLAT :], jnp.zeros((9, 3 * FLAT - ROWS), F32)], 1)
        parts[2][pl.ds(first, 9, stride=32), :] = last
    table = jnp.concatenate([part[...] for part in parts], 1)
    high = table.astype(BF16)
    rest = table - high.astype(F32)
    middle = rest.astype(BF16)
    low = (rest - middle.astype(F32)).astype(BF16)
    perm = perm_ref[...]
    spread_ref[...] = (dot(perm, high, NT) + dot(perm, middle, NT) + dot(perm, low, NT)) * LOG2E


def write_bias(spread_ref, bias_ref, apart=None):
    for query_lon in range(WIN_LON):
        first = (WIN_LON - 1 - query_lon) * BAND
        for v in LEVELS:
            block = spread_ref[first : first + WIN_TOK, v * SLAB : (v + 1) * SLAB]
            if apart is not None:
                block = block + apart
            bias_ref[v, :, query_lon * SLAB : (query_lon + 1) * SLAB] = block


def fold_scores(lows, perm_ref, folded_ref, table_ref, pack_ref):
    folded_ref[...] = jnp.zeros_like(folded_ref)
    wide = [low.astype(F32) for low in lows]
    for query_lon in range(WIN_LON):
        first = (WIN_LON - 1 - query_lon) * BAND
        block = jnp.concatenate([low[:, query_lon * SLAB : (query_lon + 1) * SLAB] for low in wide], 1)
        folded_ref[first : first + WIN_TOK, :] += block
    folded = (folded_ref[...] * (1.0 / SCALE)).astype(BF16)
    table_ref[...] = dot(folded, perm_ref[...], TN)
    for tile in range(LEV_WIN * SLAB // SHARE):
        top = tile * SHARE
        pack_ref[tile, :SHARE, :] = table_ref[top : top + SHARE, :FLAT]
        pack_ref[tile, SHARE : 2 * SHARE, :] = table_ref[top : top + SHARE, FLAT : 2 * FLAT]
        pack_ref[tile, 2 * SHARE : TERM, :] = jnp.zeros((TERM - 2 * SHARE, FLAT), F32)
        for group in range(5):
            count = min(4, SHARE - 4 * group)
            pack_ref[tile, 2 * SHARE : 2 * SHARE + count, group * REST : (group + 1) * REST] = table_ref[
                top + 4 * group : top + 4 * group + count, 2 * FLAT : ROWS
            ]


def load_windows(grid_ref, left_ref, right_ref):
    wide = grid_ref[...].astype(F32).reshape(LEV * BAND // WIN_LEV * WIN_LON, D)
    left_ref[...] = wide[:, :FLAT]
    right_ref[:, : D - FLAT] = wide[:, FLAT:]
    windows = []
    for v in LEVELS:
        halves = []
        for lev in range(WIN_LEV):
            rows = pl.ds(WIN_LEV * v + lev, WIN_LAT * WIN_LON, stride=LEV)
            halves.append(jnp.concatenate([left_ref[rows, :], right_ref[rows, :][:, : D - FLAT]], 1))
        windows.append(jnp.concatenate(halves, 0).astype(BF16))
    return windows


def store_windows(windows, grid_ref, left_ref, right_ref):
    for v in LEVELS:
        for lev in range(WIN_LEV):
            rows = pl.ds(WIN_LEV * v + lev, WIN_LAT * WIN_LON, stride=LEV)
            half = windows[v][lev * WIN_LAT * WIN_LON : (lev + 1) * WIN_LAT * WIN_LON]
            left_ref[rows, :] = half[:, :FLAT]
            right_ref[rows, :] = jnp.concatenate([half[:, FLAT:], jnp.zeros((WIN_LAT * WIN_LON, 2 * FLAT - D), F32)], 1)
    wide = jnp.concatenate([left_ref[...], right_ref[:, : D - FLAT]], 1)
    grid_ref[...] = wide.reshape(WIN_LAT * WIN_LON, LEV, D).astype(BF16)


def forward(inputs, biases, gain, w_qkv, rep, mask):
    centred = [x - jnp.mean(x, -1, keepdims=True) for x in inputs]
    inv_std = [lax.rsqrt(jnp.mean(x * x, -1, keepdims=True) + 1e-05) for x in centred]
    normed = [x * inv for x, inv in zip(centred, inv_std)]
    hidden = [(x * gain).astype(BF16) for x in normed]
    packed = [dot(x, w_qkv).astype(BF16) for x in hidden]
    k_rows = [x[:, D : 2 * D] for x in packed]
    v_rows = [x[:, 2 * D :] for x in packed]
    q_spread = [dot(rep, x[:, :D]).astype(BF16) * mask for x in packed]
    scores = [dot(k, q, NT) * (SCALE * LOG2E) + bias[...] for k, q, bias in zip(k_rows, q_spread, biases)]
    exp_scores = [jnp.exp2(x - jnp.max(x, 0, keepdims=True)) for x in scores]
    attn_probs = [x * (1.0 / jnp.sum(x, 0, keepdims=True)) for x in exp_scores]
    probs_low = [x.astype(BF16) for x in attn_probs]
    return list(zip(normed, inv_std, q_spread, k_rows, v_rows, attn_probs, probs_low))


def gathered(values, weights, rep, mask_t):
    spread = [dot(x, w, TN).astype(BF16) * mask_t for x, w in zip(values, weights)]
    return [dot(x, rep).T.astype(BF16) for x in spread]


def backward(saved, grads, gain, w_qkv_ref, w_proj, rep, mask, mask_t):
    normed, inv_std, q_spread, k_rows, v_rows, attn_probs, probs_low = zip(*saved)
    grad_mixed = [dot(x, w_proj, NT).astype(BF16) for x in grads]
    mixed_spread = [dot(rep, x).astype(BF16) * mask for x in grad_mixed]
    grad_probs = [dot(v, m, NT) for v, m in zip(v_rows, mixed_spread)]
    grad_v = [dot(p, m).astype(BF16) for p, m in zip(probs_low, mixed_spread)]
    lows = [
        ((p * (x - jnp.sum(x * p, 0, keepdims=True))) * SCALE).astype(BF16) for p, x in zip(attn_probs, grad_probs)
    ]
    grad_k = [dot(low, q).astype(BF16) for low, q in zip(lows, q_spread)]
    grad_q = gathered(k_rows, lows, rep, mask_t)
    w_q, w_k, w_v = w_qkv_ref[:, :D], w_qkv_ref[:, D : 2 * D], w_qkv_ref[:, 2 * D :]
    results = []
    for v, grad in enumerate(grads):
        grad_hidden = dot(grad_q[v], w_q, NT) + dot(grad_k[v], w_k, NT) + dot(grad_v[v], w_v, NT)
        grad_normed = grad_hidden * gain
        grad_local = inv_std[v] * (
            grad_normed
            - jnp.mean(grad_normed, -1, keepdims=True)
            - normed[v] * jnp.mean(grad_normed * normed[v], -1, keepdims=True)
        )
        results.append((grad.astype(F32) + grad_local).astype(BF16))
    return results, lows


def first_kernel(
    tokens_hbm, grad_hbm, flat_hbm, gain_hbm, w_qkv_hbm, w_proj_hbm, rep_hbm, mask_hbm, mask_t_hbm, perm_hbm, split_t_hbm, turn_hbm,
    stay_hbm, lon_ref, lat_ref, both_ref, normed_hbm, inv_hbm, q_hbm, k_hbm, v_hbm, probs_hbm,
    part_a, part_b, part_c, spread_ref, bias_ref, left_ref, right_ref, piece_ref, rows_ref, normed_ref, inv_ref,
    tokens_ref, grad_ref, w_qkv_ref, w_proj_ref, rep_ref, mask_ref, mask_t_ref, perm_ref, split_t_ref, turn_ref,
    stay_ref, q_ref, k_ref, v_ref, probs_ref, gain_ref,
    table_sem, in_sem, out_sem,
):
    table = table_copies(flat_hbm, rows_ref, table_sem)
    pairs = (
        (perm_hbm, perm_ref), (tokens_hbm, tokens_ref), (turn_hbm, turn_ref), (gain_hbm, gain_ref), (w_qkv_hbm, w_qkv_ref),
        (rep_hbm, rep_ref), (mask_hbm, mask_ref), (grad_hbm, grad_ref), (mask_t_hbm, mask_t_ref), (w_proj_hbm, w_proj_ref),
        (split_t_hbm, split_t_ref),
    )
    fetch = [pltpu.make_async_copy(src, dst, in_sem.at[k]) for k, (src, dst) in enumerate(pairs)]
    for copy in table + fetch:
        copy.start()
    for copy in fetch[1:5]:
        copy.wait()
    turn = turn_ref[...]
    inputs = [dot(turn, x) for x in load_windows(tokens_ref, left_ref, right_ref)]
    for copy in table + fetch[:1]:
        copy.wait()
    expand_table(rows_ref, perm_ref, (part_a, part_b, part_c), spread_ref)
    write_bias(spread_ref, bias_ref)
    for copy in fetch[5:]:
        copy.wait()
    rep, mask, mask_t = rep_ref[...], mask_ref[...], mask_t_ref[...]
    saved = forward(inputs, [bias_ref.at[v] for v in LEVELS], gain_ref[...], w_qkv_ref[...], rep, mask)
    normed, inv_std, q_spread, k_rows, v_rows, attn_probs, probs_low = zip(*saved)
    for v in LEVELS:
        normed_ref[v] = normed[v]
        inv_ref[v] = jnp.broadcast_to(inv_std[v], (WIN_TOK, FLAT))
        q_ref[v] = q_spread[v]
        k_ref[v] = k_rows[v]
        v_ref[v] = v_rows[v]
        probs_ref[v] = probs_low[v]
    pairs = ((normed_ref, normed_hbm), (inv_ref, inv_hbm), (q_ref, q_hbm), (k_ref, k_hbm), (v_ref, v_hbm), (probs_ref, probs_hbm))
    keep = [pltpu.make_async_copy(src, dst, out_sem.at[k]) for k, (src, dst) in enumerate(pairs)]
    for copy in keep:
        copy.start()
    attended = gathered(v_rows, probs_low, rep, mask_t)
    grads = [dot(turn, x).astype(BF16) for x in load_windows(grad_ref, left_ref, right_ref)]
    split_t = split_t_ref[...]
    for v in LEVELS:
        block_out = (inputs[v] + dot(attended[v], w_proj_ref[...])).astype(BF16)
        piece_ref[:, v * PIECE : (v + 1) * PIECE, :D] = dot(split_t, block_out).reshape(4, PIECE, D)
        piece_ref[:, v * PIECE : (v + 1) * PIECE, D:] = dot(split_t, grads[v]).reshape(4, PIECE, D)
    stay_ref[...] = piece_ref[0].astype(BF16)
    stay = pltpu.make_async_copy(stay_ref, stay_hbm, out_sem.at[6])
    stay.start()
    for place, ref in ((1, lon_ref), (2, lat_ref), (3, both_ref)):
        ref[...] = piece_ref[place].astype(BF16)
    for copy in keep + [stay]:
        copy.wait()


def bias_kernel(active_ref, flat_hbm, perm_ref, bias_ref, part_a, part_b, part_c, spread_ref, rows_ref, sem):
    table = table_copies(flat_hbm, rows_ref, sem)
    for copy in table:
        copy.start()
    for copy in table:
        copy.wait()
    expand_table(rows_ref, perm_ref, (part_a, part_b, part_c), spread_ref)
    blocked = active_ref[0, 0] * (-10000.0 * LOG2E)
    key_lat = lax.broadcasted_iota(jnp.int32, (WIN_TOK, SLAB), 0) % WIN_LAT
    query_lat = lax.broadcasted_iota(jnp.int32, (WIN_TOK, SLAB), 1) % WIN_LAT
    write_bias(spread_ref, bias_ref, jnp.where((key_lat < 3) != (query_lat < 3), blocked, 0.0))


def second_kernel(
    stay_ref, lon_ref, lat_ref, both_ref, bias_ref, gain_ref, w_qkv_ref, w_proj_ref, rep_ref, mask_ref, mask_t_ref, join_ref, join_t_ref,
    stay_out, lon_out, lat_out, both_out, low_ref,
    window_ref, piece_ref,
):
    rep, mask, mask_t = rep_ref[...], mask_ref[...], mask_t_ref[...]
    join, join_t = join_ref[...], join_t_ref[...]
    for place, ref in enumerate((stay_ref, lon_ref, lat_ref, both_ref)):
        wide = ref[...].astype(F32)
        for v in LEVELS:
            window_ref[v, place * PIECE : (place + 1) * PIECE, :] = wide[v * PIECE : (v + 1) * PIECE]
    pairs = [dot(join, window_ref[v].astype(BF16)) for v in LEVELS]
    inputs = [x[:, :D] for x in pairs]
    grads = [x[:, D:].astype(BF16) for x in pairs]
    gain, w_proj = gain_ref[...], w_proj_ref[...]
    saved = forward(inputs, [bias_ref.at[v] for v in LEVELS], gain, w_qkv_ref[...], rep, mask)
    results, lows = backward(saved, grads, gain, w_qkv_ref, w_proj, rep, mask, mask_t)
    for v in LEVELS:
        low_ref[v] = lows[v]
        row, lane = v % 2 * PIECE, v // 2 * D
        piece_ref[:, row : row + PIECE, lane : lane + D] = dot(join_t, results[v]).reshape(4, PIECE, D)
    for place, ref in enumerate((stay_out, lon_out, lat_out, both_out)):
        ref[...] = piece_ref[place].astype(BF16)


def fold_kernel(low_ref, perm_ref, pack_ref, folded_ref, table_ref):
    fold_scores([low_ref[v] for v in LEVELS], perm_ref, folded_ref, table_ref, pack_ref)


def third_kernel(
    stay_ref, lon_ref, lat_ref, both_ref, normed_ref, inv_ref, q_ref, k_ref, v_ref, probs_ref, other_ref,
    gain_ref, w_qkv_ref, w_proj_ref, rep_ref, mask_ref, mask_t_ref, perm_ref, split_ref, turn_t_ref,
    grid_ref, terms_ref,
    window_ref, left_ref, right_ref, folded_ref, table_ref, pack_ref,
):
    rep, mask, mask_t = rep_ref[...], mask_ref[...], mask_t_ref[...]
    split, turn_t = split_ref[...], turn_t_ref[...]
    for place, ref in enumerate((stay_ref, lon_ref, lat_ref, both_ref)):
        wide = ref[...].astype(F32)
        for v in LEVELS:
            row, lane = v % 2 * PIECE, v // 2 * D
            window_ref[v, place * PIECE : (place + 1) * PIECE, :] = wide[row : row + PIECE, lane : lane + D]
    grads = [dot(split, window_ref[v].astype(BF16)).astype(BF16) for v in LEVELS]
    saved = [
        (normed_ref[v], inv_ref[v][:, :1], q_ref[v], k_ref[v], v_ref[v], probs_ref[v].astype(F32), probs_ref[v])
        for v in LEVELS
    ]
    results, lows = backward(saved, grads, gain_ref[...], w_qkv_ref, w_proj_ref[...], rep, mask, mask_t)
    store_windows([dot(turn_t, x) for x in results], grid_ref, left_ref, right_ref)
    fold_scores(lows, perm_ref, folded_ref, table_ref, pack_ref)
    terms_ref[...] = jnp.concatenate([pack_ref[...], other_ref[...]], 1).astype(BF16)


def sum_kernel(arrived_ref, one_ref, two_ref, total_ref):
    total = arrived_ref[0].astype(F32)
    for tile in range(1, arrived_ref.shape[0]):
        total = total + arrived_ref[tile].astype(F32)
    total_ref[...] = total
    for base, out_ref in ((0, one_ref), (TERM, two_ref)):
        for row in range(SHARE):
            lane = ROWS * row
            out_ref[:, lane : lane + FLAT] = total_ref[base + row : base + row + 1, :]
            place = base + SHARE + row
            out_ref[:, lane + FLAT : lane + 2 * FLAT] = total_ref[place : place + 1, :]
            place, shift = base + 2 * SHARE + row % 4, row // 4 * REST
            out_ref[:, lane + 2 * FLAT : lane + ROWS] = total_ref[place : place + 1, shift : shift + REST]


def call(kernel, out_shapes, scratch, flops, scalars=0):
    return pl.pallas_call(
        kernel,
        out_shape=[jax.ShapeDtypeStruct(shape, dtype) for shape, dtype in out_shapes],
        scratch_shapes=[pltpu.VMEM(shape, F32) for shape in scratch],
        compiler_params=pltpu.CompilerParams(vmem_limit_bytes=VMEM_LIMIT),
        cost_estimate=pl.CostEstimate(flops=flops, bytes_accessed=4_000_000, transcendentals=500_000),
    )


ALL_VMEM = 62 * 1024 * 1024
VMEM_LIMIT = 40 * 1024 * 1024
HBM = pl.BlockSpec(memory_space=pltpu.HBM)
VMEM = pl.BlockSpec(memory_space=pltpu.VMEM)


def shifted(axes, by):
    sizes = [lax.axis_size(axis) for axis in axes]
    if len(sizes) == 1:
        return [(i, (i + by) % sizes[0]) for i in range(sizes[0])]
    rows, columns = sizes
    return [
        (a * columns + o, (a + by) % rows * columns + (o + by) % columns)
        for a in range(rows)
        for o in range(columns)
    ]


def exchange(pieces, by):
    stay, lon, lat, both = pieces
    return (
        stay,
        lax.ppermute(lon, ("lon",), shifted(("lon",), by)),
        lax.ppermute(lat, ("lat",), shifted(("lat",), by)),
        lax.ppermute(both, ("lat", "lon"), shifted(("lat", "lon"), by)),
    )


def body(
    tokens, grad_out, gain_one, qkv_one, proj_one, bias_one, gain_two, qkv_two, proj_two, bias_two
):
    const = {name: jnp.asarray(value) for name, value in CONST.items()}
    spread = (const["rep"], const["mask"], const["mask_t"])
    perm = const["perm"]
    block_one = (gain_one.reshape(1, D), qkv_one, proj_one) + spread
    block_two = (gain_two.reshape(1, D), qkv_two, proj_two) + spread
    columns = (WIN_LAT * WIN_LON, LEV, D)

    def level_last(grid):
        return grid.transpose(1, 2, 0, 3).reshape(columns)

    pair = ((LEV_WIN * PIECE, 2 * D), BF16)
    single = ((LEV_WIN * PIECE // 2, 2 * D), BF16)
    rows = (LEV_WIN, WIN_TOK, D)
    scores = (LEV_WIN, WIN_TOK, LANES)
    parts = [(LEV_WIN * SLAB, FLAT)] * 3
    folded = (ROWS, LEV_WIN * SLAB)
    grid = [(LEV * WIN_LAT * WIN_LON, FLAT)] * 2
    table = (LEV_WIN * SLAB, 3 * FLAT)
    tiles = LEV_WIN * SLAB // SHARE

    outs = (
        [pair] * 4
        + [(rows, F32), ((LEV_WIN, WIN_TOK, FLAT), F32), ((LEV_WIN, LANES, D), BF16), (rows, BF16), (rows, BF16), (scores, BF16)]
    )
    table_rows = (9, PERIOD)
    operands = (
        level_last(tokens), level_last(grad_out), bias_one, *block_one, perm, const["split_t"], const["turn"]
    )
    held = [0, 1, 4, 5, 6, 7, 8, 9, 10, 11]
    first = pl.pallas_call(
        first_kernel,
        in_specs=[HBM] * len(operands),
        out_specs=[HBM] + [VMEM] * 3 + [HBM] * 6,
        out_shape=[jax.ShapeDtypeStruct(shape, dtype) for shape, dtype in outs],
        scratch_shapes=[
            pltpu.VMEM(shape, F32)
            for shape in parts
            + [folded, scores]
            + grid
            + [(4, LEV_WIN * PIECE, 2 * D), table_rows, rows, (LEV_WIN, WIN_TOK, FLAT)]
        ]
        + [pltpu.VMEM(operands[k].shape, BF16) for k in held]
        + [pltpu.VMEM(shape, BF16) for shape, _ in [outs[0]] + outs[6:]]
        + [pltpu.VMEM((1, D), F32)]
        + [pltpu.SemaphoreType.DMA((9,)), pltpu.SemaphoreType.DMA((11,)), pltpu.SemaphoreType.DMA((7,))],
        compiler_params=pltpu.CompilerParams(vmem_limit_bytes=ALL_VMEM),
        cost_estimate=pl.CostEstimate(flops=2_000_000_000, bytes_accessed=4_000_000, transcendentals=500_000),
    )(*operands)
    pieces, saved = first[:4], first[4:]
    pieces, bias_two = lax.optimization_barrier((tuple(pieces), bias_two))
    pieces = exchange(pieces, -1)

    active = jnp.where(lax.axis_index("lat") == lax.axis_size("lat") - 1, 1.0, 0.0).astype(F32).reshape(1, 1)
    (bias_full,) = pl.pallas_call(
        bias_kernel,
        in_specs=[pl.BlockSpec(memory_space=pltpu.SMEM), HBM, VMEM],
        out_shape=[jax.ShapeDtypeStruct(scores, F32)],
        scratch_shapes=[pltpu.VMEM(shape, F32) for shape in parts + [folded, table_rows]] + [pltpu.SemaphoreType.DMA((9,))],
        compiler_params=pltpu.CompilerParams(vmem_limit_bytes=VMEM_LIMIT),
        cost_estimate=pl.CostEstimate(flops=500_000_000, bytes_accessed=4_000_000, transcendentals=0),
    )(active, bias_two, perm)

    second = call(
        second_kernel,
        [single] * 4 + [(scores, BF16)],
        [(LEV_WIN, WIN_TOK, 2 * D), (4, LEV_WIN * PIECE // 2, 2 * D)],
        4_000_000_000,
    )(*pieces, bias_full, *block_two, const["join"], const["join_t"])
    grad_pieces, low_two = second[:4], second[4]
    grad_pieces = exchange(grad_pieces, 1)

    (term_two,) = call(fold_kernel, [((tiles, TERM, FLAT), F32)], [folded, table], 500_000_000)(low_two, perm)

    grid_out, terms = call(
        third_kernel,
        [(columns, BF16), ((tiles, 2 * TERM, FLAT), BF16)],
        [rows] + grid + [folded, table, (tiles, TERM, FLAT)],
        4_000_000_000,
    )(*grad_pieces, *saved, term_two, *block_one, perm, const["split"], const["turn_t"])
    grad_tokens = grid_out.reshape(WIN_LAT, WIN_LON, LEV, D).transpose(2, 0, 1, 3)

    arrived = lax.all_to_all(terms, "lon", 0, 0, tiled=True)
    width = SHARE * ROWS
    summed_one, summed_two = call(
        sum_kernel, [((1, width), F32), ((1, width), F32)], [(2 * TERM, FLAT)], 1_000_000
    )(arrived)
    return grad_tokens, summed_one, summed_two


def solution(mesh):
    in_specs = (
        P(None, "lat", "lon", None),
        P(None, "lat", "lon", None),
        P(),
        P(),
        P(),
        P("lat", None),
        P(),
        P(),
        P(),
        P("lat", None),
    )
    out_specs = (P(None, "lat", "lon", None), P("lat", "lon"), P("lat", "lon"))
    return jax.shard_map(body, mesh=mesh, in_specs=in_specs, out_specs=out_specs, check_vma=False)
```

```python
import math

import jax
import jax.numpy as jnp
import numpy as np
from jax import lax
from jax.experimental import pallas as pl
from jax.experimental.pallas import tpu as pltpu
from jax.sharding import PartitionSpec as P

D = 192
HEADS = 6
HEAD_DIM = 32
WIN_LEV = 2
WIN_LAT = 6
WIN_LON = 12
WIN_TOK = 144
LEV = 8
LEV_WIN = LEV // WIN_LEV
BAND = WIN_LEV * WIN_LAT
OFFSETS = 2 * WIN_LON - 1
ROWS = OFFSETS * BAND
SLAB = HEADS * BAND
LANES = WIN_LON * SLAB
PIECE = 36
FLAT = 128
PERIOD = 32 * ROWS
COLUMNS = LEV * WIN_LAT * WIN_LON
TERM = 40
SHARE = 18
REST = ROWS - 2 * FLAT
LOG2E = math.log2(math.e)
SCALE = HEAD_DIM ** (-0.5)
BF16 = jnp.bfloat16
F32 = jnp.float32
LEVELS = range(LEV_WIN)


def constants():
    lanes = np.arange(LANES)
    lane_lon, lane_head, lane_pair = lanes // SLAB, lanes // BAND % HEADS, lanes % BAND
    rep = (lane_lon * BAND + lane_pair)[:, None] == np.arange(WIN_TOK)[None, :]
    mask_t = (np.arange(D) // HEAD_DIM)[:, None] == lane_head[None, :]
    pairs = np.arange(2 * WIN_TOK)
    twice = (pairs // (2 * BAND) * BAND + pairs % BAND)[:, None] == np.arange(WIN_TOK)[None, :]
    rows = np.arange(ROWS)
    source = (rows % BAND) * OFFSETS + (OFFSETS - 1 - rows // BAND)
    perm = source[:, None] == np.arange(3 * FLAT)[None, :]
    tok = np.arange(WIN_TOK)
    lon, lev, lat = tok // BAND, tok // WIN_LAT % WIN_LEV, tok % WIN_LAT
    within = (lon % 6) * 6 + lev * 3 + lat % 3
    cut = 2 * (lat < 3) + (lon < 6)
    joined = 2 * (lat >= 3) + (lon >= 6)
    split = (cut * PIECE + within)[:, None] == tok[None, :]
    join = (joined * PIECE + within)[:, None] == tok[None, :]
    return dict(
        rep=rep, twice=twice, mask_t=mask_t, perm=perm, split=split, split_t=split.T, join=join, join_t=join.T,
    )


CONST = {name: value.astype(jnp.bfloat16) for name, value in constants().items()}


def dot(a, b, contract=((1,), (0,))):
    return lax.dot_general(a, b, (contract, ((), ())), preferred_element_type=F32)


NT = ((1,), (1,))
TN = ((0,), (0,))


def table_copies(flat_ref, rows_ref, sem):
    return [
        pltpu.make_async_copy(flat_ref.at[:, pl.ds(PERIOD * k, PERIOD)], rows_ref.at[pl.ds(k, 1), :], sem.at[k])
        for k in range(9)
    ]


def expand_table(rows_ref, perm_ref, parts, spread_ref):
    for first in range(32):
        value = rows_ref[:, ROWS * first : ROWS * (first + 1)]
        parts[0][pl.ds(first, 9, stride=32), :] = value[:, :FLAT]
        parts[1][pl.ds(first, 9, stride=32), :] = value[:, FLAT : 2 * FLAT]
        last = jnp.concatenate([value[:, 2 * FLAT :], jnp.zeros((9, 3 * FLAT - ROWS), F32)], 1)
        parts[2][pl.ds(first, 9, stride=32), :] = last
    table = jnp.concatenate([part[...] for part in parts], 1)
    high = table.astype(BF16)
    rest = table - high.astype(F32)
    middle = rest.astype(BF16)
    low = (rest - middle.astype(F32)).astype(BF16)
    perm = perm_ref[...]
    spread_ref[...] = (dot(perm, high, NT) + dot(perm, middle, NT) + dot(perm, low, NT)) * LOG2E


def write_bias(spread_ref, bias_ref, apart=None):
    for query_lon in range(WIN_LON):
        first = (WIN_LON - 1 - query_lon) * BAND
        for v in LEVELS:
            block = spread_ref[first : first + WIN_TOK, v * SLAB : (v + 1) * SLAB]
            if apart is not None:
                block = block + apart
            bias_ref[v, :, query_lon * SLAB : (query_lon + 1) * SLAB] = block


def fold_scores(lows, perm_ref, folded_ref, table_ref, pack_ref):
    folded_ref[...] = jnp.zeros_like(folded_ref)
    wide = [low.astype(F32) for low in lows]
    for query_lon in range(WIN_LON):
        first = (WIN_LON - 1 - query_lon) * BAND
        block = jnp.concatenate([low[:, query_lon * SLAB : (query_lon + 1) * SLAB] for low in wide], 1)
        folded_ref[first : first + WIN_TOK, :] += block
    folded = (folded_ref[...] * (1.0 / SCALE)).astype(BF16)
    table_ref[...] = dot(folded, perm_ref[...], TN)
    for tile in range(LEV_WIN * SLAB // SHARE):
        top = tile * SHARE
        pack_ref[tile, :SHARE, :] = table_ref[top : top + SHARE, :FLAT]
        pack_ref[tile, SHARE : 2 * SHARE, :] = table_ref[top : top + SHARE, FLAT : 2 * FLAT]
        pack_ref[tile, 2 * SHARE : TERM, :] = jnp.zeros((TERM - 2 * SHARE, FLAT), F32)
        for group in range(5):
            count = min(4, SHARE - 4 * group)
            pack_ref[tile, 2 * SHARE : 2 * SHARE + count, group * REST : (group + 1) * REST] = table_ref[
                top + 4 * group : top + 4 * group + count, 2 * FLAT : ROWS
            ]


def picks():
    row = lax.broadcasted_iota(jnp.int32, (WIN_TOK, COLUMNS), 0)
    lane = lax.broadcasted_iota(jnp.int32, (WIN_TOK, COLUMNS), 1)
    lon, pair = row // BAND, row % BAND
    place = (pair % WIN_LAT * WIN_LON + lon) * LEV + pair // WIN_LAT
    return [jnp.where(place + WIN_LEV * v == lane, 1.0, 0.0).astype(BF16) for v in LEVELS]


def spreaders():
    row = lax.broadcasted_iota(jnp.int32, (LANES, WIN_TOK), 0)
    lane = lax.broadcasted_iota(jnp.int32, (LANES, WIN_TOK), 1)
    rep = jnp.where(row // SLAB * BAND + row % BAND == lane, 1.0, 0.0).astype(BF16)
    row = lax.broadcasted_iota(jnp.int32, (D, LANES), 0)
    lane = lax.broadcasted_iota(jnp.int32, (D, LANES), 1)
    return rep, jnp.where(row // HEAD_DIM == lane // BAND % HEADS, 1.0, 0.0).astype(BF16)


def load_windows(grid_ref, picked):
    wide = grid_ref[...].astype(F32).reshape(COLUMNS, D).astype(BF16)
    return [dot(pick, wide) for pick in picked]


def store_windows(windows, picked, grid_ref):
    wide = sum(dot(pick, x, TN) for pick, x in zip(picked, windows))
    grid_ref[...] = wide.reshape(WIN_LAT * WIN_LON, LEV, D).astype(BF16)


class Fetch:
    def __init__(self, pairs, sem):
        self.copies = [pltpu.make_async_copy(src, dst, sem.at[k]) for k, (src, dst) in enumerate(pairs)]
        for copy in self.copies:
            copy.start()

    def wait(self, first=0, last=None):
        for copy in self.copies[first:last]:
            copy.wait()


def spread_heads(rows, twice):
    row = lax.broadcasted_iota(jnp.int32, (SLAB, D), 0)
    lane = lax.broadcasted_iota(jnp.int32, (SLAB, D), 1)
    own = jnp.zeros((SLAB, D), F32)
    for head in range(HEADS):
        in_rows = (row >= head * BAND) & (row < (head + 1) * BAND)
        own = jnp.where(in_rows & (lane >= head * HEAD_DIM) & (lane < (head + 1) * HEAD_DIM), 1.0, own)
    own = own.reshape(1, HEADS // 2, 2 * BAND, D)
    spread = []
    for x in rows:
        doubled = dot(twice, x).reshape(WIN_LON, 1, 2 * BAND, D)
        spread.append((doubled * own).reshape(LANES, D).astype(BF16))
    return spread


def project(inputs, gain, w_qkv):
    centred = [x - jnp.mean(x, -1, keepdims=True) for x in inputs]
    inv_std = [lax.rsqrt(jnp.mean(x * x, -1, keepdims=True) + 1e-05) for x in centred]
    normed = [x * inv for x, inv in zip(centred, inv_std)]
    hidden = [(x * gain).astype(BF16) for x in normed]
    packed = [dot(x, w_qkv).astype(BF16) for x in hidden]
    return normed, inv_std, *([x[:, k * D : (k + 1) * D] for x in packed] for k in range(3))


def forward(inputs, biases, gain, w_qkv, twice):
    normed, inv_std, q_rows, k_rows, v_rows = project(inputs, gain, w_qkv)
    q_spread = spread_heads(q_rows, twice)
    scores = [dot(k, q, NT) * (SCALE * LOG2E) + bias[...] for k, q, bias in zip(k_rows, q_spread, biases)]
    exp_scores = [jnp.exp2(x - jnp.max(x, 0, keepdims=True)) for x in scores]
    attn_probs = [x * (1.0 / jnp.sum(x, 0, keepdims=True)) for x in exp_scores]
    probs_low = [x.astype(BF16) for x in attn_probs]
    return normed, inv_std, q_rows, q_spread, k_rows, v_rows, attn_probs, probs_low


def gathered(values, weights, rep, mask_t):
    spread = [dot(x, w, TN).astype(BF16) * mask_t for x, w in zip(values, weights)]
    return [dot(x, rep).T.astype(BF16) for x in spread]


def score_grads(v_rows, attn_probs, grads, w_proj, twice):
    grad_mixed = [dot(x, w_proj, NT).astype(BF16) for x in grads]
    mixed_spread = spread_heads(grad_mixed, twice)
    grad_probs = [dot(v, m, NT) for v, m in zip(v_rows, mixed_spread)]
    lows = [
        ((p * (x - jnp.sum(x * p, 0, keepdims=True))) * SCALE).astype(BF16) for p, x in zip(attn_probs, grad_probs)
    ]
    return grad_mixed, mixed_spread, lows


def input_grads(normed, inv_std, q_spread, k_rows, probs_low, mixed_spread, lows, grads, gain, w_qkv_ref, rep, mask_t):
    grad_q = gathered(k_rows, lows, rep, mask_t)
    grad_k = [dot(low, q).astype(BF16) for low, q in zip(lows, q_spread)]
    grad_v = [dot(p, m).astype(BF16) for p, m in zip(probs_low, mixed_spread)]
    w_q, w_k, w_v = w_qkv_ref[:, :D], w_qkv_ref[:, D : 2 * D], w_qkv_ref[:, 2 * D :]
    results = []
    for v, grad in enumerate(grads):
        grad_hidden = dot(grad_q[v], w_q, NT) + dot(grad_k[v], w_k, NT) + dot(grad_v[v], w_v, NT)
        grad_normed = grad_hidden * gain
        grad_local = inv_std[v] * (
            grad_normed
            - jnp.mean(grad_normed, -1, keepdims=True)
            - normed[v] * jnp.mean(grad_normed * normed[v], -1, keepdims=True)
        )
        results.append((grad.astype(F32) + grad_local).astype(BF16))
    return results


def first_kernel(
    tokens_hbm, grad_hbm, flat_hbm, gain_hbm, w_qkv_hbm, w_proj_hbm, twice_hbm, perm_hbm, split_t_hbm,
    stay_hbm, lon_hbm, lat_hbm, both_hbm, v_hbm, probs_hbm,
    part_a, part_b, part_c, spread_ref, bias_ref, piece_ref, rows_ref, gain_ref,
    tokens_ref, grad_ref, w_qkv_ref, w_proj_ref, twice_ref, perm_ref, split_t_ref, rep_ref, mask_t_ref,
    out_ref, v_ref, probs_ref,
    table_sem, in_sem, out_sem,
):
    table = table_copies(flat_hbm, rows_ref, table_sem)
    for copy in table:
        copy.start()
    fetch = Fetch(
        (
            (perm_hbm, perm_ref), (tokens_hbm, tokens_ref), (gain_hbm, gain_ref), (w_qkv_hbm, w_qkv_ref),
            (twice_hbm, twice_ref), (grad_hbm, grad_ref), (w_proj_hbm, w_proj_ref), (split_t_hbm, split_t_ref),
        ),
        in_sem,
    )
    picked = picks()
    rep_ref[...], mask_t_ref[...] = spreaders()
    for copy in table:
        copy.wait()
    fetch.wait()
    expand_table(rows_ref, perm_ref, (part_a, part_b, part_c), spread_ref)
    write_bias(spread_ref, bias_ref)
    inputs = load_windows(tokens_ref, picked)
    _, _, _, _, _, v_rows, _, probs_low = forward(
        inputs, [bias_ref.at[v] for v in LEVELS], gain_ref[...], w_qkv_ref[...], twice_ref[...]
    )
    for v in LEVELS:
        v_ref[v] = v_rows[v]
        probs_ref[v] = probs_low[v]
    grads = [x.astype(BF16) for x in load_windows(grad_ref, picked)]
    attended = gathered(v_rows, probs_low, rep_ref[...], mask_t_ref[...])
    split_t = split_t_ref[...]
    for v in LEVELS:
        block_out = (inputs[v] + dot(attended[v], w_proj_ref[...])).astype(BF16)
        piece_ref[:, v * PIECE : (v + 1) * PIECE, :D] = dot(split_t, block_out).reshape(4, PIECE, D)
        piece_ref[:, v * PIECE : (v + 1) * PIECE, D:] = dot(split_t, grads[v]).reshape(4, PIECE, D)
    out_ref[...] = piece_ref[...].astype(BF16)
    pairs = [(out_ref.at[k], ref) for k, ref in enumerate((stay_hbm, lon_hbm, lat_hbm, both_hbm))]
    Fetch(pairs + [(v_ref, v_hbm), (probs_ref, probs_hbm)], out_sem).wait()


def bias_kernel(active_ref, flat_hbm, perm_ref, bias_ref, part_a, part_b, part_c, spread_ref, rows_ref, sem):
    table = table_copies(flat_hbm, rows_ref, sem)
    for copy in table:
        copy.start()
    for copy in table:
        copy.wait()
    expand_table(rows_ref, perm_ref, (part_a, part_b, part_c), spread_ref)
    blocked = active_ref[0, 0] * (-10000.0 * LOG2E)
    key_lat = lax.broadcasted_iota(jnp.int32, (WIN_TOK, SLAB), 0) % WIN_LAT
    query_lat = lax.broadcasted_iota(jnp.int32, (WIN_TOK, SLAB), 1) % WIN_LAT
    write_bias(spread_ref, bias_ref, jnp.where((key_lat < 3) != (query_lat < 3), blocked, 0.0))


def second_kernel(
    stay_ref, lon_ref, lat_ref, both_ref, bias_ref, gain_ref, w_qkv_ref, w_proj_ref, rep_ref, twice_ref, mask_t_ref, join_ref, join_t_ref,
    stay_out, lon_out, lat_out, both_out, low_ref,
    window_ref, piece_ref,
):
    twice = twice_ref[...]
    join, join_t = join_ref[...], join_t_ref[...]
    for place, ref in enumerate((stay_ref, lon_ref, lat_ref, both_ref)):
        wide = ref[...].astype(F32)
        for v in LEVELS:
            window_ref[v, place * PIECE : (place + 1) * PIECE, :] = wide[v * PIECE : (v + 1) * PIECE]
    pairs = [dot(join, window_ref[v].astype(BF16)) for v in LEVELS]
    inputs = [x[:, :D] for x in pairs]
    grads = [x[:, D:].astype(BF16) for x in pairs]
    gain, w_proj = gain_ref[...], w_proj_ref[...]
    normed, inv_std, _, q_spread, k_rows, v_rows, attn_probs, probs_low = forward(
        inputs, [bias_ref.at[v] for v in LEVELS], gain, w_qkv_ref[...], twice
    )
    _, mixed_spread, lows = score_grads(v_rows, attn_probs, grads, w_proj, twice)
    results = input_grads(
        normed, inv_std, q_spread, k_rows, probs_low, mixed_spread, lows, grads, gain, w_qkv_ref, rep_ref[...], mask_t_ref[...]
    )
    for v in LEVELS:
        low_ref[v] = lows[v]
        row, lane = v % 2 * PIECE, v // 2 * D
        piece_ref[:, row : row + PIECE, lane : lane + D] = dot(join_t, results[v]).reshape(4, PIECE, D)
    for place, ref in enumerate((stay_out, lon_out, lat_out, both_out)):
        ref[...] = piece_ref[place].astype(BF16)


def fold_kernel(low_ref, perm_ref, pack_ref, folded_ref, table_ref):
    fold_scores([low_ref[v] for v in LEVELS], perm_ref, folded_ref, table_ref, pack_ref)


def third_kernel(
    stay_ref, lon_ref, lat_ref, both_ref, v_ref, probs_ref, other_ref, w_proj_ref, twice_ref, perm_ref, split_ref,
    terms_ref, grad_ref,
    window_ref, folded_ref, table_ref, pack_ref,
):
    split = split_ref[...]
    for place, ref in enumerate((stay_ref, lon_ref, lat_ref, both_ref)):
        wide = ref[...].astype(F32)
        for v in LEVELS:
            row, lane = v % 2 * PIECE, v // 2 * D
            window_ref[v, place * PIECE : (place + 1) * PIECE, :] = wide[row : row + PIECE, lane : lane + D]
    grads = [dot(split, window_ref[v].astype(BF16)).astype(BF16) for v in LEVELS]
    attn_probs = [probs_ref[v].astype(F32) for v in LEVELS]
    _, _, lows = score_grads([v_ref[v] for v in LEVELS], attn_probs, grads, w_proj_ref[...], twice_ref[...])
    for v in LEVELS:
        grad_ref[v] = grads[v]
    fold_scores(lows, perm_ref, folded_ref, table_ref, pack_ref)
    terms_ref[...] = jnp.concatenate([pack_ref[...], other_ref[...]], 1).astype(BF16)


def last_kernel(
    tokens_hbm, probs_hbm, grad_hbm, gain_hbm, w_qkv_hbm, w_proj_hbm, twice_hbm,
    grid_ref,
    tokens_ref, probs_ref, grad_ref, gain_ref, w_qkv_ref, w_proj_ref, twice_ref,
    sem,
):
    fetch = Fetch(
        (
            (tokens_hbm, tokens_ref), (gain_hbm, gain_ref), (w_qkv_hbm, w_qkv_ref), (twice_hbm, twice_ref), (w_proj_hbm, w_proj_ref),
            (grad_hbm, grad_ref), (probs_hbm, probs_ref),
        ),
        sem,
    )
    picked = picks()
    rep, mask_t = spreaders()
    fetch.wait()
    twice, gain = twice_ref[...], gain_ref[...]
    normed, inv_std, q_rows, k_rows, v_rows = project(load_windows(tokens_ref, picked), gain, w_qkv_ref[...])
    grads = [grad_ref[v] for v in LEVELS]
    probs = [probs_ref[v] for v in LEVELS]
    _, mixed_spread, lows = score_grads(v_rows, [x.astype(F32) for x in probs], grads, w_proj_ref[...], twice)
    results = input_grads(
        normed,
        inv_std,
        spread_heads(q_rows, twice),
        k_rows,
        probs,
        mixed_spread,
        lows,
        grads,
        gain,
        w_qkv_ref,
        rep,
        mask_t,
    )
    store_windows(results, picked, grid_ref)


def sum_kernel(arrived_ref, one_ref, two_ref, total_ref):
    total = arrived_ref[0].astype(F32)
    for tile in range(1, arrived_ref.shape[0]):
        total = total + arrived_ref[tile].astype(F32)
    total_ref[...] = total
    for base, out_ref in ((0, one_ref), (TERM, two_ref)):
        for row in range(SHARE):
            lane = ROWS * row
            out_ref[:, lane : lane + FLAT] = total_ref[base + row : base + row + 1, :]
            place = base + SHARE + row
            out_ref[:, lane + FLAT : lane + 2 * FLAT] = total_ref[place : place + 1, :]
            place, shift = base + 2 * SHARE + row % 4, row // 4 * REST
            out_ref[:, lane + 2 * FLAT : lane + ROWS] = total_ref[place : place + 1, shift : shift + REST]


def call(kernel, out_shapes, scratch, flops, scalars=0):
    return pl.pallas_call(
        kernel,
        out_shape=[jax.ShapeDtypeStruct(shape, dtype) for shape, dtype in out_shapes],
        scratch_shapes=[pltpu.VMEM(shape, F32) for shape in scratch],
        compiler_params=pltpu.CompilerParams(vmem_limit_bytes=VMEM_LIMIT),
        cost_estimate=pl.CostEstimate(flops=flops, bytes_accessed=4_000_000, transcendentals=500_000),
    )


ALL_VMEM = 62 * 1024 * 1024
VMEM_LIMIT = 40 * 1024 * 1024
HBM = pl.BlockSpec(memory_space=pltpu.HBM)
VMEM = pl.BlockSpec(memory_space=pltpu.VMEM)


def shifted(axes, by):
    sizes = [lax.axis_size(axis) for axis in axes]
    if len(sizes) == 1:
        return [(i, (i + by) % sizes[0]) for i in range(sizes[0])]
    rows, columns = sizes
    return [
        (a * columns + o, (a + by) % rows * columns + (o + by) % columns)
        for a in range(rows)
        for o in range(columns)
    ]


def exchange(pieces, by):
    stay, lon, lat, both = pieces
    return (
        stay,
        lax.ppermute(lon, ("lon",), shifted(("lon",), by)),
        lax.ppermute(lat, ("lat",), shifted(("lat",), by)),
        lax.ppermute(both, ("lat", "lon"), shifted(("lat", "lon"), by)),
    )


def body(
    tokens, grad_out, gain_one, qkv_one, proj_one, bias_one, gain_two, qkv_two, proj_two, bias_two
):
    const = {name: jnp.asarray(value) for name, value in CONST.items()}
    spread = (const["rep"], const["twice"], const["mask_t"])
    perm = const["perm"]
    block_two = (gain_two.reshape(1, D), qkv_two, proj_two) + spread
    columns = (WIN_LAT * WIN_LON, LEV, D)

    def level_last(grid):
        return grid.transpose(1, 2, 0, 3).reshape(columns)

    pair = ((LEV_WIN * PIECE, 2 * D), BF16)
    single = ((LEV_WIN * PIECE // 2, 2 * D), BF16)
    rows = (LEV_WIN, WIN_TOK, D)
    scores = (LEV_WIN, WIN_TOK, LANES)
    parts = [(LEV_WIN * SLAB, FLAT)] * 3
    folded = (ROWS, LEV_WIN * SLAB)
    table = (LEV_WIN * SLAB, 3 * FLAT)
    tiles = LEV_WIN * SLAB // SHARE

    outs = [pair[0]] * 4 + [rows, scores]
    table_rows = (9, PERIOD)
    operands = (
        level_last(tokens), level_last(grad_out), bias_one, gain_one.reshape(1, D), qkv_one, proj_one,
        const["twice"], perm, const["split_t"],
    )
    held = [0, 1, 4, 5, 6, 7, 8]
    first = pl.pallas_call(
        first_kernel,
        in_specs=[HBM] * len(operands),
        out_specs=[HBM] * len(outs),
        out_shape=[jax.ShapeDtypeStruct(shape, BF16) for shape in outs],
        scratch_shapes=[
            pltpu.VMEM(shape, F32)
            for shape in parts + [folded, scores, (4, LEV_WIN * PIECE, 2 * D), table_rows, (1, D)]
        ]
        + [pltpu.VMEM(operands[k].shape, BF16) for k in held]
        + [pltpu.VMEM(shape, BF16) for shape in ((LANES, WIN_TOK), (D, LANES), (4,) + pair[0], rows, scores)]
        + [pltpu.SemaphoreType.DMA((9,)), pltpu.SemaphoreType.DMA((8,)), pltpu.SemaphoreType.DMA((6,))],
        compiler_params=pltpu.CompilerParams(vmem_limit_bytes=ALL_VMEM),
        cost_estimate=pl.CostEstimate(flops=2_000_000_000, bytes_accessed=4_000_000, transcendentals=500_000),
    )(*operands)
    pieces, saved = first[:4], first[4:]
    pieces, bias_two = lax.optimization_barrier((tuple(pieces), bias_two))
    pieces = exchange(pieces, -1)

    active = jnp.where(lax.axis_index("lat") == lax.axis_size("lat") - 1, 1.0, 0.0).astype(F32).reshape(1, 1)
    (bias_full,) = pl.pallas_call(
        bias_kernel,
        in_specs=[pl.BlockSpec(memory_space=pltpu.SMEM), HBM, VMEM],
        out_shape=[jax.ShapeDtypeStruct(scores, F32)],
        scratch_shapes=[pltpu.VMEM(shape, F32) for shape in parts + [folded, table_rows]] + [pltpu.SemaphoreType.DMA((9,))],
        compiler_params=pltpu.CompilerParams(vmem_limit_bytes=VMEM_LIMIT),
        cost_estimate=pl.CostEstimate(flops=500_000_000, bytes_accessed=4_000_000, transcendentals=0),
    )(active, bias_two, perm)

    second = call(
        second_kernel,
        [single] * 4 + [(scores, BF16)],
        [(LEV_WIN, WIN_TOK, 2 * D), (4, LEV_WIN * PIECE // 2, 2 * D)],
        4_000_000_000,
    )(*pieces, bias_full, *block_two, const["join"], const["join_t"])
    grad_pieces, low_two = second[:4], second[4]
    grad_pieces = exchange(grad_pieces, 1)

    (term_two,) = call(fold_kernel, [((tiles, TERM, FLAT), F32)], [folded, table], 500_000_000)(low_two, perm)

    v_rows, probs = saved
    operands = (*grad_pieces, v_rows, probs, term_two, proj_one, const["twice"], perm, const["split"])
    terms, grads = call(
        third_kernel,
        [((tiles, 2 * TERM, FLAT), BF16), (rows, BF16)],
        [rows, folded, table, (tiles, TERM, FLAT)],
        2_000_000_000,
    )(*operands)

    arrived = lax.all_to_all(terms, "lon", 0, 0, tiled=True)
    operands = (level_last(tokens), probs, grads, gain_one.reshape(1, D), qkv_one, proj_one, const["twice"])
    grid_out = pl.pallas_call(
        last_kernel,
        in_specs=[HBM] * len(operands),
        out_shape=jax.ShapeDtypeStruct(columns, BF16),
        scratch_shapes=[pltpu.VMEM(x.shape, x.dtype) for x in operands]
        + [pltpu.SemaphoreType.DMA((len(operands),))],
        compiler_params=pltpu.CompilerParams(vmem_limit_bytes=ALL_VMEM),
        cost_estimate=pl.CostEstimate(flops=3_000_000_000, bytes_accessed=5_000_000, transcendentals=0),
    )(*operands)
    grad_tokens = grid_out.reshape(WIN_LAT, WIN_LON, LEV, D).transpose(2, 0, 1, 3)
    width = SHARE * ROWS
    summed_one, summed_two = call(
        sum_kernel, [((1, width), F32), ((1, width), F32)], [(2 * TERM, FLAT)], 1_000_000
    )(arrived)
    return grad_tokens, summed_one, summed_two


def solution(mesh):
    in_specs = (
        P(None, "lat", "lon", None),
        P(None, "lat", "lon", None),
        P(),
        P(),
        P(),
        P("lat", None),
        P(),
        P(),
        P(),
        P("lat", None),
    )
    out_specs = (P(None, "lat", "lon", None), P("lat", "lon"), P("lat", "lon"))
    return jax.shard_map(body, mesh=mesh, in_specs=in_specs, out_specs=out_specs, check_vma=False)
```

```python
import math

import jax
import jax.numpy as jnp
import numpy as np
from jax import lax
from jax.experimental import pallas as pl
from jax.experimental.pallas import tpu as pltpu
from jax.sharding import PartitionSpec as P

D = 192
HEADS = 6
HEAD_DIM = 32
WIN_LEV = 2
WIN_LAT = 6
WIN_LON = 12
WIN_TOK = 144
LEV = 8
LEV_WIN = LEV // WIN_LEV
BAND = WIN_LEV * WIN_LAT
OFFSETS = 2 * WIN_LON - 1
ROWS = OFFSETS * BAND
SLAB = HEADS * BAND
LANES = WIN_LON * SLAB
PIECE = 36
FLAT = 128
PERIOD = 32 * ROWS
COLUMNS = LEV * WIN_LAT * WIN_LON
TERM = 40
SHARE = 18
REST = ROWS - 2 * FLAT
LOG2E = math.log2(math.e)
SCALE = HEAD_DIM ** (-0.5)
BF16 = jnp.bfloat16
F32 = jnp.float32
LEVELS = range(LEV_WIN)


def constants():
    lanes = np.arange(LANES)
    lane_lon, lane_head, lane_pair = lanes // SLAB, lanes // BAND % HEADS, lanes % BAND
    rep = (lane_lon * BAND + lane_pair)[:, None] == np.arange(WIN_TOK)[None, :]
    mask_t = (np.arange(D) // HEAD_DIM)[:, None] == lane_head[None, :]
    pairs = np.arange(2 * WIN_TOK)
    twice = (pairs // (2 * BAND) * BAND + pairs % BAND)[:, None] == np.arange(WIN_TOK)[None, :]
    rows = np.arange(ROWS)
    source = (rows % BAND) * OFFSETS + (OFFSETS - 1 - rows // BAND)
    perm = source[:, None] == np.arange(3 * FLAT)[None, :]
    tok = np.arange(WIN_TOK)
    lon, lev, lat = tok // BAND, tok // WIN_LAT % WIN_LEV, tok % WIN_LAT
    within = (lon % 6) * 6 + lev * 3 + lat % 3
    cut = 2 * (lat < 3) + (lon < 6)
    joined = 2 * (lat >= 3) + (lon >= 6)
    split = (cut * PIECE + within)[:, None] == tok[None, :]
    join = (joined * PIECE + within)[:, None] == tok[None, :]
    return dict(
        rep=rep, twice=twice, mask_t=mask_t, perm=perm, split=split, split_t=split.T, join=join, join_t=join.T,
    )


CONST = {name: value.astype(jnp.bfloat16) for name, value in constants().items()}


def dot(a, b, contract=((1,), (0,))):
    return lax.dot_general(a, b, (contract, ((), ())), preferred_element_type=F32)


NT = ((1,), (1,))
TN = ((0,), (0,))


def table_copies(flat_ref, rows_ref, sem):
    return [
        pltpu.make_async_copy(flat_ref.at[:, pl.ds(PERIOD * k, PERIOD)], rows_ref.at[pl.ds(k, 1), :], sem.at[k])
        for k in range(9)
    ]


def expand_table(rows_ref, perm_ref, parts, spread_ref):
    for first in range(32):
        value = rows_ref[:, ROWS * first : ROWS * (first + 1)]
        parts[0][pl.ds(first, 9, stride=32), :] = value[:, :FLAT]
        parts[1][pl.ds(first, 9, stride=32), :] = value[:, FLAT : 2 * FLAT]
        last = jnp.concatenate([value[:, 2 * FLAT :], jnp.zeros((9, 3 * FLAT - ROWS), F32)], 1)
        parts[2][pl.ds(first, 9, stride=32), :] = last
    table = jnp.concatenate([part[...] for part in parts], 1)
    high = table.astype(BF16)
    rest = table - high.astype(F32)
    middle = rest.astype(BF16)
    low = (rest - middle.astype(F32)).astype(BF16)
    perm = perm_ref[...]
    spread = (dot(perm, high, NT) + dot(perm, middle, NT) + dot(perm, low, NT)) * LOG2E
    for v in LEVELS:
        own = spread[:, v * SLAB : (v + 1) * SLAB]
        spread_ref[0, v] = own[: ROWS - BAND]
        spread_ref[1, v] = own[BAND:]


def write_bias(spread_ref, bias_ref, apart=None):
    for query_lon in range(WIN_LON):
        first = WIN_LON - 1 - query_lon
        for v in LEVELS:
            block = spread_ref[first % 2, v, first // 2 * 2 * BAND : first // 2 * 2 * BAND + WIN_TOK, :]
            if apart is not None:
                block = block + apart
            bias_ref[v, :, query_lon * SLAB : (query_lon + 1) * SLAB] = block


def fold_scores(lows, perm_ref, folded_ref, table_ref, pack_ref):
    folded_ref[...] = jnp.zeros_like(folded_ref)
    wide = [low.astype(F32) for low in lows]
    for query_lon in range(WIN_LON):
        first = (WIN_LON - 1 - query_lon) * BAND
        block = jnp.concatenate([low[:, query_lon * SLAB : (query_lon + 1) * SLAB] for low in wide], 1)
        folded_ref[first : first + WIN_TOK, :] += block
    folded = (folded_ref[...] * (1.0 / SCALE)).astype(BF16)
    table_ref[...] = dot(folded, perm_ref[...], TN)
    for tile in range(LEV_WIN * SLAB // SHARE):
        top = tile * SHARE
        pack_ref[tile, :SHARE, :] = table_ref[top : top + SHARE, :FLAT]
        pack_ref[tile, SHARE : 2 * SHARE, :] = table_ref[top : top + SHARE, FLAT : 2 * FLAT]
        pack_ref[tile, 2 * SHARE : TERM, :] = jnp.zeros((TERM - 2 * SHARE, FLAT), F32)
        for group in range(5):
            count = min(4, SHARE - 4 * group)
            pack_ref[tile, 2 * SHARE : 2 * SHARE + count, group * REST : (group + 1) * REST] = table_ref[
                top + 4 * group : top + 4 * group + count, 2 * FLAT : ROWS
            ]


def picks():
    row = lax.broadcasted_iota(jnp.int32, (WIN_TOK, COLUMNS), 0)
    lane = lax.broadcasted_iota(jnp.int32, (WIN_TOK, COLUMNS), 1)
    lon, pair = row // BAND, row % BAND
    place = (pair % WIN_LAT * WIN_LON + lon) * LEV + pair // WIN_LAT
    return [jnp.where(place + WIN_LEV * v == lane, 1.0, 0.0).astype(BF16) for v in LEVELS]


def spreaders():
    row = lax.broadcasted_iota(jnp.int32, (LANES, WIN_TOK), 0)
    lane = lax.broadcasted_iota(jnp.int32, (LANES, WIN_TOK), 1)
    rep = jnp.where(row // SLAB * BAND + row % BAND == lane, 1.0, 0.0).astype(BF16)
    row = lax.broadcasted_iota(jnp.int32, (D, LANES), 0)
    lane = lax.broadcasted_iota(jnp.int32, (D, LANES), 1)
    return rep, jnp.where(row // HEAD_DIM == lane // BAND % HEADS, 1.0, 0.0).astype(BF16)


def load_windows(grid_ref, picked):
    wide = grid_ref[...].astype(F32).reshape(COLUMNS, D).astype(BF16)
    return [dot(pick, wide) for pick in picked]


def store_windows(windows, picked, grid_ref):
    wide = sum(dot(pick, x, TN) for pick, x in zip(picked, windows))
    grid_ref[...] = wide.reshape(WIN_LAT * WIN_LON, LEV, D).astype(BF16)


class Fetch:
    def __init__(self, pairs, sem):
        self.copies = [pltpu.make_async_copy(src, dst, sem.at[k]) for k, (src, dst) in enumerate(pairs)]
        for copy in self.copies:
            copy.start()

    def wait(self, first=0, last=None):
        for copy in self.copies[first:last]:
            copy.wait()


def spread_heads(rows, twice):
    row = lax.broadcasted_iota(jnp.int32, (SLAB, D), 0)
    lane = lax.broadcasted_iota(jnp.int32, (SLAB, D), 1)
    own = jnp.zeros((SLAB, D), F32)
    for head in range(HEADS):
        in_rows = (row >= head * BAND) & (row < (head + 1) * BAND)
        own = jnp.where(in_rows & (lane >= head * HEAD_DIM) & (lane < (head + 1) * HEAD_DIM), 1.0, own)
    own = own.reshape(1, HEADS // 2, 2 * BAND, D)
    spread = []
    for x in rows:
        doubled = dot(twice, x).reshape(WIN_LON, 1, 2 * BAND, D)
        spread.append((doubled * own).reshape(LANES, D).astype(BF16))
    return spread


def project(inputs, gain, w_qkv):
    centred = [x - jnp.mean(x, -1, keepdims=True) for x in inputs]
    inv_std = [lax.rsqrt(jnp.mean(x * x, -1, keepdims=True) + 1e-05) for x in centred]
    normed = [x * inv for x, inv in zip(centred, inv_std)]
    hidden = [(x * gain).astype(BF16) for x in normed]
    packed = [dot(x, w_qkv).astype(BF16) for x in hidden]
    return normed, inv_std, *([x[:, k * D : (k + 1) * D] for x in packed] for k in range(3))


def attend(q_spread, k_rows, biases):
    scores = [dot(k, q, NT) * (SCALE * LOG2E) + bias[...] for k, q, bias in zip(k_rows, q_spread, biases)]
    exp_scores = [jnp.exp2(x - jnp.max(x, 0, keepdims=True)) for x in scores]
    attn_probs = [x * (1.0 / jnp.sum(x, 0, keepdims=True)) for x in exp_scores]
    return attn_probs, [x.astype(BF16) for x in attn_probs]


def gathered(values, weights, rep, mask_t):
    spread = [dot(x, w, TN).astype(BF16) * mask_t for x, w in zip(values, weights)]
    return [dot(x, rep).T.astype(BF16) for x in spread]


def score_grads(v_rows, attn_probs, grads, w_proj, twice):
    grad_mixed = [dot(x, w_proj, NT).astype(BF16) for x in grads]
    mixed_spread = spread_heads(grad_mixed, twice)
    grad_probs = [dot(v, m, NT) for v, m in zip(v_rows, mixed_spread)]
    lows = [
        ((p * (x - jnp.sum(x * p, 0, keepdims=True))) * SCALE).astype(BF16) for p, x in zip(attn_probs, grad_probs)
    ]
    return grad_mixed, mixed_spread, lows


def input_grads(normed, inv_std, q_spread, k_rows, probs_low, mixed_spread, lows, grads, gain, w_qkv_ref, rep, mask_t):
    grad_q = gathered(k_rows, lows, rep, mask_t)
    grad_k = [dot(low, q).astype(BF16) for low, q in zip(lows, q_spread)]
    grad_v = [dot(p, m).astype(BF16) for p, m in zip(probs_low, mixed_spread)]
    w_q, w_k, w_v = w_qkv_ref[:, :D], w_qkv_ref[:, D : 2 * D], w_qkv_ref[:, 2 * D :]
    results = []
    for v, grad in enumerate(grads):
        grad_hidden = dot(grad_q[v], w_q, NT) + dot(grad_k[v], w_k, NT) + dot(grad_v[v], w_v, NT)
        grad_normed = grad_hidden * gain
        grad_local = inv_std[v] * (
            grad_normed
            - jnp.mean(grad_normed, -1, keepdims=True)
            - normed[v] * jnp.mean(grad_normed * normed[v], -1, keepdims=True)
        )
        results.append((grad.astype(F32) + grad_local).astype(BF16))
    return results


def first_kernel(
    tokens_hbm, grad_hbm, flat_hbm, gain_hbm, w_qkv_hbm, w_proj_hbm, twice_hbm, perm_hbm, split_t_hbm,
    stay_hbm, lon_hbm, lat_hbm, both_hbm, v_hbm, probs_hbm,
    part_a, part_b, part_c, spread_ref, bias_ref, piece_ref, rows_ref, gain_ref,
    tokens_ref, grad_ref, w_qkv_ref, w_proj_ref, twice_ref, perm_ref, split_t_ref, rep_ref, mask_t_ref,
    out_ref, v_ref, probs_ref,
    table_sem, in_sem, out_sem, keep_sem,
):
    table = table_copies(flat_hbm, rows_ref, table_sem)
    for copy in table:
        copy.start()
    fetch = Fetch(
        (
            (perm_hbm, perm_ref), (tokens_hbm, tokens_ref), (gain_hbm, gain_ref), (w_qkv_hbm, w_qkv_ref),
            (twice_hbm, twice_ref), (grad_hbm, grad_ref), (w_proj_hbm, w_proj_ref), (split_t_hbm, split_t_ref),
        ),
        in_sem,
    )
    picked = picks()
    rep_ref[...], mask_t_ref[...] = spreaders()
    for copy in table:
        copy.wait()
    fetch.wait()
    inputs = load_windows(tokens_ref, picked)
    expand_table(rows_ref, perm_ref, (part_a, part_b, part_c), spread_ref)
    _, _, q_rows, k_rows, v_rows = project(inputs, gain_ref[...], w_qkv_ref[...])
    q_spread = spread_heads(q_rows, twice_ref[...])
    write_bias(spread_ref, bias_ref)
    _, probs_low = attend(q_spread, k_rows, [bias_ref.at[v] for v in LEVELS])
    for v in LEVELS:
        v_ref[v] = v_rows[v]
        probs_ref[v] = probs_low[v]
    grads = [x.astype(BF16) for x in load_windows(grad_ref, picked)]
    keep = Fetch([(v_ref, v_hbm), (probs_ref, probs_hbm)], keep_sem)
    attended = gathered(v_rows, probs_low, rep_ref[...], mask_t_ref[...])
    split_t = split_t_ref[...]
    for v in LEVELS:
        block_out = (inputs[v] + dot(attended[v], w_proj_ref[...])).astype(BF16)
        piece_ref[:, v * PIECE : (v + 1) * PIECE, :D] = dot(split_t, block_out).reshape(4, PIECE, D)
        piece_ref[:, v * PIECE : (v + 1) * PIECE, D:] = dot(split_t, grads[v]).reshape(4, PIECE, D)
    out_ref[...] = piece_ref[...].astype(BF16)
    pairs = [(out_ref.at[k], ref) for k, ref in enumerate((stay_hbm, lon_hbm, lat_hbm, both_hbm))]
    sent = Fetch(pairs, out_sem)
    keep.wait()
    sent.wait()


def bias_kernel(active_ref, flat_hbm, perm_ref, bias_ref, part_a, part_b, part_c, spread_ref, rows_ref, sem):
    table = table_copies(flat_hbm, rows_ref, sem)
    for copy in table:
        copy.start()
    for copy in table:
        copy.wait()
    expand_table(rows_ref, perm_ref, (part_a, part_b, part_c), spread_ref)
    blocked = active_ref[0, 0] * (-10000.0 * LOG2E)
    key_lat = lax.broadcasted_iota(jnp.int32, (WIN_TOK, SLAB), 0) % WIN_LAT
    query_lat = lax.broadcasted_iota(jnp.int32, (WIN_TOK, SLAB), 1) % WIN_LAT
    write_bias(spread_ref, bias_ref, jnp.where((key_lat < 3) != (query_lat < 3), blocked, 0.0))


def second_kernel(
    stay_ref, lon_ref, lat_ref, both_ref, bias_ref, gain_ref, w_qkv_ref, w_proj_ref, rep_ref, twice_ref, mask_t_ref, join_ref, join_t_ref,
    stay_out, lon_out, lat_out, both_out, low_ref,
    window_ref, piece_ref,
):
    twice = twice_ref[...]
    join, join_t = join_ref[...], join_t_ref[...]
    for place, ref in enumerate((stay_ref, lon_ref, lat_ref, both_ref)):
        wide = ref[...].astype(F32)
        for v in LEVELS:
            window_ref[v, place * PIECE : (place + 1) * PIECE, :] = wide[v * PIECE : (v + 1) * PIECE]
    pairs = [dot(join, window_ref[v].astype(BF16)) for v in LEVELS]
    inputs = [x[:, :D] for x in pairs]
    grads = [x[:, D:].astype(BF16) for x in pairs]
    gain, w_proj = gain_ref[...], w_proj_ref[...]
    normed, inv_std, q_rows, k_rows, v_rows = project(inputs, gain, w_qkv_ref[...])
    q_spread = spread_heads(q_rows, twice)
    attn_probs, probs_low = attend(q_spread, k_rows, [bias_ref.at[v] for v in LEVELS])
    _, mixed_spread, lows = score_grads(v_rows, attn_probs, grads, w_proj, twice)
    results = input_grads(
        normed, inv_std, q_spread, k_rows, probs_low, mixed_spread, lows, grads, gain, w_qkv_ref, rep_ref[...], mask_t_ref[...]
    )
    for v in LEVELS:
        low_ref[v] = lows[v]
        row, lane = v % 2 * PIECE, v // 2 * D
        piece_ref[:, row : row + PIECE, lane : lane + D] = dot(join_t, results[v]).reshape(4, PIECE, D)
    for place, ref in enumerate((stay_out, lon_out, lat_out, both_out)):
        ref[...] = piece_ref[place].astype(BF16)


def fold_kernel(low_ref, perm_ref, pack_ref, folded_ref, table_ref):
    fold_scores([low_ref[v] for v in LEVELS], perm_ref, folded_ref, table_ref, pack_ref)


def third_kernel(
    stay_ref, lon_ref, lat_ref, both_ref, v_ref, probs_ref, other_ref, w_proj_ref, twice_ref, perm_ref, split_ref,
    terms_ref, grad_ref,
    window_ref, folded_ref, table_ref, pack_ref,
):
    split = split_ref[...]
    for place, ref in enumerate((stay_ref, lon_ref, lat_ref, both_ref)):
        wide = ref[...].astype(F32)
        for v in LEVELS:
            row, lane = v % 2 * PIECE, v // 2 * D
            window_ref[v, place * PIECE : (place + 1) * PIECE, :] = wide[row : row + PIECE, lane : lane + D]
    grads = [dot(split, window_ref[v].astype(BF16)).astype(BF16) for v in LEVELS]
    attn_probs = [probs_ref[v].astype(F32) for v in LEVELS]
    _, _, lows = score_grads([v_ref[v] for v in LEVELS], attn_probs, grads, w_proj_ref[...], twice_ref[...])
    for v in LEVELS:
        grad_ref[v] = grads[v]
    fold_scores(lows, perm_ref, folded_ref, table_ref, pack_ref)
    terms_ref[...] = jnp.concatenate([pack_ref[...], other_ref[...]], 1).astype(BF16)


def last_kernel(
    tokens_hbm, probs_hbm, grad_hbm, gain_hbm, w_qkv_hbm, w_proj_hbm, twice_hbm,
    grid_ref,
    tokens_ref, probs_ref, grad_ref, gain_ref, w_qkv_ref, w_proj_ref, twice_ref,
    sem,
):
    fetch = Fetch(
        (
            (tokens_hbm, tokens_ref), (gain_hbm, gain_ref), (w_qkv_hbm, w_qkv_ref), (twice_hbm, twice_ref), (w_proj_hbm, w_proj_ref),
            (grad_hbm, grad_ref), (probs_hbm, probs_ref),
        ),
        sem,
    )
    picked = picks()
    rep, mask_t = spreaders()
    fetch.wait()
    twice, gain = twice_ref[...], gain_ref[...]
    normed, inv_std, q_rows, k_rows, v_rows = project(load_windows(tokens_ref, picked), gain, w_qkv_ref[...])
    grads = [grad_ref[v] for v in LEVELS]
    probs = [probs_ref[v] for v in LEVELS]
    _, mixed_spread, lows = score_grads(v_rows, [x.astype(F32) for x in probs], grads, w_proj_ref[...], twice)
    results = input_grads(
        normed,
        inv_std,
        spread_heads(q_rows, twice),
        k_rows,
        probs,
        mixed_spread,
        lows,
        grads,
        gain,
        w_qkv_ref,
        rep,
        mask_t,
    )
    store_windows(results, picked, grid_ref)


def sum_kernel(arrived_ref, one_ref, two_ref, total_ref):
    total = arrived_ref[0].astype(F32)
    for tile in range(1, arrived_ref.shape[0]):
        total = total + arrived_ref[tile].astype(F32)
    total_ref[...] = total
    for base, out_ref in ((0, one_ref), (TERM, two_ref)):
        for row in range(SHARE):
            lane = ROWS * row
            out_ref[:, lane : lane + FLAT] = total_ref[base + row : base + row + 1, :]
            place = base + SHARE + row
            out_ref[:, lane + FLAT : lane + 2 * FLAT] = total_ref[place : place + 1, :]
            place, shift = base + 2 * SHARE + row % 4, row // 4 * REST
            out_ref[:, lane + 2 * FLAT : lane + ROWS] = total_ref[place : place + 1, shift : shift + REST]


def call(kernel, out_shapes, scratch, flops, scalars=0):
    return pl.pallas_call(
        kernel,
        out_shape=[jax.ShapeDtypeStruct(shape, dtype) for shape, dtype in out_shapes],
        scratch_shapes=[pltpu.VMEM(shape, F32) for shape in scratch],
        compiler_params=pltpu.CompilerParams(vmem_limit_bytes=VMEM_LIMIT),
        cost_estimate=pl.CostEstimate(flops=flops, bytes_accessed=4_000_000, transcendentals=500_000),
    )


ALL_VMEM = 62 * 1024 * 1024
VMEM_LIMIT = 40 * 1024 * 1024
HBM = pl.BlockSpec(memory_space=pltpu.HBM)
VMEM = pl.BlockSpec(memory_space=pltpu.VMEM)


def shifted(axes, by):
    sizes = [lax.axis_size(axis) for axis in axes]
    if len(sizes) == 1:
        return [(i, (i + by) % sizes[0]) for i in range(sizes[0])]
    rows, columns = sizes
    return [
        (a * columns + o, (a + by) % rows * columns + (o + by) % columns)
        for a in range(rows)
        for o in range(columns)
    ]


def exchange(pieces, by):
    stay, lon, lat, both = pieces
    return (
        stay,
        lax.ppermute(lon, ("lon",), shifted(("lon",), by)),
        lax.ppermute(lat, ("lat",), shifted(("lat",), by)),
        lax.ppermute(both, ("lat", "lon"), shifted(("lat", "lon"), by)),
    )


def body(
    tokens, grad_out, gain_one, qkv_one, proj_one, bias_one, gain_two, qkv_two, proj_two, bias_two
):
    const = {name: jnp.asarray(value) for name, value in CONST.items()}
    spread = (const["rep"], const["twice"], const["mask_t"])
    perm = const["perm"]
    block_two = (gain_two.reshape(1, D), qkv_two, proj_two) + spread
    columns = (WIN_LAT * WIN_LON, LEV, D)

    def level_last(grid):
        return grid.transpose(1, 2, 0, 3).reshape(columns)

    pair = ((LEV_WIN * PIECE, 2 * D), BF16)
    single = ((LEV_WIN * PIECE // 2, 2 * D), BF16)
    rows = (LEV_WIN, WIN_TOK, D)
    scores = (LEV_WIN, WIN_TOK, LANES)
    parts = [(LEV_WIN * SLAB, FLAT)] * 3
    spread_rows = (2, LEV_WIN, ROWS - BAND, SLAB)
    folded = (ROWS, LEV_WIN * SLAB)
    table = (LEV_WIN * SLAB, 3 * FLAT)
    tiles = LEV_WIN * SLAB // SHARE

    outs = [pair[0]] * 4 + [rows, scores]
    table_rows = (9, PERIOD)
    operands = (
        level_last(tokens), level_last(grad_out), bias_one, gain_one.reshape(1, D), qkv_one, proj_one,
        const["twice"], perm, const["split_t"],
    )
    held = [0, 1, 4, 5, 6, 7, 8]
    first = pl.pallas_call(
        first_kernel,
        in_specs=[HBM] * len(operands),
        out_specs=[HBM] * len(outs),
        out_shape=[jax.ShapeDtypeStruct(shape, BF16) for shape in outs],
        scratch_shapes=[
            pltpu.VMEM(shape, F32)
            for shape in parts + [spread_rows, scores, (4, LEV_WIN * PIECE, 2 * D), table_rows, (1, D)]
        ]
        + [pltpu.VMEM(operands[k].shape, BF16) for k in held]
        + [pltpu.VMEM(shape, BF16) for shape in ((LANES, WIN_TOK), (D, LANES), (4,) + pair[0], rows, scores)]
        + [pltpu.SemaphoreType.DMA((9,)), pltpu.SemaphoreType.DMA((8,)), pltpu.SemaphoreType.DMA((4,)), pltpu.SemaphoreType.DMA((2,))],
        compiler_params=pltpu.CompilerParams(vmem_limit_bytes=ALL_VMEM),
        cost_estimate=pl.CostEstimate(flops=2_000_000_000, bytes_accessed=4_000_000, transcendentals=500_000),
    )(*operands)
    pieces, saved = first[:4], first[4:]
    pieces, bias_two = lax.optimization_barrier((tuple(pieces), bias_two))
    pieces = exchange(pieces, -1)

    active = jnp.where(lax.axis_index("lat") == lax.axis_size("lat") - 1, 1.0, 0.0).astype(F32).reshape(1, 1)
    (bias_full,) = pl.pallas_call(
        bias_kernel,
        in_specs=[pl.BlockSpec(memory_space=pltpu.SMEM), HBM, VMEM],
        out_shape=[jax.ShapeDtypeStruct(scores, F32)],
        scratch_shapes=[pltpu.VMEM(shape, F32) for shape in parts + [spread_rows, table_rows]] + [pltpu.SemaphoreType.DMA((9,))],
        compiler_params=pltpu.CompilerParams(vmem_limit_bytes=VMEM_LIMIT),
        cost_estimate=pl.CostEstimate(flops=500_000_000, bytes_accessed=4_000_000, transcendentals=0),
    )(active, bias_two, perm)

    second = call(
        second_kernel,
        [single] * 4 + [(scores, BF16)],
        [(LEV_WIN, WIN_TOK, 2 * D), (4, LEV_WIN * PIECE // 2, 2 * D)],
        4_000_000_000,
    )(*pieces, bias_full, *block_two, const["join"], const["join_t"])
    grad_pieces, low_two = second[:4], second[4]
    grad_pieces = exchange(grad_pieces, 1)

    (term_two,) = call(fold_kernel, [((tiles, TERM, FLAT), F32)], [folded, table], 500_000_000)(low_two, perm)

    v_rows, probs = saved
    operands = (*grad_pieces, v_rows, probs, term_two, proj_one, const["twice"], perm, const["split"])
    terms, grads = call(
        third_kernel,
        [((tiles, 2 * TERM, FLAT), BF16), (rows, BF16)],
        [rows, folded, table, (tiles, TERM, FLAT)],
        2_000_000_000,
    )(*operands)

    arrived = lax.all_to_all(terms, "lon", 0, 0, tiled=True)
    operands = (level_last(tokens), probs, grads, gain_one.reshape(1, D), qkv_one, proj_one, const["twice"])
    grid_out = pl.pallas_call(
        last_kernel,
        in_specs=[HBM] * len(operands),
        out_shape=jax.ShapeDtypeStruct(columns, BF16),
        scratch_shapes=[pltpu.VMEM(x.shape, x.dtype) for x in operands]
        + [pltpu.SemaphoreType.DMA((len(operands),))],
        compiler_params=pltpu.CompilerParams(vmem_limit_bytes=ALL_VMEM),
        cost_estimate=pl.CostEstimate(flops=3_000_000_000, bytes_accessed=5_000_000, transcendentals=0),
    )(*operands)
    grad_tokens = grid_out.reshape(WIN_LAT, WIN_LON, LEV, D).transpose(2, 0, 1, 3)
    width = SHARE * ROWS
    summed_one, summed_two = call(
        sum_kernel, [((1, width), F32), ((1, width), F32)], [(2 * TERM, FLAT)], 1_000_000
    )(arrived)
    return grad_tokens, summed_one, summed_two


def solution(mesh):
    in_specs = (
        P(None, "lat", "lon", None),
        P(None, "lat", "lon", None),
        P(),
        P(),
        P(),
        P("lat", None),
        P(),
        P(),
        P(),
        P("lat", None),
    )
    out_specs = (P(None, "lat", "lon", None), P("lat", "lon"), P("lat", "lon"))
    return jax.shard_map(body, mesh=mesh, in_specs=in_specs, out_specs=out_specs, check_vma=False)
```

```python
import math

import jax
import jax.numpy as jnp
import numpy as np
from jax import lax
from jax.experimental import pallas as pl
from jax.experimental.pallas import tpu as pltpu
from jax.sharding import PartitionSpec as P

D = 192
HEADS = 6
HEAD_DIM = 32
WIN_LEV = 2
WIN_LAT = 6
WIN_LON = 12
WIN_TOK = 144
LEV = 8
LEV_WIN = LEV // WIN_LEV
BAND = WIN_LEV * WIN_LAT
OFFSETS = 2 * WIN_LON - 1
ROWS = OFFSETS * BAND
SLAB = HEADS * BAND
LANES = WIN_LON * SLAB
PIECE = 36
FLAT = 128
PERIOD = 32 * ROWS
COLUMNS = LEV * WIN_LAT * WIN_LON
TERM = 40
SHARE = 18
REST = ROWS - 2 * FLAT
LOG2E = math.log2(math.e)
SCALE = HEAD_DIM ** (-0.5)
BF16 = jnp.bfloat16
F32 = jnp.float32
LEVELS = range(LEV_WIN)


def constants():
    lanes = np.arange(LANES)
    lane_lon, lane_head, lane_pair = lanes // SLAB, lanes // BAND % HEADS, lanes % BAND
    rep = (lane_lon * BAND + lane_pair)[:, None] == np.arange(WIN_TOK)[None, :]
    mask_t = (np.arange(D) // HEAD_DIM)[:, None] == lane_head[None, :]
    pairs = np.arange(2 * WIN_TOK)
    twice = (pairs // (2 * BAND) * BAND + pairs % BAND)[:, None] == np.arange(WIN_TOK)[None, :]
    rows = np.arange(ROWS)
    source = (rows % BAND) * OFFSETS + (OFFSETS - 1 - rows // BAND)
    perm = source[:, None] == np.arange(3 * FLAT)[None, :]
    tok = np.arange(WIN_TOK)
    lon, lev, lat = tok // BAND, tok // WIN_LAT % WIN_LEV, tok % WIN_LAT
    within = (lon % 6) * 6 + lev * 3 + lat % 3
    cut = 2 * (lat < 3) + (lon < 6)
    joined = 2 * (lat >= 3) + (lon >= 6)
    split = (cut * PIECE + within)[:, None] == tok[None, :]
    join = (joined * PIECE + within)[:, None] == tok[None, :]
    return dict(
        rep=rep, twice=twice, mask_t=mask_t, perm=perm, split=split, split_t=split.T, join=join, join_t=join.T,
    )


CONST = {name: value.astype(jnp.bfloat16) for name, value in constants().items()}


def dot(a, b, contract=((1,), (0,))):
    return lax.dot_general(a, b, (contract, ((), ())), preferred_element_type=F32)


NT = ((1,), (1,))
TN = ((0,), (0,))


def table_copies(flat_ref, rows_ref, sem):
    return [
        pltpu.make_async_copy(flat_ref.at[:, pl.ds(PERIOD * k, PERIOD)], rows_ref.at[pl.ds(k, 1), :], sem.at[k])
        for k in range(9)
    ]


def expand_table(rows_ref, perm_ref, parts, spread_ref):
    for first in range(32):
        value = rows_ref[:, ROWS * first : ROWS * (first + 1)]
        parts[0][pl.ds(first, 9, stride=32), :] = value[:, :FLAT]
        parts[1][pl.ds(first, 9, stride=32), :] = value[:, FLAT : 2 * FLAT]
        last = jnp.concatenate([value[:, 2 * FLAT :], jnp.zeros((9, 3 * FLAT - ROWS), F32)], 1)
        parts[2][pl.ds(first, 9, stride=32), :] = last
    table = jnp.concatenate([part[...] for part in parts], 1)
    high = table.astype(BF16)
    rest = table - high.astype(F32)
    middle = rest.astype(BF16)
    low = (rest - middle.astype(F32)).astype(BF16)
    perm = perm_ref[...]
    spread = (dot(perm, high, NT) + dot(perm, middle, NT) + dot(perm, low, NT)) * LOG2E
    for v in LEVELS:
        own = spread[:, v * SLAB : (v + 1) * SLAB]
        spread_ref[0, v] = own[: ROWS - BAND]
        spread_ref[1, v] = own[BAND:]


def write_bias(spread_ref, bias_ref, apart=None):
    for query_lon in range(WIN_LON):
        first = WIN_LON - 1 - query_lon
        for v in LEVELS:
            block = spread_ref[first % 2, v, first // 2 * 2 * BAND : first // 2 * 2 * BAND + WIN_TOK, :]
            if apart is not None:
                block = block + apart
            bias_ref[v, :, query_lon * SLAB : (query_lon + 1) * SLAB] = block


def fold_scores(lows, perm_ref, folded_ref, table_ref, pack_ref):
    folded_ref[...] = jnp.zeros_like(folded_ref)
    wide = [low.astype(F32) for low in lows]
    for query_lon in range(WIN_LON):
        first = (WIN_LON - 1 - query_lon) * BAND
        block = jnp.concatenate([low[:, query_lon * SLAB : (query_lon + 1) * SLAB] for low in wide], 1)
        folded_ref[first : first + WIN_TOK, :] += block
    folded = (folded_ref[...] * (1.0 / SCALE)).astype(BF16)
    table_ref[...] = dot(folded, perm_ref[...], TN)
    for tile in range(LEV_WIN * SLAB // SHARE):
        top = tile * SHARE
        pack_ref[tile, :SHARE, :] = table_ref[top : top + SHARE, :FLAT]
        pack_ref[tile, SHARE : 2 * SHARE, :] = table_ref[top : top + SHARE, FLAT : 2 * FLAT]
        pack_ref[tile, 2 * SHARE : TERM, :] = jnp.zeros((TERM - 2 * SHARE, FLAT), F32)
        for group in range(5):
            count = min(4, SHARE - 4 * group)
            pack_ref[tile, 2 * SHARE : 2 * SHARE + count, group * REST : (group + 1) * REST] = table_ref[
                top + 4 * group : top + 4 * group + count, 2 * FLAT : ROWS
            ]


def picks():
    row = lax.broadcasted_iota(jnp.int32, (WIN_TOK, COLUMNS), 0)
    lane = lax.broadcasted_iota(jnp.int32, (WIN_TOK, COLUMNS), 1)
    lon, pair = row // BAND, row % BAND
    place = (pair % WIN_LAT * WIN_LON + lon) * LEV + pair // WIN_LAT
    return [jnp.where(place + WIN_LEV * v == lane, 1.0, 0.0).astype(BF16) for v in LEVELS]


def spreaders():
    row = lax.broadcasted_iota(jnp.int32, (LANES, WIN_TOK), 0)
    lane = lax.broadcasted_iota(jnp.int32, (LANES, WIN_TOK), 1)
    rep = jnp.where(row // SLAB * BAND + row % BAND == lane, 1.0, 0.0).astype(BF16)
    row = lax.broadcasted_iota(jnp.int32, (D, LANES), 0)
    lane = lax.broadcasted_iota(jnp.int32, (D, LANES), 1)
    return rep, jnp.where(row // HEAD_DIM == lane // BAND % HEADS, 1.0, 0.0).astype(BF16)


def load_windows(grid_ref, picked):
    wide = grid_ref[...].astype(F32).reshape(COLUMNS, D).astype(BF16)
    return [dot(pick, wide) for pick in picked]


def store_windows(windows, picked, grid_ref):
    wide = sum(dot(pick, x, TN) for pick, x in zip(picked, windows))
    grid_ref[...] = wide.reshape(WIN_LAT * WIN_LON, LEV, D).astype(BF16)


class Fetch:
    def __init__(self, pairs, sem):
        self.copies = [pltpu.make_async_copy(src, dst, sem.at[k]) for k, (src, dst) in enumerate(pairs)]
        for copy in self.copies:
            copy.start()

    def wait(self, first=0, last=None):
        for copy in self.copies[first:last]:
            copy.wait()


def spread_heads(rows, twice):
    row = lax.broadcasted_iota(jnp.int32, (SLAB, D), 0)
    lane = lax.broadcasted_iota(jnp.int32, (SLAB, D), 1)
    own = jnp.zeros((SLAB, D), F32)
    for head in range(HEADS):
        in_rows = (row >= head * BAND) & (row < (head + 1) * BAND)
        own = jnp.where(in_rows & (lane >= head * HEAD_DIM) & (lane < (head + 1) * HEAD_DIM), 1.0, own)
    own = own.reshape(1, HEADS // 2, 2 * BAND, D)
    spread = []
    for x in rows:
        doubled = dot(twice, x).reshape(WIN_LON, 1, 2 * BAND, D)
        spread.append((doubled * own).reshape(LANES, D).astype(BF16))
    return spread


def project(inputs, gain, w_qkv):
    centred = [x - jnp.mean(x, -1, keepdims=True) for x in inputs]
    inv_std = [lax.rsqrt(jnp.mean(x * x, -1, keepdims=True) + 1e-05) for x in centred]
    normed = [x * inv for x, inv in zip(centred, inv_std)]
    hidden = [(x * gain).astype(BF16) for x in normed]
    packed = [dot(x, w_qkv).astype(BF16) for x in hidden]
    return normed, inv_std, *([x[:, k * D : (k + 1) * D] for x in packed] for k in range(3))


def attend(q_spread, k_rows, biases):
    scores = [dot(k, q, NT) * (SCALE * LOG2E) + bias[...] for k, q, bias in zip(k_rows, q_spread, biases)]
    exp_scores = [jnp.exp2(x - jnp.max(x, 0, keepdims=True)) for x in scores]
    attn_probs = [x * (1.0 / jnp.sum(x, 0, keepdims=True)) for x in exp_scores]
    return attn_probs, [x.astype(BF16) for x in attn_probs]


def gathered(values, weights, rep, mask_t):
    spread = [dot(x, w, TN).astype(BF16) * mask_t for x, w in zip(values, weights)]
    return [dot(x, rep).T.astype(BF16) for x in spread]


def score_grads(v_rows, attn_probs, grads, w_proj, twice):
    grad_mixed = [dot(x, w_proj, NT).astype(BF16) for x in grads]
    mixed_spread = spread_heads(grad_mixed, twice)
    grad_probs = [dot(v, m, NT) for v, m in zip(v_rows, mixed_spread)]
    lows = [
        ((p * (x - jnp.sum(x * p, 0, keepdims=True))) * SCALE).astype(BF16) for p, x in zip(attn_probs, grad_probs)
    ]
    return grad_mixed, mixed_spread, lows


def input_grads(normed, inv_std, q_spread, k_rows, probs_low, mixed_spread, lows, grads, gain, w_qkv_ref, rep, mask_t):
    grad_q = gathered(k_rows, lows, rep, mask_t)
    grad_k = [dot(low, q).astype(BF16) for low, q in zip(lows, q_spread)]
    grad_v = [dot(p, m).astype(BF16) for p, m in zip(probs_low, mixed_spread)]
    w_q, w_k, w_v = w_qkv_ref[:, :D], w_qkv_ref[:, D : 2 * D], w_qkv_ref[:, 2 * D :]
    results = []
    for v, grad in enumerate(grads):
        grad_hidden = dot(grad_q[v], w_q, NT) + dot(grad_k[v], w_k, NT) + dot(grad_v[v], w_v, NT)
        grad_normed = grad_hidden * gain
        grad_local = inv_std[v] * (
            grad_normed
            - jnp.mean(grad_normed, -1, keepdims=True)
            - normed[v] * jnp.mean(grad_normed * normed[v], -1, keepdims=True)
        )
        results.append((grad.astype(F32) + grad_local).astype(BF16))
    return results


def first_kernel(
    tokens_hbm, grad_hbm, flat_hbm, gain_hbm, w_qkv_hbm, w_proj_hbm, twice_hbm, perm_hbm, split_t_hbm,
    stay_hbm, lon_hbm, lat_hbm, both_hbm, v_hbm, probs_hbm,
    part_a, part_b, part_c, spread_ref, bias_ref, piece_ref, rows_ref, gain_ref,
    tokens_ref, grad_ref, w_qkv_ref, w_proj_ref, twice_ref, perm_ref, split_t_ref, rep_ref, mask_t_ref,
    out_ref, v_ref, probs_ref,
    table_sem, in_sem, out_sem, keep_sem,
):
    table = table_copies(flat_hbm, rows_ref, table_sem)
    for copy in table:
        copy.start()
    fetch = Fetch(
        (
            (perm_hbm, perm_ref), (tokens_hbm, tokens_ref), (gain_hbm, gain_ref), (w_qkv_hbm, w_qkv_ref),
            (twice_hbm, twice_ref), (grad_hbm, grad_ref), (w_proj_hbm, w_proj_ref), (split_t_hbm, split_t_ref),
        ),
        in_sem,
    )
    picked = picks()
    rep_ref[...], mask_t_ref[...] = spreaders()
    for copy in table:
        copy.wait()
    fetch.wait()
    inputs = load_windows(tokens_ref, picked)
    expand_table(rows_ref, perm_ref, (part_a, part_b, part_c), spread_ref)
    _, _, q_rows, k_rows, v_rows = project(inputs, gain_ref[...], w_qkv_ref[...])
    q_spread = spread_heads(q_rows, twice_ref[...])
    write_bias(spread_ref, bias_ref)
    _, probs_low = attend(q_spread, k_rows, [bias_ref.at[v] for v in LEVELS])
    for v in LEVELS:
        v_ref[v] = v_rows[v]
        probs_ref[v] = probs_low[v]
    grads = [x.astype(BF16) for x in load_windows(grad_ref, picked)]
    keep = Fetch([(v_ref, v_hbm), (probs_ref, probs_hbm)], keep_sem)
    attended = gathered(v_rows, probs_low, rep_ref[...], mask_t_ref[...])
    split_t = split_t_ref[...]
    for v in LEVELS:
        block_out = (inputs[v] + dot(attended[v], w_proj_ref[...])).astype(BF16)
        piece_ref[:, v * PIECE : (v + 1) * PIECE, :D] = dot(split_t, block_out).reshape(4, PIECE, D)
        piece_ref[:, v * PIECE : (v + 1) * PIECE, D:] = dot(split_t, grads[v]).reshape(4, PIECE, D)
    out_ref[...] = piece_ref[...].astype(BF16)
    pairs = [(out_ref.at[k], ref) for k, ref in enumerate((stay_hbm, lon_hbm, lat_hbm, both_hbm))]
    sent = Fetch(pairs, out_sem)
    keep.wait()
    sent.wait()


def bias_kernel(active_ref, flat_hbm, perm_ref, bias_ref, part_a, part_b, part_c, spread_ref, rows_ref, sem):
    table = table_copies(flat_hbm, rows_ref, sem)
    for copy in table:
        copy.start()
    for copy in table:
        copy.wait()
    expand_table(rows_ref, perm_ref, (part_a, part_b, part_c), spread_ref)
    blocked = active_ref[0, 0] * (-10000.0 * LOG2E)
    key_lat = lax.broadcasted_iota(jnp.int32, (WIN_TOK, SLAB), 0) % WIN_LAT
    query_lat = lax.broadcasted_iota(jnp.int32, (WIN_TOK, SLAB), 1) % WIN_LAT
    write_bias(spread_ref, bias_ref, jnp.where((key_lat < 3) != (query_lat < 3), blocked, 0.0))


def second_kernel(
    stay_ref, lon_ref, lat_ref, both_ref, bias_ref, gain_ref, w_qkv_ref, w_proj_ref, rep_ref, twice_ref, mask_t_ref, join_ref, join_t_ref,
    stay_out, lon_out, lat_out, both_out, low_ref,
    window_ref, piece_ref,
):
    twice = twice_ref[...]
    join, join_t = join_ref[...], join_t_ref[...]
    for place, ref in enumerate((stay_ref, lon_ref, lat_ref, both_ref)):
        wide = ref[...].astype(F32)
        for v in LEVELS:
            window_ref[v, place * PIECE : (place + 1) * PIECE, :] = wide[v * PIECE : (v + 1) * PIECE]
    pairs = [dot(join, window_ref[v].astype(BF16)) for v in LEVELS]
    inputs = [x[:, :D] for x in pairs]
    grads = [x[:, D:].astype(BF16) for x in pairs]
    gain, w_proj = gain_ref[...], w_proj_ref[...]
    normed, inv_std, q_rows, k_rows, v_rows = project(inputs, gain, w_qkv_ref[...])
    q_spread = spread_heads(q_rows, twice)
    attn_probs, probs_low = attend(q_spread, k_rows, [bias_ref.at[v] for v in LEVELS])
    _, mixed_spread, lows = score_grads(v_rows, attn_probs, grads, w_proj, twice)
    results = input_grads(
        normed, inv_std, q_spread, k_rows, probs_low, mixed_spread, lows, grads, gain, w_qkv_ref, rep_ref[...], mask_t_ref[...]
    )
    for v in LEVELS:
        low_ref[v] = lows[v]
        row, lane = v % 2 * PIECE, v // 2 * D
        piece_ref[:, row : row + PIECE, lane : lane + D] = dot(join_t, results[v]).reshape(4, PIECE, D)
    for place, ref in enumerate((stay_out, lon_out, lat_out, both_out)):
        ref[...] = piece_ref[place].astype(BF16)


def fold_kernel(low_ref, perm_ref, pack_ref, folded_ref, table_ref):
    fold_scores([low_ref[v] for v in LEVELS], perm_ref, folded_ref, table_ref, pack_ref)


def third_kernel(
    stay_ref, lon_ref, lat_ref, both_ref, v_ref, probs_ref, other_ref, w_proj_ref, twice_ref, perm_ref, split_ref,
    terms_ref, grad_ref,
    window_ref, folded_ref, table_ref, pack_ref,
):
    split = split_ref[...]
    for place, ref in enumerate((stay_ref, lon_ref, lat_ref, both_ref)):
        wide = ref[...].astype(F32)
        for v in LEVELS:
            row, lane = v % 2 * PIECE, v // 2 * D
            window_ref[v, place * PIECE : (place + 1) * PIECE, :] = wide[row : row + PIECE, lane : lane + D]
    grads = [dot(split, window_ref[v].astype(BF16)).astype(BF16) for v in LEVELS]
    attn_probs = [probs_ref[v].astype(F32) for v in LEVELS]
    _, _, lows = score_grads([v_ref[v] for v in LEVELS], attn_probs, grads, w_proj_ref[...], twice_ref[...])
    for v in LEVELS:
        grad_ref[v] = grads[v]
    fold_scores(lows, perm_ref, folded_ref, table_ref, pack_ref)
    terms_ref[...] = jnp.concatenate([pack_ref[...], other_ref[...]], 1).astype(BF16)


def last_kernel(
    tokens_ref, probs_ref, grad_ref, gain_ref, w_qkv_ref, w_proj_ref, twice_ref,
    grid_ref,
):
    picked = picks()
    rep, mask_t = spreaders()
    twice, gain = twice_ref[...], gain_ref[...]
    normed, inv_std, q_rows, k_rows, v_rows = project(load_windows(tokens_ref, picked), gain, w_qkv_ref[...])
    grads = [grad_ref[v] for v in LEVELS]
    probs = [probs_ref[v] for v in LEVELS]
    _, mixed_spread, lows = score_grads(v_rows, [x.astype(F32) for x in probs], grads, w_proj_ref[...], twice)
    results = input_grads(
        normed,
        inv_std,
        spread_heads(q_rows, twice),
        k_rows,
        probs,
        mixed_spread,
        lows,
        grads,
        gain,
        w_qkv_ref,
        rep,
        mask_t,
    )
    store_windows(results, picked, grid_ref)


def sum_kernel(arrived_ref, one_ref, two_ref, total_ref):
    total = arrived_ref[0].astype(F32)
    for tile in range(1, arrived_ref.shape[0]):
        total = total + arrived_ref[tile].astype(F32)
    total_ref[...] = total
    for base, out_ref in ((0, one_ref), (TERM, two_ref)):
        for row in range(SHARE):
            lane = ROWS * row
            out_ref[:, lane : lane + FLAT] = total_ref[base + row : base + row + 1, :]
            place = base + SHARE + row
            out_ref[:, lane + FLAT : lane + 2 * FLAT] = total_ref[place : place + 1, :]
            place, shift = base + 2 * SHARE + row % 4, row // 4 * REST
            out_ref[:, lane + 2 * FLAT : lane + ROWS] = total_ref[place : place + 1, shift : shift + REST]


def call(kernel, out_shapes, scratch, flops, scalars=0):
    return pl.pallas_call(
        kernel,
        out_shape=[jax.ShapeDtypeStruct(shape, dtype) for shape, dtype in out_shapes],
        scratch_shapes=[pltpu.VMEM(shape, F32) for shape in scratch],
        compiler_params=pltpu.CompilerParams(vmem_limit_bytes=VMEM_LIMIT),
        cost_estimate=pl.CostEstimate(flops=flops, bytes_accessed=4_000_000, transcendentals=500_000),
    )


ALL_VMEM = 62 * 1024 * 1024
VMEM_LIMIT = 40 * 1024 * 1024
HBM = pl.BlockSpec(memory_space=pltpu.HBM)
VMEM = pl.BlockSpec(memory_space=pltpu.VMEM)


def shifted(axes, by):
    sizes = [lax.axis_size(axis) for axis in axes]
    if len(sizes) == 1:
        return [(i, (i + by) % sizes[0]) for i in range(sizes[0])]
    rows, columns = sizes
    return [
        (a * columns + o, (a + by) % rows * columns + (o + by) % columns)
        for a in range(rows)
        for o in range(columns)
    ]


def exchange(pieces, by):
    stay, lon, lat, both = pieces
    return (
        stay,
        lax.ppermute(lon, ("lon",), shifted(("lon",), by)),
        lax.ppermute(lat, ("lat",), shifted(("lat",), by)),
        lax.ppermute(both, ("lat", "lon"), shifted(("lat", "lon"), by)),
    )


def body(
    tokens, grad_out, gain_one, qkv_one, proj_one, bias_one, gain_two, qkv_two, proj_two, bias_two
):
    const = {name: jnp.asarray(value) for name, value in CONST.items()}
    spread = (const["rep"], const["twice"], const["mask_t"])
    perm = const["perm"]
    block_two = (gain_two.reshape(1, D), qkv_two, proj_two) + spread
    columns = (WIN_LAT * WIN_LON, LEV, D)

    def level_last(grid):
        return grid.transpose(1, 2, 0, 3).reshape(columns)

    pair = ((LEV_WIN * PIECE, 2 * D), BF16)
    single = ((LEV_WIN * PIECE // 2, 2 * D), BF16)
    rows = (LEV_WIN, WIN_TOK, D)
    scores = (LEV_WIN, WIN_TOK, LANES)
    parts = [(LEV_WIN * SLAB, FLAT)] * 3
    spread_rows = (2, LEV_WIN, ROWS - BAND, SLAB)
    folded = (ROWS, LEV_WIN * SLAB)
    table = (LEV_WIN * SLAB, 3 * FLAT)
    tiles = LEV_WIN * SLAB // SHARE

    outs = [pair[0]] * 4 + [rows, scores]
    table_rows = (9, PERIOD)
    operands = (
        level_last(tokens), level_last(grad_out), bias_one, gain_one.reshape(1, D), qkv_one, proj_one,
        const["twice"], perm, const["split_t"],
    )
    held = [0, 1, 4, 5, 6, 7, 8]
    first = pl.pallas_call(
        first_kernel,
        in_specs=[HBM] * len(operands),
        out_specs=[HBM] * len(outs),
        out_shape=[jax.ShapeDtypeStruct(shape, BF16) for shape in outs],
        scratch_shapes=[
            pltpu.VMEM(shape, F32)
            for shape in parts + [spread_rows, scores, (4, LEV_WIN * PIECE, 2 * D), table_rows, (1, D)]
        ]
        + [pltpu.VMEM(operands[k].shape, BF16) for k in held]
        + [pltpu.VMEM(shape, BF16) for shape in ((LANES, WIN_TOK), (D, LANES), (4,) + pair[0], rows, scores)]
        + [pltpu.SemaphoreType.DMA((9,)), pltpu.SemaphoreType.DMA((8,)), pltpu.SemaphoreType.DMA((4,)), pltpu.SemaphoreType.DMA((2,))],
        compiler_params=pltpu.CompilerParams(vmem_limit_bytes=ALL_VMEM),
        cost_estimate=pl.CostEstimate(flops=2_000_000_000, bytes_accessed=4_000_000, transcendentals=500_000),
    )(*operands)
    pieces, saved = first[:4], first[4:]
    pieces, bias_two = lax.optimization_barrier((tuple(pieces), bias_two))
    pieces = exchange(pieces, -1)

    active = jnp.where(lax.axis_index("lat") == lax.axis_size("lat") - 1, 1.0, 0.0).astype(F32).reshape(1, 1)
    (bias_full,) = pl.pallas_call(
        bias_kernel,
        in_specs=[pl.BlockSpec(memory_space=pltpu.SMEM), HBM, VMEM],
        out_shape=[jax.ShapeDtypeStruct(scores, F32)],
        scratch_shapes=[pltpu.VMEM(shape, F32) for shape in parts + [spread_rows, table_rows]] + [pltpu.SemaphoreType.DMA((9,))],
        compiler_params=pltpu.CompilerParams(vmem_limit_bytes=VMEM_LIMIT),
        cost_estimate=pl.CostEstimate(flops=500_000_000, bytes_accessed=4_000_000, transcendentals=0),
    )(active, bias_two, perm)

    second = call(
        second_kernel,
        [single] * 4 + [(scores, BF16)],
        [(LEV_WIN, WIN_TOK, 2 * D), (4, LEV_WIN * PIECE // 2, 2 * D)],
        4_000_000_000,
    )(*pieces, bias_full, *block_two, const["join"], const["join_t"])
    grad_pieces, low_two = second[:4], second[4]
    grad_pieces = exchange(grad_pieces, 1)

    (term_two,) = call(fold_kernel, [((tiles, TERM, FLAT), F32)], [folded, table], 500_000_000)(low_two, perm)

    v_rows, probs = saved
    operands = (*grad_pieces, v_rows, probs, term_two, proj_one, const["twice"], perm, const["split"])
    terms, grads = call(
        third_kernel,
        [((tiles, 2 * TERM, FLAT), BF16), (rows, BF16)],
        [rows, folded, table, (tiles, TERM, FLAT)],
        2_000_000_000,
    )(*operands)

    arrived = lax.all_to_all(terms, "lon", 0, 0, tiled=True)
    operands = (level_last(tokens), probs, grads, gain_one.reshape(1, D), qkv_one, proj_one, const["twice"])
    (grid_out,) = call(last_kernel, [(columns, BF16)], [], 3_000_000_000)(*operands)
    grad_tokens = grid_out.reshape(WIN_LAT, WIN_LON, LEV, D).transpose(2, 0, 1, 3)
    width = SHARE * ROWS
    summed_one, summed_two = call(
        sum_kernel, [((1, width), F32), ((1, width), F32)], [(2 * TERM, FLAT)], 1_000_000
    )(arrived)
    return grad_tokens, summed_one, summed_two


def solution(mesh):
    in_specs = (
        P(None, "lat", "lon", None),
        P(None, "lat", "lon", None),
        P(),
        P(),
        P(),
        P("lat", None),
        P(),
        P(),
        P(),
        P("lat", None),
    )
    out_specs = (P(None, "lat", "lon", None), P("lat", "lon"), P("lat", "lon"))
    return jax.shard_map(body, mesh=mesh, in_specs=in_specs, out_specs=out_specs, check_vma=False)
```

```python
import math

import jax
import jax.numpy as jnp
import numpy as np
from jax import lax
from jax.experimental import pallas as pl
from jax.experimental.pallas import tpu as pltpu
from jax.sharding import PartitionSpec as P

D = 192
HEADS = 6
HEAD_DIM = 32
WIN_LEV = 2
WIN_LAT = 6
WIN_LON = 12
WIN_TOK = 144
LEV = 8
LEV_WIN = LEV // WIN_LEV
BAND = WIN_LEV * WIN_LAT
OFFSETS = 2 * WIN_LON - 1
ROWS = OFFSETS * BAND
SLAB = HEADS * BAND
LANES = WIN_LON * SLAB
PIECE = 36
FLAT = 128
PERIOD = 32 * ROWS
COLUMNS = LEV * WIN_LAT * WIN_LON
TERM = 40
SHARE = 18
REST = ROWS - 2 * FLAT
LOG2E = math.log2(math.e)
SCALE = HEAD_DIM ** (-0.5)
BF16 = jnp.bfloat16
F32 = jnp.float32
LEVELS = range(LEV_WIN)


def constants():
    lanes = np.arange(LANES)
    lane_lon, lane_head, lane_pair = lanes // SLAB, lanes // BAND % HEADS, lanes % BAND
    rep = (lane_lon * BAND + lane_pair)[:, None] == np.arange(WIN_TOK)[None, :]
    mask_t = (np.arange(D) // HEAD_DIM)[:, None] == lane_head[None, :]
    pairs = np.arange(2 * WIN_TOK)
    twice = (pairs // (2 * BAND) * BAND + pairs % BAND)[:, None] == np.arange(WIN_TOK)[None, :]
    rows = np.arange(ROWS)
    source = (rows % BAND) * OFFSETS + (OFFSETS - 1 - rows // BAND)
    perm = source[:, None] == np.arange(3 * FLAT)[None, :]
    tok = np.arange(WIN_TOK)
    lon, lev, lat = tok // BAND, tok // WIN_LAT % WIN_LEV, tok % WIN_LAT
    within = (lon % 6) * 6 + lev * 3 + lat % 3
    cut = 2 * (lat < 3) + (lon < 6)
    joined = 2 * (lat >= 3) + (lon >= 6)
    split = (cut * PIECE + within)[:, None] == tok[None, :]
    join = (joined * PIECE + within)[:, None] == tok[None, :]
    return dict(
        rep=rep, twice=twice, mask_t=mask_t, perm=perm, split=split, split_t=split.T, join=join, join_t=join.T,
    )


CONST = {name: value.astype(jnp.bfloat16) for name, value in constants().items()}


def dot(a, b, contract=((1,), (0,))):
    return lax.dot_general(a, b, (contract, ((), ())), preferred_element_type=F32)


NT = ((1,), (1,))
TN = ((0,), (0,))


def table_copies(flat_ref, rows_ref, sem):
    return [
        pltpu.make_async_copy(flat_ref.at[:, pl.ds(PERIOD * k, PERIOD)], rows_ref.at[pl.ds(k, 1), :], sem.at[k])
        for k in range(9)
    ]


def expand_table(rows_ref, perm_ref, parts, spread_ref):
    for first in range(32):
        value = rows_ref[:, ROWS * first : ROWS * (first + 1)]
        parts[0][pl.ds(first, 9, stride=32), :] = value[:, :FLAT]
        parts[1][pl.ds(first, 9, stride=32), :] = value[:, FLAT : 2 * FLAT]
        last = jnp.concatenate([value[:, 2 * FLAT :], jnp.zeros((9, 3 * FLAT - ROWS), F32)], 1)
        parts[2][pl.ds(first, 9, stride=32), :] = last
    table = jnp.concatenate([part[...] for part in parts], 1)
    high = table.astype(BF16)
    rest = table - high.astype(F32)
    middle = rest.astype(BF16)
    low = (rest - middle.astype(F32)).astype(BF16)
    perm = perm_ref[...]
    spread = (dot(perm, high, NT) + dot(perm, middle, NT) + dot(perm, low, NT)) * LOG2E
    for v in LEVELS:
        own = spread[:, v * SLAB : (v + 1) * SLAB]
        spread_ref[0, v] = own[: ROWS - BAND]
        spread_ref[1, v] = own[BAND:]


def write_bias(spread_ref, bias_ref, apart=None):
    for query_lon in range(WIN_LON):
        first = WIN_LON - 1 - query_lon
        for v in LEVELS:
            block = spread_ref[first % 2, v, first // 2 * 2 * BAND : first // 2 * 2 * BAND + WIN_TOK, :]
            if apart is not None:
                block = block + apart
            bias_ref[v, :, query_lon * SLAB : (query_lon + 1) * SLAB] = block


def fold_scores(lows, perm_ref, folded_ref, table_ref, pack_ref):
    folded_ref[...] = jnp.zeros_like(folded_ref)
    wide = [low.astype(F32) for low in lows]
    for query_lon in range(WIN_LON):
        first = (WIN_LON - 1 - query_lon) * BAND
        block = jnp.concatenate([low[:, query_lon * SLAB : (query_lon + 1) * SLAB] for low in wide], 1)
        folded_ref[first : first + WIN_TOK, :] += block
    folded = (folded_ref[...] * (1.0 / SCALE)).astype(BF16)
    table_ref[...] = dot(folded, perm_ref[...], TN)
    for tile in range(LEV_WIN * SLAB // SHARE):
        top = tile * SHARE
        pack_ref[tile, :SHARE, :] = table_ref[top : top + SHARE, :FLAT]
        pack_ref[tile, SHARE : 2 * SHARE, :] = table_ref[top : top + SHARE, FLAT : 2 * FLAT]
        pack_ref[tile, 2 * SHARE : TERM, :] = jnp.zeros((TERM - 2 * SHARE, FLAT), F32)
        for group in range(5):
            count = min(4, SHARE - 4 * group)
            pack_ref[tile, 2 * SHARE : 2 * SHARE + count, group * REST : (group + 1) * REST] = table_ref[
                top + 4 * group : top + 4 * group + count, 2 * FLAT : ROWS
            ]


def picks():
    row = lax.broadcasted_iota(jnp.int32, (WIN_TOK, COLUMNS), 0)
    lane = lax.broadcasted_iota(jnp.int32, (WIN_TOK, COLUMNS), 1)
    lon, pair = row // BAND, row % BAND
    place = (pair % WIN_LAT * WIN_LON + lon) * LEV + pair // WIN_LAT
    return [jnp.where(place + WIN_LEV * v == lane, 1.0, 0.0).astype(BF16) for v in LEVELS]


def spreaders():
    row = lax.broadcasted_iota(jnp.int32, (LANES, WIN_TOK), 0)
    lane = lax.broadcasted_iota(jnp.int32, (LANES, WIN_TOK), 1)
    rep = jnp.where(row // SLAB * BAND + row % BAND == lane, 1.0, 0.0).astype(BF16)
    row = lax.broadcasted_iota(jnp.int32, (D, LANES), 0)
    lane = lax.broadcasted_iota(jnp.int32, (D, LANES), 1)
    return rep, jnp.where(row // HEAD_DIM == lane // BAND % HEADS, 1.0, 0.0).astype(BF16)


def load_windows(grid_ref, picked):
    wide = grid_ref[...].astype(F32).reshape(COLUMNS, D).astype(BF16)
    return [dot(pick, wide) for pick in picked]


def store_windows(windows, picked, grid_ref):
    wide = sum(dot(pick, x, TN) for pick, x in zip(picked, windows))
    grid_ref[...] = wide.reshape(WIN_LAT * WIN_LON, LEV, D).astype(BF16)


class Fetch:
    def __init__(self, pairs, sem):
        self.copies = [pltpu.make_async_copy(src, dst, sem.at[k]) for k, (src, dst) in enumerate(pairs)]
        for copy in self.copies:
            copy.start()

    def wait(self, first=0, last=None):
        for copy in self.copies[first:last]:
            copy.wait()


def spread_heads(rows, twice):
    row = lax.broadcasted_iota(jnp.int32, (SLAB, D), 0)
    lane = lax.broadcasted_iota(jnp.int32, (SLAB, D), 1)
    own = jnp.zeros((SLAB, D), F32)
    for head in range(HEADS):
        in_rows = (row >= head * BAND) & (row < (head + 1) * BAND)
        own = jnp.where(in_rows & (lane >= head * HEAD_DIM) & (lane < (head + 1) * HEAD_DIM), 1.0, own)
    own = own.reshape(1, HEADS // 2, 2 * BAND, D)
    spread = []
    for x in rows:
        doubled = dot(twice, x).reshape(WIN_LON, 1, 2 * BAND, D)
        spread.append((doubled * own).reshape(LANES, D).astype(BF16))
    return spread


def project(inputs, gain, w_qkv):
    centred = [x - jnp.mean(x, -1, keepdims=True) for x in inputs]
    inv_std = [lax.rsqrt(jnp.mean(x * x, -1, keepdims=True) + 1e-05) for x in centred]
    normed = [x * inv for x, inv in zip(centred, inv_std)]
    hidden = [(x * gain).astype(BF16) for x in normed]
    packed = [dot(x, w_qkv).astype(BF16) for x in hidden]
    return normed, inv_std, *([x[:, k * D : (k + 1) * D] for x in packed] for k in range(3))


def attend(q_spread, k_rows, biases):
    scores = [dot(k, q, NT) * (SCALE * LOG2E) + bias[...] for k, q, bias in zip(k_rows, q_spread, biases)]
    exp_scores = [jnp.exp2(x - jnp.max(x, 0, keepdims=True)) for x in scores]
    attn_probs = [x * (1.0 / jnp.sum(x, 0, keepdims=True)) for x in exp_scores]
    return attn_probs, [x.astype(BF16) for x in attn_probs]


def gathered(values, weights, rep, mask_t):
    spread = [dot(x, w, TN).astype(BF16) * mask_t for x, w in zip(values, weights)]
    return [dot(x, rep).T.astype(BF16) for x in spread]


def score_grads(v_rows, attn_probs, grads, w_proj, twice):
    grad_mixed = [dot(x, w_proj, NT).astype(BF16) for x in grads]
    mixed_spread = spread_heads(grad_mixed, twice)
    grad_probs = [dot(v, m, NT) for v, m in zip(v_rows, mixed_spread)]
    lows = [
        ((p * (x - jnp.sum(x * p, 0, keepdims=True))) * SCALE).astype(BF16) for p, x in zip(attn_probs, grad_probs)
    ]
    return grad_mixed, mixed_spread, lows


def input_grads(normed, inv_std, q_spread, k_rows, probs_low, mixed_spread, lows, grads, gain, w_qkv_ref, rep, mask_t):
    grad_q = gathered(k_rows, lows, rep, mask_t)
    grad_k = [dot(low, q).astype(BF16) for low, q in zip(lows, q_spread)]
    grad_v = [dot(p, m).astype(BF16) for p, m in zip(probs_low, mixed_spread)]
    w_q, w_k, w_v = w_qkv_ref[:, :D], w_qkv_ref[:, D : 2 * D], w_qkv_ref[:, 2 * D :]
    results = []
    for v, grad in enumerate(grads):
        grad_hidden = dot(grad_q[v], w_q, NT) + dot(grad_k[v], w_k, NT) + dot(grad_v[v], w_v, NT)
        grad_normed = grad_hidden * gain
        grad_local = inv_std[v] * (
            grad_normed
            - jnp.mean(grad_normed, -1, keepdims=True)
            - normed[v] * jnp.mean(grad_normed * normed[v], -1, keepdims=True)
        )
        results.append((grad.astype(F32) + grad_local).astype(BF16))
    return results


def first_kernel(
    tokens_hbm, grad_hbm, flat_hbm, gain_hbm, w_qkv_hbm, w_proj_hbm, twice_hbm, perm_hbm, split_t_hbm,
    stay_hbm, lon_hbm, lat_hbm, both_hbm, v_hbm, probs_hbm,
    part_a, part_b, part_c, spread_ref, bias_ref, piece_ref, rows_ref, gain_ref,
    tokens_ref, grad_ref, w_qkv_ref, w_proj_ref, twice_ref, perm_ref, split_t_ref, rep_ref, mask_t_ref,
    out_ref, v_ref, probs_ref,
    table_sem, in_sem, out_sem, keep_sem,
):
    table = table_copies(flat_hbm, rows_ref, table_sem)
    for copy in table:
        copy.start()
    fetch = Fetch(
        (
            (perm_hbm, perm_ref), (tokens_hbm, tokens_ref), (gain_hbm, gain_ref), (w_qkv_hbm, w_qkv_ref),
            (twice_hbm, twice_ref), (grad_hbm, grad_ref), (w_proj_hbm, w_proj_ref), (split_t_hbm, split_t_ref),
        ),
        in_sem,
    )
    picked = picks()
    rep_ref[...], mask_t_ref[...] = spreaders()
    for copy in table:
        copy.wait()
    fetch.wait()
    inputs = load_windows(tokens_ref, picked)
    expand_table(rows_ref, perm_ref, (part_a, part_b, part_c), spread_ref)
    _, _, q_rows, k_rows, v_rows = project(inputs, gain_ref[...], w_qkv_ref[...])
    q_spread = spread_heads(q_rows, twice_ref[...])
    write_bias(spread_ref, bias_ref)
    split_t = split_t_ref[...]
    for v, grad in enumerate(load_windows(grad_ref, picked)):
        piece_ref[:, v * PIECE : (v + 1) * PIECE, D:] = dot(split_t, grad.astype(BF16)).reshape(4, PIECE, D)
    _, probs_low = attend(q_spread, k_rows, [bias_ref.at[v] for v in LEVELS])
    for v in LEVELS:
        v_ref[v] = v_rows[v]
        probs_ref[v] = probs_low[v]
    keep = Fetch([(v_ref, v_hbm), (probs_ref, probs_hbm)], keep_sem)
    attended = gathered(v_rows, probs_low, rep_ref[...], mask_t_ref[...])
    split_t = split_t_ref[...]
    for v in LEVELS:
        block_out = (inputs[v] + dot(attended[v], w_proj_ref[...])).astype(BF16)
        piece_ref[:, v * PIECE : (v + 1) * PIECE, :D] = dot(split_t, block_out).reshape(4, PIECE, D)
    out_ref[...] = piece_ref[...].astype(BF16)
    pairs = [(out_ref.at[k], ref) for k, ref in enumerate((stay_hbm, lon_hbm, lat_hbm, both_hbm))]
    sent = Fetch(pairs, out_sem)
    keep.wait()
    sent.wait()


def bias_kernel(active_ref, flat_hbm, perm_ref, bias_ref, part_a, part_b, part_c, spread_ref, rows_ref, sem):
    table = table_copies(flat_hbm, rows_ref, sem)
    for copy in table:
        copy.start()
    for copy in table:
        copy.wait()
    expand_table(rows_ref, perm_ref, (part_a, part_b, part_c), spread_ref)
    blocked = active_ref[0, 0] * (-10000.0 * LOG2E)
    key_lat = lax.broadcasted_iota(jnp.int32, (WIN_TOK, SLAB), 0) % WIN_LAT
    query_lat = lax.broadcasted_iota(jnp.int32, (WIN_TOK, SLAB), 1) % WIN_LAT
    write_bias(spread_ref, bias_ref, jnp.where((key_lat < 3) != (query_lat < 3), blocked, 0.0))


def second_kernel(
    stay_ref, lon_ref, lat_ref, both_ref, bias_ref, gain_ref, w_qkv_ref, w_proj_ref, rep_ref, twice_ref, mask_t_ref, join_ref, join_t_ref,
    stay_out, lon_out, lat_out, both_out, low_ref,
    window_ref, piece_ref,
):
    twice = twice_ref[...]
    join, join_t = join_ref[...], join_t_ref[...]
    for place, ref in enumerate((stay_ref, lon_ref, lat_ref, both_ref)):
        wide = ref[...].astype(F32)
        for v in LEVELS:
            window_ref[v, place * PIECE : (place + 1) * PIECE, :] = wide[v * PIECE : (v + 1) * PIECE]
    pairs = [dot(join, window_ref[v].astype(BF16)) for v in LEVELS]
    inputs = [x[:, :D] for x in pairs]
    grads = [x[:, D:].astype(BF16) for x in pairs]
    gain, w_proj = gain_ref[...], w_proj_ref[...]
    normed, inv_std, q_rows, k_rows, v_rows = project(inputs, gain, w_qkv_ref[...])
    q_spread = spread_heads(q_rows, twice)
    attn_probs, probs_low = attend(q_spread, k_rows, [bias_ref.at[v] for v in LEVELS])
    _, mixed_spread, lows = score_grads(v_rows, attn_probs, grads, w_proj, twice)
    results = []
    for part in (slice(0, 2), slice(2, 4)):
        rows = [x[part] for x in (normed, inv_std, q_spread, k_rows, probs_low, mixed_spread, lows, grads)]
        results += input_grads(*rows, gain, w_qkv_ref, rep_ref[...], mask_t_ref[...])
    for v in LEVELS:
        low_ref[v] = lows[v]
        row, lane = v % 2 * PIECE, v // 2 * D
        piece_ref[:, row : row + PIECE, lane : lane + D] = dot(join_t, results[v]).reshape(4, PIECE, D)
    for place, ref in enumerate((stay_out, lon_out, lat_out, both_out)):
        ref[...] = piece_ref[place].astype(BF16)


def fold_kernel(low_ref, perm_ref, pack_ref, folded_ref, table_ref):
    fold_scores([low_ref[v] for v in LEVELS], perm_ref, folded_ref, table_ref, pack_ref)


def third_kernel(
    stay_ref, lon_ref, lat_ref, both_ref, v_ref, probs_ref, other_ref, w_proj_ref, twice_ref, perm_ref, split_ref,
    terms_ref, grad_ref,
    window_ref, folded_ref, table_ref, pack_ref,
):
    split = split_ref[...]
    for place, ref in enumerate((stay_ref, lon_ref, lat_ref, both_ref)):
        wide = ref[...].astype(F32)
        for v in LEVELS:
            row, lane = v % 2 * PIECE, v // 2 * D
            window_ref[v, place * PIECE : (place + 1) * PIECE, :] = wide[row : row + PIECE, lane : lane + D]
    grads = [dot(split, window_ref[v].astype(BF16)).astype(BF16) for v in LEVELS]
    attn_probs = [probs_ref[v].astype(F32) for v in LEVELS]
    _, _, lows = score_grads([v_ref[v] for v in LEVELS], attn_probs, grads, w_proj_ref[...], twice_ref[...])
    for v in LEVELS:
        grad_ref[v] = grads[v]
    fold_scores(lows, perm_ref, folded_ref, table_ref, pack_ref)
    terms_ref[...] = jnp.concatenate([pack_ref[...], other_ref[...]], 1).astype(BF16)


def last_kernel(
    tokens_ref, probs_ref, grad_ref, gain_ref, w_qkv_ref, w_proj_ref, twice_ref,
    grid_ref,
):
    picked = picks()
    rep, mask_t = spreaders()
    twice, gain = twice_ref[...], gain_ref[...]
    normed, inv_std, q_rows, k_rows, v_rows = project(load_windows(tokens_ref, picked), gain, w_qkv_ref[...])
    grads = [grad_ref[v] for v in LEVELS]
    probs = [probs_ref[v] for v in LEVELS]
    _, mixed_spread, lows = score_grads(v_rows, [x.astype(F32) for x in probs], grads, w_proj_ref[...], twice)
    results = input_grads(
        normed,
        inv_std,
        spread_heads(q_rows, twice),
        k_rows,
        probs,
        mixed_spread,
        lows,
        grads,
        gain,
        w_qkv_ref,
        rep,
        mask_t,
    )
    store_windows(results, picked, grid_ref)


def sum_kernel(arrived_ref, one_ref, two_ref, total_ref):
    total = arrived_ref[0].astype(F32)
    for tile in range(1, arrived_ref.shape[0]):
        total = total + arrived_ref[tile].astype(F32)
    total_ref[...] = total
    for base, out_ref in ((0, one_ref), (TERM, two_ref)):
        for row in range(SHARE):
            lane = ROWS * row
            out_ref[:, lane : lane + FLAT] = total_ref[base + row : base + row + 1, :]
            place = base + SHARE + row
            out_ref[:, lane + FLAT : lane + 2 * FLAT] = total_ref[place : place + 1, :]
            place, shift = base + 2 * SHARE + row % 4, row // 4 * REST
            out_ref[:, lane + 2 * FLAT : lane + ROWS] = total_ref[place : place + 1, shift : shift + REST]


def call(kernel, out_shapes, scratch, flops, scalars=0):
    return pl.pallas_call(
        kernel,
        out_shape=[jax.ShapeDtypeStruct(shape, dtype) for shape, dtype in out_shapes],
        scratch_shapes=[pltpu.VMEM(shape, F32) for shape in scratch],
        compiler_params=pltpu.CompilerParams(vmem_limit_bytes=VMEM_LIMIT),
        cost_estimate=pl.CostEstimate(flops=flops, bytes_accessed=4_000_000, transcendentals=500_000),
    )


ALL_VMEM = 62 * 1024 * 1024
VMEM_LIMIT = 40 * 1024 * 1024
HBM = pl.BlockSpec(memory_space=pltpu.HBM)
VMEM = pl.BlockSpec(memory_space=pltpu.VMEM)


def shifted(axes, by):
    sizes = [lax.axis_size(axis) for axis in axes]
    if len(sizes) == 1:
        return [(i, (i + by) % sizes[0]) for i in range(sizes[0])]
    rows, columns = sizes
    return [
        (a * columns + o, (a + by) % rows * columns + (o + by) % columns)
        for a in range(rows)
        for o in range(columns)
    ]


def exchange(pieces, by):
    stay, lon, lat, both = pieces
    return (
        stay,
        lax.ppermute(lon, ("lon",), shifted(("lon",), by)),
        lax.ppermute(lat, ("lat",), shifted(("lat",), by)),
        lax.ppermute(both, ("lat", "lon"), shifted(("lat", "lon"), by)),
    )


def body(
    tokens, grad_out, gain_one, qkv_one, proj_one, bias_one, gain_two, qkv_two, proj_two, bias_two
):
    const = {name: jnp.asarray(value) for name, value in CONST.items()}
    spread = (const["rep"], const["twice"], const["mask_t"])
    perm = const["perm"]
    block_two = (gain_two.reshape(1, D), qkv_two, proj_two) + spread
    columns = (WIN_LAT * WIN_LON, LEV, D)

    def level_last(grid):
        return grid.transpose(1, 2, 0, 3).reshape(columns)

    pair = ((LEV_WIN * PIECE, 2 * D), BF16)
    single = ((LEV_WIN * PIECE // 2, 2 * D), BF16)
    rows = (LEV_WIN, WIN_TOK, D)
    scores = (LEV_WIN, WIN_TOK, LANES)
    parts = [(LEV_WIN * SLAB, FLAT)] * 3
    spread_rows = (2, LEV_WIN, ROWS - BAND, SLAB)
    folded = (ROWS, LEV_WIN * SLAB)
    table = (LEV_WIN * SLAB, 3 * FLAT)
    tiles = LEV_WIN * SLAB // SHARE

    outs = [pair[0]] * 4 + [rows, scores]
    table_rows = (9, PERIOD)
    operands = (
        level_last(tokens), level_last(grad_out), bias_one, gain_one.reshape(1, D), qkv_one, proj_one,
        const["twice"], perm, const["split_t"],
    )
    held = [0, 1, 4, 5, 6, 7, 8]
    first = pl.pallas_call(
        first_kernel,
        in_specs=[HBM] * len(operands),
        out_specs=[HBM] * len(outs),
        out_shape=[jax.ShapeDtypeStruct(shape, BF16) for shape in outs],
        scratch_shapes=[
            pltpu.VMEM(shape, F32)
            for shape in parts + [spread_rows, scores, (4, LEV_WIN * PIECE, 2 * D), table_rows, (1, D)]
        ]
        + [pltpu.VMEM(operands[k].shape, BF16) for k in held]
        + [pltpu.VMEM(shape, BF16) for shape in ((LANES, WIN_TOK), (D, LANES), (4,) + pair[0], rows, scores)]
        + [pltpu.SemaphoreType.DMA((9,)), pltpu.SemaphoreType.DMA((8,)), pltpu.SemaphoreType.DMA((4,)), pltpu.SemaphoreType.DMA((2,))],
        compiler_params=pltpu.CompilerParams(vmem_limit_bytes=ALL_VMEM),
        cost_estimate=pl.CostEstimate(flops=2_000_000_000, bytes_accessed=4_000_000, transcendentals=500_000),
    )(*operands)
    pieces, saved = first[:4], first[4:]
    pieces, bias_two = lax.optimization_barrier((tuple(pieces), bias_two))
    pieces = exchange(pieces, -1)

    active = jnp.where(lax.axis_index("lat") == lax.axis_size("lat") - 1, 1.0, 0.0).astype(F32).reshape(1, 1)
    (bias_full,) = pl.pallas_call(
        bias_kernel,
        in_specs=[pl.BlockSpec(memory_space=pltpu.SMEM), HBM, VMEM],
        out_shape=[jax.ShapeDtypeStruct(scores, F32)],
        scratch_shapes=[pltpu.VMEM(shape, F32) for shape in parts + [spread_rows, table_rows]] + [pltpu.SemaphoreType.DMA((9,))],
        compiler_params=pltpu.CompilerParams(vmem_limit_bytes=VMEM_LIMIT),
        cost_estimate=pl.CostEstimate(flops=500_000_000, bytes_accessed=4_000_000, transcendentals=0),
    )(active, bias_two, perm)

    second = call(
        second_kernel,
        [single] * 4 + [(scores, BF16)],
        [(LEV_WIN, WIN_TOK, 2 * D), (4, LEV_WIN * PIECE // 2, 2 * D)],
        4_000_000_000,
    )(*pieces, bias_full, *block_two, const["join"], const["join_t"])
    grad_pieces, low_two = second[:4], second[4]
    grad_pieces = exchange(grad_pieces, 1)

    (term_two,) = call(fold_kernel, [((tiles, TERM, FLAT), F32)], [folded, table], 500_000_000)(low_two, perm)

    v_rows, probs = saved
    operands = (*grad_pieces, v_rows, probs, term_two, proj_one, const["twice"], perm, const["split"])
    terms, grads = call(
        third_kernel,
        [((tiles, 2 * TERM, FLAT), BF16), (rows, BF16)],
        [rows, folded, table, (tiles, TERM, FLAT)],
        2_000_000_000,
    )(*operands)

    arrived = lax.all_to_all(terms, "lon", 0, 0, tiled=True)
    operands = (level_last(tokens), probs, grads, gain_one.reshape(1, D), qkv_one, proj_one, const["twice"])
    (grid_out,) = call(last_kernel, [(columns, BF16)], [], 3_000_000_000)(*operands)
    grad_tokens = grid_out.reshape(WIN_LAT, WIN_LON, LEV, D).transpose(2, 0, 1, 3)
    width = SHARE * ROWS
    summed_one, summed_two = call(
        sum_kernel, [((1, width), F32), ((1, width), F32)], [(2 * TERM, FLAT)], 1_000_000
    )(arrived)
    return grad_tokens, summed_one, summed_two


def solution(mesh):
    in_specs = (
        P(None, "lat", "lon", None),
        P(None, "lat", "lon", None),
        P(),
        P(),
        P(),
        P("lat", None),
        P(),
        P(),
        P(),
        P("lat", None),
    )
    out_specs = (P(None, "lat", "lon", None), P("lat", "lon"), P("lat", "lon"))
    return jax.shard_map(body, mesh=mesh, in_specs=in_specs, out_specs=out_specs, check_vma=False)
```

```python
import math

import jax
import jax.numpy as jnp
import numpy as np
from jax import lax
from jax.experimental import pallas as pl
from jax.experimental.pallas import tpu as pltpu
from jax.sharding import PartitionSpec as P

D = 192
HEADS = 6
HEAD_DIM = 32
WIN_LEV = 2
WIN_LAT = 6
WIN_LON = 12
WIN_TOK = 144
LEV = 8
LEV_WIN = LEV // WIN_LEV
BAND = WIN_LEV * WIN_LAT
OFFSETS = 2 * WIN_LON - 1
ROWS = OFFSETS * BAND
SLAB = HEADS * BAND
LANES = WIN_LON * SLAB
PIECE = 36
FLAT = 128
PERIOD = 32 * ROWS
COLUMNS = LEV * WIN_LAT * WIN_LON
TERM = 40
SHARE = 18
REST = ROWS - 2 * FLAT
LOG2E = math.log2(math.e)
SCALE = HEAD_DIM ** (-0.5)
BF16 = jnp.bfloat16
F32 = jnp.float32
LEVELS = range(LEV_WIN)


def constants():
    lanes = np.arange(LANES)
    lane_lon, lane_head, lane_pair = lanes // SLAB, lanes // BAND % HEADS, lanes % BAND
    rep = (lane_lon * BAND + lane_pair)[:, None] == np.arange(WIN_TOK)[None, :]
    mask_t = (np.arange(D) // HEAD_DIM)[:, None] == lane_head[None, :]
    pairs = np.arange(2 * WIN_TOK)
    twice = (pairs // (2 * BAND) * BAND + pairs % BAND)[:, None] == np.arange(WIN_TOK)[None, :]
    rows = np.arange(ROWS)
    source = (rows % BAND) * OFFSETS + (OFFSETS - 1 - rows // BAND)
    perm = source[:, None] == np.arange(3 * FLAT)[None, :]
    tok = np.arange(WIN_TOK)
    lon, lev, lat = tok // BAND, tok // WIN_LAT % WIN_LEV, tok % WIN_LAT
    within = (lon % 6) * 6 + lev * 3 + lat % 3
    cut = 2 * (lat < 3) + (lon < 6)
    joined = 2 * (lat >= 3) + (lon >= 6)
    split = (cut * PIECE + within)[:, None] == tok[None, :]
    join = (joined * PIECE + within)[:, None] == tok[None, :]
    return dict(
        rep=rep, twice=twice, mask_t=mask_t, perm=perm, split=split, split_t=split.T, join=join, join_t=join.T,
    )


CONST = {name: value.astype(jnp.bfloat16) for name, value in constants().items()}


def dot(a, b, contract=((1,), (0,))):
    return lax.dot_general(a, b, (contract, ((), ())), preferred_element_type=F32)


NT = ((1,), (1,))
TN = ((0,), (0,))


def table_copies(flat_ref, rows_ref, sem):
    return [
        pltpu.make_async_copy(flat_ref.at[:, pl.ds(PERIOD * k, PERIOD)], rows_ref.at[pl.ds(k, 1), :], sem.at[k])
        for k in range(9)
    ]


def expand_table(rows_ref, perm_ref, parts, spread_ref):
    for first in range(32):
        value = rows_ref[:, ROWS * first : ROWS * (first + 1)]
        parts[0][pl.ds(first, 9, stride=32), :] = value[:, :FLAT]
        parts[1][pl.ds(first, 9, stride=32), :] = value[:, FLAT : 2 * FLAT]
        last = jnp.concatenate([value[:, 2 * FLAT :], jnp.zeros((9, 3 * FLAT - ROWS), F32)], 1)
        parts[2][pl.ds(first, 9, stride=32), :] = last
    table = jnp.concatenate([part[...] for part in parts], 1)
    high = table.astype(BF16)
    rest = table - high.astype(F32)
    middle = rest.astype(BF16)
    low = (rest - middle.astype(F32)).astype(BF16)
    perm = perm_ref[...]
    spread = (dot(perm, high, NT) + dot(perm, middle, NT) + dot(perm, low, NT)) * LOG2E
    for v in LEVELS:
        own = spread[:, v * SLAB : (v + 1) * SLAB]
        spread_ref[0, v] = own[: ROWS - BAND]
        spread_ref[1, v] = own[BAND:]


def write_bias(spread_ref, bias_ref, apart=None):
    for query_lon in range(WIN_LON):
        first = WIN_LON - 1 - query_lon
        for v in LEVELS:
            block = spread_ref[first % 2, v, first // 2 * 2 * BAND : first // 2 * 2 * BAND + WIN_TOK, :]
            if apart is not None:
                block = block + apart
            bias_ref[v, :, query_lon * SLAB : (query_lon + 1) * SLAB] = block


def fold_scores(lows, factor, perm_ref, folded_ref, table_ref, pack_ref):
    folded_ref[...] = jnp.zeros_like(folded_ref)
    wide = [low.astype(F32) for low in lows]
    for query_lon in range(WIN_LON):
        first = (WIN_LON - 1 - query_lon) * BAND
        block = jnp.concatenate([low[:, query_lon * SLAB : (query_lon + 1) * SLAB] for low in wide], 1)
        folded_ref[first : first + WIN_TOK, :] += block
    folded = (folded_ref[...] * factor).astype(BF16)
    table_ref[...] = dot(folded, perm_ref[...], TN)
    for tile in range(LEV_WIN * SLAB // SHARE):
        top = tile * SHARE
        pack_ref[tile, :SHARE, :] = table_ref[top : top + SHARE, :FLAT]
        pack_ref[tile, SHARE : 2 * SHARE, :] = table_ref[top : top + SHARE, FLAT : 2 * FLAT]
        pack_ref[tile, 2 * SHARE : TERM, :] = jnp.zeros((TERM - 2 * SHARE, FLAT), F32)
        for group in range(5):
            count = min(4, SHARE - 4 * group)
            pack_ref[tile, 2 * SHARE : 2 * SHARE + count, group * REST : (group + 1) * REST] = table_ref[
                top + 4 * group : top + 4 * group + count, 2 * FLAT : ROWS
            ]


def picks():
    row = lax.broadcasted_iota(jnp.int32, (WIN_TOK, COLUMNS), 0)
    lane = lax.broadcasted_iota(jnp.int32, (WIN_TOK, COLUMNS), 1)
    lon, pair = row // BAND, row % BAND
    place = (pair % WIN_LAT * WIN_LON + lon) * LEV + pair // WIN_LAT
    return [jnp.where(place + WIN_LEV * v == lane, 1.0, 0.0).astype(BF16) for v in LEVELS]


def spreaders():
    row = lax.broadcasted_iota(jnp.int32, (LANES, WIN_TOK), 0)
    lane = lax.broadcasted_iota(jnp.int32, (LANES, WIN_TOK), 1)
    rep = jnp.where(row // SLAB * BAND + row % BAND == lane, 1.0, 0.0).astype(BF16)
    row = lax.broadcasted_iota(jnp.int32, (D, LANES), 0)
    lane = lax.broadcasted_iota(jnp.int32, (D, LANES), 1)
    return rep, jnp.where(row // HEAD_DIM == lane // BAND % HEADS, 1.0, 0.0).astype(BF16)


def load_windows(grid_ref, picked):
    wide = grid_ref[...].astype(F32).reshape(COLUMNS, D).astype(BF16)
    return [dot(pick, wide) for pick in picked]


def store_windows(windows, picked, grid_ref):
    wide = sum(dot(pick, x, TN) for pick, x in zip(picked, windows))
    grid_ref[...] = wide.reshape(WIN_LAT * WIN_LON, LEV, D).astype(BF16)


class Fetch:
    def __init__(self, pairs, sem):
        self.copies = [pltpu.make_async_copy(src, dst, sem.at[k]) for k, (src, dst) in enumerate(pairs)]
        for copy in self.copies:
            copy.start()

    def wait(self, first=0, last=None):
        for copy in self.copies[first:last]:
            copy.wait()


def spread_heads(rows, twice):
    row = lax.broadcasted_iota(jnp.int32, (SLAB, D), 0)
    lane = lax.broadcasted_iota(jnp.int32, (SLAB, D), 1)
    own = jnp.zeros((SLAB, D), F32)
    for head in range(HEADS):
        in_rows = (row >= head * BAND) & (row < (head + 1) * BAND)
        own = jnp.where(in_rows & (lane >= head * HEAD_DIM) & (lane < (head + 1) * HEAD_DIM), 1.0, own)
    own = own.reshape(1, HEADS // 2, 2 * BAND, D)
    spread = []
    for x in rows:
        doubled = dot(twice, x).reshape(WIN_LON, 1, 2 * BAND, D)
        spread.append((doubled * own).reshape(LANES, D).astype(BF16))
    return spread


def project(inputs, gain, w_qkv):
    centred = [x - jnp.mean(x, -1, keepdims=True) for x in inputs]
    inv_std = [lax.rsqrt(jnp.mean(x * x, -1, keepdims=True) + 1e-05) for x in centred]
    normed = [x * inv for x, inv in zip(centred, inv_std)]
    hidden = [(x * gain).astype(BF16) for x in normed]
    packed = [dot(x, w_qkv).astype(BF16) for x in hidden]
    return normed, inv_std, *([x[:, k * D : (k + 1) * D] for x in packed] for k in range(3))


def attend(q_spread, k_rows, biases):
    scores = [dot(k, q, NT) * (SCALE * LOG2E) + bias[...] for k, q, bias in zip(k_rows, q_spread, biases)]
    exp_scores = [jnp.exp2(x - jnp.max(x, 0, keepdims=True)) for x in scores]
    attn_probs = [x * (1.0 / jnp.sum(x, 0, keepdims=True)) for x in exp_scores]
    return attn_probs, [x.astype(BF16) for x in attn_probs]


def gathered(values, weights, rep, mask_t):
    spread = [dot(x, w, TN).astype(BF16) * mask_t for x, w in zip(values, weights)]
    return [dot(x, rep).T.astype(BF16) for x in spread]


def score_grads(v_rows, attn_probs, grads, w_proj, twice, scale=SCALE):
    grad_mixed = [dot(x, w_proj, NT).astype(BF16) for x in grads]
    mixed_spread = spread_heads(grad_mixed, twice)
    grad_probs = [dot(v, m, NT) for v, m in zip(v_rows, mixed_spread)]
    lows = [
        (p * (x - jnp.sum(x * p, 0, keepdims=True)) * scale).astype(BF16) for p, x in zip(attn_probs, grad_probs)
    ]
    return grad_mixed, mixed_spread, lows


def input_grads(normed, inv_std, q_spread, k_rows, probs_low, mixed_spread, lows, grads, gain, w_qkv_ref, rep, mask_t):
    grad_q = gathered(k_rows, lows, rep, mask_t)
    grad_k = [dot(low, q).astype(BF16) for low, q in zip(lows, q_spread)]
    grad_v = [dot(p, m).astype(BF16) for p, m in zip(probs_low, mixed_spread)]
    w_q, w_k, w_v = w_qkv_ref[:, :D], w_qkv_ref[:, D : 2 * D], w_qkv_ref[:, 2 * D :]
    results = []
    for v, grad in enumerate(grads):
        grad_hidden = dot(grad_q[v], w_q, NT) + dot(grad_k[v], w_k, NT) + dot(grad_v[v], w_v, NT)
        grad_normed = grad_hidden * gain
        grad_local = inv_std[v] * (
            grad_normed
            - jnp.mean(grad_normed, -1, keepdims=True)
            - normed[v] * jnp.mean(grad_normed * normed[v], -1, keepdims=True)
        )
        results.append((grad.astype(F32) + grad_local).astype(BF16))
    return results


def first_kernel(
    tokens_hbm, grad_hbm, flat_hbm, gain_hbm, w_qkv_hbm, w_proj_hbm, twice_hbm, perm_hbm, split_t_hbm,
    stay_hbm, lon_hbm, lat_hbm, both_hbm, v_hbm, probs_hbm,
    part_a, part_b, part_c, spread_ref, bias_ref, piece_ref, rows_ref, gain_ref,
    tokens_ref, grad_ref, w_qkv_ref, w_proj_ref, twice_ref, perm_ref, split_t_ref, rep_ref, mask_t_ref,
    out_ref, v_ref, probs_ref,
    table_sem, in_sem, out_sem, keep_sem,
):
    table = table_copies(flat_hbm, rows_ref, table_sem)
    for copy in table:
        copy.start()
    fetch = Fetch(
        (
            (perm_hbm, perm_ref), (tokens_hbm, tokens_ref), (gain_hbm, gain_ref), (w_qkv_hbm, w_qkv_ref),
            (twice_hbm, twice_ref), (grad_hbm, grad_ref), (w_proj_hbm, w_proj_ref), (split_t_hbm, split_t_ref),
        ),
        in_sem,
    )
    picked = picks()
    rep_ref[...], mask_t_ref[...] = spreaders()
    for copy in table:
        copy.wait()
    fetch.wait()
    inputs = load_windows(tokens_ref, picked)
    expand_table(rows_ref, perm_ref, (part_a, part_b, part_c), spread_ref)
    _, _, q_rows, k_rows, v_rows = project(inputs, gain_ref[...], w_qkv_ref[...])
    q_spread = spread_heads(q_rows, twice_ref[...])
    split_t = split_t_ref[...]
    for v, grad in enumerate(load_windows(grad_ref, picked)):
        piece_ref[:, v * PIECE : (v + 1) * PIECE, D:] = dot(split_t, grad.astype(BF16)).reshape(4, PIECE, D)
    write_bias(spread_ref, bias_ref)
    _, probs_low = attend(q_spread, k_rows, [bias_ref.at[v] for v in LEVELS])
    for v in LEVELS:
        v_ref[v] = v_rows[v]
        probs_ref[v] = probs_low[v]
    attended = gathered(v_rows, probs_low, rep_ref[...], mask_t_ref[...])
    keep = Fetch([(v_ref, v_hbm), (probs_ref, probs_hbm)], keep_sem)
    split_t = split_t_ref[...]
    for v in LEVELS:
        block_out = (inputs[v] + dot(attended[v], w_proj_ref[...])).astype(BF16)
        piece_ref[:, v * PIECE : (v + 1) * PIECE, :D] = dot(split_t, block_out).reshape(4, PIECE, D)
    out_ref[...] = piece_ref[...].astype(BF16)
    pairs = [(out_ref.at[k], ref) for k, ref in enumerate((stay_hbm, lon_hbm, lat_hbm, both_hbm))]
    sent = Fetch(pairs, out_sem)
    keep.wait()
    sent.wait()


def bias_kernel(active_ref, flat_hbm, perm_ref, bias_ref, part_a, part_b, part_c, spread_ref, rows_ref, sem):
    table = table_copies(flat_hbm, rows_ref, sem)
    for copy in table:
        copy.start()
    for copy in table:
        copy.wait()
    expand_table(rows_ref, perm_ref, (part_a, part_b, part_c), spread_ref)
    blocked = active_ref[0, 0] * (-10000.0 * LOG2E)
    key_lat = lax.broadcasted_iota(jnp.int32, (WIN_TOK, SLAB), 0) % WIN_LAT
    query_lat = lax.broadcasted_iota(jnp.int32, (WIN_TOK, SLAB), 1) % WIN_LAT
    write_bias(spread_ref, bias_ref, jnp.where((key_lat < 3) != (query_lat < 3), blocked, 0.0))


def second_kernel(
    stay_ref, lon_ref, lat_ref, both_ref, bias_ref, gain_ref, w_qkv_ref, w_proj_ref, rep_ref, twice_ref, mask_t_ref, join_ref, join_t_ref,
    stay_out, lon_out, lat_out, both_out, low_ref,
    window_ref, piece_ref,
):
    twice = twice_ref[...]
    join, join_t = join_ref[...], join_t_ref[...]
    for place, ref in enumerate((stay_ref, lon_ref, lat_ref, both_ref)):
        wide = ref[...].astype(F32)
        for v in LEVELS:
            window_ref[v, place * PIECE : (place + 1) * PIECE, :] = wide[v * PIECE : (v + 1) * PIECE]
    pairs = [dot(join, window_ref[v].astype(BF16)) for v in LEVELS]
    inputs = [x[:, :D] for x in pairs]
    grads = [x[:, D:].astype(BF16) for x in pairs]
    gain, w_proj = gain_ref[...], w_proj_ref[...]
    normed, inv_std, q_rows, k_rows, v_rows = project(inputs, gain, w_qkv_ref[...])
    q_spread = spread_heads(q_rows, twice)
    attn_probs, probs_low = attend(q_spread, k_rows, [bias_ref.at[v] for v in LEVELS])
    _, mixed_spread, lows = score_grads(v_rows, attn_probs, grads, w_proj, twice)
    results = []
    for part in (slice(0, 2), slice(2, 4)):
        rows = [x[part] for x in (normed, inv_std, q_spread, k_rows, probs_low, mixed_spread, lows, grads)]
        results += input_grads(*rows, gain, w_qkv_ref, rep_ref[...], mask_t_ref[...])
    for v in LEVELS:
        low_ref[v] = lows[v]
        row, lane = v % 2 * PIECE, v // 2 * D
        piece_ref[:, row : row + PIECE, lane : lane + D] = dot(join_t, results[v]).reshape(4, PIECE, D)
    for place, ref in enumerate((stay_out, lon_out, lat_out, both_out)):
        ref[...] = piece_ref[place].astype(BF16)


def fold_kernel(low_ref, perm_ref, pack_ref, folded_ref, table_ref):
    fold_scores([low_ref[v] for v in LEVELS], 1.0 / SCALE, perm_ref, folded_ref, table_ref, pack_ref)


def third_kernel(
    stay_ref, lon_ref, lat_ref, both_ref, v_ref, probs_ref, other_ref, w_proj_ref, twice_ref, perm_ref, split_ref,
    terms_ref, grad_ref,
    window_ref, folded_ref, table_ref, pack_ref,
):
    split = split_ref[...]
    for place, ref in enumerate((stay_ref, lon_ref, lat_ref, both_ref)):
        wide = ref[...].astype(F32)
        for v in LEVELS:
            row, lane = v % 2 * PIECE, v // 2 * D
            window_ref[v, place * PIECE : (place + 1) * PIECE, :] = wide[row : row + PIECE, lane : lane + D]
    grads = [dot(split, window_ref[v].astype(BF16)).astype(BF16) for v in LEVELS]
    attn_probs = [probs_ref[v].astype(F32) for v in LEVELS]
    _, _, lows = score_grads([v_ref[v] for v in LEVELS], attn_probs, grads, w_proj_ref[...], twice_ref[...], 1.0)
    for v in LEVELS:
        grad_ref[v] = grads[v]
    fold_scores(lows, 1.0, perm_ref, folded_ref, table_ref, pack_ref)
    terms_ref[...] = jnp.concatenate([pack_ref[...], other_ref[...]], 1).astype(BF16)


def last_kernel(
    tokens_ref, probs_ref, grad_ref, gain_ref, w_qkv_ref, w_proj_ref, twice_ref,
    grid_ref,
):
    picked = picks()
    rep, mask_t = spreaders()
    twice, gain = twice_ref[...], gain_ref[...]
    normed, inv_std, q_rows, k_rows, v_rows = project(load_windows(tokens_ref, picked), gain, w_qkv_ref[...])
    grads = [grad_ref[v] for v in LEVELS]
    probs = [probs_ref[v] for v in LEVELS]
    _, mixed_spread, lows = score_grads(v_rows, [x.astype(F32) for x in probs], grads, w_proj_ref[...], twice)
    results = input_grads(
        normed,
        inv_std,
        spread_heads(q_rows, twice),
        k_rows,
        probs,
        mixed_spread,
        lows,
        grads,
        gain,
        w_qkv_ref,
        rep,
        mask_t,
    )
    store_windows(results, picked, grid_ref)


def sum_kernel(arrived_ref, one_ref, two_ref, total_ref):
    total = arrived_ref[0].astype(F32)
    for tile in range(1, arrived_ref.shape[0]):
        total = total + arrived_ref[tile].astype(F32)
    total_ref[...] = total
    for base, out_ref in ((0, one_ref), (TERM, two_ref)):
        for row in range(SHARE):
            lane = ROWS * row
            out_ref[:, lane : lane + FLAT] = total_ref[base + row : base + row + 1, :]
            place = base + SHARE + row
            out_ref[:, lane + FLAT : lane + 2 * FLAT] = total_ref[place : place + 1, :]
            place, shift = base + 2 * SHARE + row % 4, row // 4 * REST
            out_ref[:, lane + 2 * FLAT : lane + ROWS] = total_ref[place : place + 1, shift : shift + REST]


def call(kernel, out_shapes, scratch, flops, scalars=0):
    return pl.pallas_call(
        kernel,
        out_shape=[jax.ShapeDtypeStruct(shape, dtype) for shape, dtype in out_shapes],
        scratch_shapes=[pltpu.VMEM(shape, F32) for shape in scratch],
        compiler_params=pltpu.CompilerParams(vmem_limit_bytes=VMEM_LIMIT),
        cost_estimate=pl.CostEstimate(flops=flops, bytes_accessed=4_000_000, transcendentals=500_000),
    )


ALL_VMEM = 62 * 1024 * 1024
VMEM_LIMIT = 40 * 1024 * 1024
HBM = pl.BlockSpec(memory_space=pltpu.HBM)
VMEM = pl.BlockSpec(memory_space=pltpu.VMEM)


def shifted(axes, by):
    sizes = [lax.axis_size(axis) for axis in axes]
    if len(sizes) == 1:
        return [(i, (i + by) % sizes[0]) for i in range(sizes[0])]
    rows, columns = sizes
    return [
        (a * columns + o, (a + by) % rows * columns + (o + by) % columns)
        for a in range(rows)
        for o in range(columns)
    ]


def exchange(pieces, by):
    stay, lon, lat, both = pieces
    return (
        stay,
        lax.ppermute(lon, ("lon",), shifted(("lon",), by)),
        lax.ppermute(lat, ("lat",), shifted(("lat",), by)),
        lax.ppermute(both, ("lat", "lon"), shifted(("lat", "lon"), by)),
    )


def body(
    tokens, grad_out, gain_one, qkv_one, proj_one, bias_one, gain_two, qkv_two, proj_two, bias_two
):
    const = {name: jnp.asarray(value) for name, value in CONST.items()}
    spread = (const["rep"], const["twice"], const["mask_t"])
    perm = const["perm"]
    block_two = (gain_two.reshape(1, D), qkv_two, proj_two) + spread
    columns = (WIN_LAT * WIN_LON, LEV, D)

    def level_last(grid):
        return grid.transpose(1, 2, 0, 3).reshape(columns)

    pair = ((LEV_WIN * PIECE, 2 * D), BF16)
    single = ((LEV_WIN * PIECE // 2, 2 * D), BF16)
    rows = (LEV_WIN, WIN_TOK, D)
    scores = (LEV_WIN, WIN_TOK, LANES)
    parts = [(LEV_WIN * SLAB, FLAT)] * 3
    spread_rows = (2, LEV_WIN, ROWS - BAND, SLAB)
    folded = (ROWS, LEV_WIN * SLAB)
    table = (LEV_WIN * SLAB, 3 * FLAT)
    tiles = LEV_WIN * SLAB // SHARE

    outs = [pair[0]] * 4 + [rows, scores]
    table_rows = (9, PERIOD)
    operands = (
        level_last(tokens), level_last(grad_out), bias_one, gain_one.reshape(1, D), qkv_one, proj_one,
        const["twice"], perm, const["split_t"],
    )
    held = [0, 1, 4, 5, 6, 7, 8]
    first = pl.pallas_call(
        first_kernel,
        in_specs=[HBM] * len(operands),
        out_specs=[HBM] * len(outs),
        out_shape=[jax.ShapeDtypeStruct(shape, BF16) for shape in outs],
        scratch_shapes=[
            pltpu.VMEM(shape, F32)
            for shape in parts + [spread_rows, scores, (4, LEV_WIN * PIECE, 2 * D), table_rows, (1, D)]
        ]
        + [pltpu.VMEM(operands[k].shape, BF16) for k in held]
        + [pltpu.VMEM(shape, BF16) for shape in ((LANES, WIN_TOK), (D, LANES), (4,) + pair[0], rows, scores)]
        + [pltpu.SemaphoreType.DMA((9,)), pltpu.SemaphoreType.DMA((8,)), pltpu.SemaphoreType.DMA((4,)), pltpu.SemaphoreType.DMA((2,))],
        compiler_params=pltpu.CompilerParams(vmem_limit_bytes=ALL_VMEM),
        cost_estimate=pl.CostEstimate(flops=2_000_000_000, bytes_accessed=4_000_000, transcendentals=500_000),
    )(*operands)
    pieces, saved = first[:4], first[4:]
    pieces, bias_two = lax.optimization_barrier((tuple(pieces), bias_two))
    pieces = exchange(pieces, -1)

    active = jnp.where(lax.axis_index("lat") == lax.axis_size("lat") - 1, 1.0, 0.0).astype(F32).reshape(1, 1)
    (bias_full,) = pl.pallas_call(
        bias_kernel,
        in_specs=[pl.BlockSpec(memory_space=pltpu.SMEM), HBM, VMEM],
        out_shape=[jax.ShapeDtypeStruct(scores, F32)],
        scratch_shapes=[pltpu.VMEM(shape, F32) for shape in parts + [spread_rows, table_rows]] + [pltpu.SemaphoreType.DMA((9,))],
        compiler_params=pltpu.CompilerParams(vmem_limit_bytes=VMEM_LIMIT),
        cost_estimate=pl.CostEstimate(flops=500_000_000, bytes_accessed=4_000_000, transcendentals=0),
    )(active, bias_two, perm)

    second = call(
        second_kernel,
        [single] * 4 + [(scores, BF16)],
        [(LEV_WIN, WIN_TOK, 2 * D), (4, LEV_WIN * PIECE // 2, 2 * D)],
        4_000_000_000,
    )(*pieces, bias_full, *block_two, const["join"], const["join_t"])
    grad_pieces, low_two = second[:4], second[4]
    grad_pieces = exchange(grad_pieces, 1)

    (term_two,) = call(fold_kernel, [((tiles, TERM, FLAT), F32)], [folded, table], 500_000_000)(low_two, perm)

    v_rows, probs = saved
    operands = (*grad_pieces, v_rows, probs, term_two, proj_one, const["twice"], perm, const["split"])
    terms, grads = call(
        third_kernel,
        [((tiles, 2 * TERM, FLAT), BF16), (rows, BF16)],
        [rows, folded, table, (tiles, TERM, FLAT)],
        2_000_000_000,
    )(*operands)

    arrived = lax.all_to_all(terms, "lon", 0, 0, tiled=True)
    operands = (level_last(tokens), probs, grads, gain_one.reshape(1, D), qkv_one, proj_one, const["twice"])
    (grid_out,) = call(last_kernel, [(columns, BF16)], [], 3_000_000_000)(*operands)
    grad_tokens = grid_out.reshape(WIN_LAT, WIN_LON, LEV, D).transpose(2, 0, 1, 3)
    width = SHARE * ROWS
    summed_one, summed_two = call(
        sum_kernel, [((1, width), F32), ((1, width), F32)], [(2 * TERM, FLAT)], 1_000_000
    )(arrived)
    return grad_tokens, summed_one, summed_two


def solution(mesh):
    in_specs = (
        P(None, "lat", "lon", None),
        P(None, "lat", "lon", None),
        P(),
        P(),
        P(),
        P("lat", None),
        P(),
        P(),
        P(),
        P("lat", None),
    )
    out_specs = (P(None, "lat", "lon", None), P("lat", "lon"), P("lat", "lon"))
    return jax.shard_map(body, mesh=mesh, in_specs=in_specs, out_specs=out_specs, check_vma=False)
```
